128 devices in a mesh: gx: 8 (over y, core), gy: 16 (over x, z).
Axes of the slice: x: 4, y: 4, z: 4, core: 2. Of those that a mesh axis runs over, the one named last changes fastest.
Arguments:
- load: float32 [3, 72, 256, 128], P(None, 'gx', 'gy'), may hold values from -6 to 6
- plastic_flags: int32 [8, 72, 256, 128], P(None, 'gx', 'gy'), may hold values from 0 to 1, as said below
- flow_dir: float32 [6, 72, 256, 128], P(None, 'gx', 'gy'), may hold values from -1 to 1, as said below
- contact_flags: int32 [72, 256], P('gx', 'gy'), may hold values from 0 to 1, as said below
- die_depth: float32 [72, 256], P('gx', 'gy'), may hold values from -0.5 to -0.05
Outputs:
- displacement: float32 [3, 72, 256, 128], P(None, 'gx', 'gy')
- residual: float32 [3, 72, 256, 128], P(None, 'gx', 'gy')
The draws below stay inside these ranges and needn't reach their ends.
Inputs may be any that keep to these rules, and one draw needn't show every extreme that they name: `plastic_flags`: 0 or 1 for each Gauss point. `contact_flags`: 0 or 1 for each top-face node. `flow_dir`: each element's six entries form a traceless tensor of unit norm, the off-diagonal entries counted twice in the norm.
All inputs are finite; a program needn't handle non-finite values.
Results may differ from the reference program's by a relative error of at most 0.0003.
Values sent between devices are 32-bit elements; how exact they have to be, the bound alone decides.
No kernel may reach another device: no remote copies, remote signals or barrier semaphores. Data moves between devices by JAX's collectives and lax.ppermute only.
A program may use at most 64 MiB of HBM per device.

```python
import math
import jax
import jax.numpy as jnp
from jax import lax

EZ = 128
NEWTON = 2
CG_STEPS = 3
NX = 72
NY = 256


def draw_plastic_flags(key, part):
    key = jax.random.fold_in(key, 11)
    keys = jax.random.split(key, 3)
    centre_x = jax.random.randint(keys[0], (), 0, NX)
    centre_y = jax.random.randint(keys[1], (), 0, NY)
    offset_x = jnp.arange(NX, dtype=jnp.int32)[:, None] - centre_x
    offset_y = jnp.arange(NY, dtype=jnp.int32)[None, :] - centre_y
    reach = (NX // 4 + 1) ** 2 + (NY // 4 + 1) ** 2
    distance = jnp.minimum(offset_x * offset_x + offset_y * offset_y, reach)
    level = 150 + 700 * (reach - distance) // reach
    rolled = jax.random.randint(keys[2], (8, NX, NY, EZ), 0, 1000)
    return (rolled < level[None, :, :, None]).astype(jnp.int32)


def draw_flow_dir(key, part):
    key = jax.random.fold_in(key, 17)
    raw_values = jax.random.normal(key, (6, NX, NY, EZ), jnp.float32)
    diagonal = raw_values[:3] - jnp.mean(raw_values[:3], axis=0, keepdims=True)
    shear_part = raw_values[3:]
    length = jnp.sqrt(jnp.sum(diagonal * diagonal, axis=0) + 2.0 * jnp.sum(shear_part * shear_part, axis=0) + 1e-12)
    return jnp.concatenate([diagonal, shear_part], axis=0) / length[None]


def draw_contact_flags(key, part):
    key = jax.random.fold_in(key, 23)
    keys = jax.random.split(key, 3)
    width_x = NX // 2
    width_y = NY // 2
    start_x = jax.random.randint(keys[0], (), 0, NX - width_x + 1)
    start_y = jax.random.randint(keys[1], (), 0, NY - width_y + 1)
    place_x = jnp.arange(NX, dtype=jnp.int32)[:, None]
    place_y = jnp.arange(NY, dtype=jnp.int32)[None, :]
    inside = (place_x >= start_x) & (place_x < start_x + width_x) & (place_y >= start_y) & (place_y < start_y + width_y)
    touching = jax.random.randint(keys[2], (NX, NY), 0, 10) < 9
    return (inside & touching).astype(jnp.int32)


def block_scale(key, dims, pieces, least, top_value):
    def one(axis_at, blocks):
        heights = jax.random.uniform(jax.random.fold_in(jax.random.fold_in(key, 6), axis_at), (blocks,), jnp.float32, least / len(pieces), top_value / len(pieces))
        return jnp.repeat(jnp.exp(heights), dims[axis_at] // blocks).reshape((-1,) + (1,) * (len(dims) - axis_at - 1))

    factor_of = one(*pieces[0])
    for cut in pieces[1:]:
        factor_of = factor_of * one(*cut)
    return factor_of


def scatter_about(key, dims, scale, bound, cuts=(), kind=jnp.bfloat16):
    array = jax.random.normal(key, dims, jnp.float32) * scale
    if len(cuts) > 0:
        array = block_scale(key, dims, cuts, -0.22, 0.18) * array
    return jnp.clip(array, min=-bound, max=bound).astype(kind)


def setup_inputs(seed: int = 0) -> dict:
    key_list = jax.random.split(jax.random.key(seed), 6)
    load = scatter_about(key_list[0], (3, NX, NY, EZ), 1.0, 6.0, ((1, 8), (2, 16)), jnp.float32)
    plastic_flags = draw_plastic_flags(jax.random.fold_in(key_list[5], 71), 0)
    flow_dir = draw_flow_dir(jax.random.fold_in(key_list[5], 71), 0)
    contact_flags = draw_contact_flags(jax.random.fold_in(key_list[5], 71), 0)
    die_depth = jnp.clip(-0.5 + 0.45 * jax.random.uniform(key_list[4], (NX, NY), jnp.float32) ** block_scale(key_list[4], (NX, NY), ((0, 8), (1, 16)), -0.2, 0.2), -0.5, -0.05)
    return {"load": load, "plastic_flags": plastic_flags, "flow_dir": flow_dir, "contact_flags": contact_flags, "die_depth": die_depth}


LAME_FIRST = 1.0
SHEAR_MOD = 1.0
PLASTIC_GAIN = 6.0 / 3.1
YIELD_OFFSET = 0.05
CONTACT_STIFF = 4.0
POINT_WEIGHT = 0.125
GAUSS_POINTS = (0.5 - 0.5 / math.sqrt(3.0), 0.5 + 0.5 / math.sqrt(3.0))
FLOW_SLOT = ((0, 3, 5), (3, 1, 4), (5, 4, 2))

def lower_part(values, dimension):
    return lax.slice_in_dim(values, 0, values.shape[dimension] - 1, axis=dimension)

def upper_part(values, dimension):
    return lax.slice_in_dim(values, 1, values.shape[dimension], axis=dimension)

def blend_at(values, dimension, weight_at):
    return (1.0 - weight_at) * lower_part(values, dimension) + weight_at * upper_part(values, dimension)

def pad_pair(values, dimension):
    pad_before = [(0, 0)] * values.ndim
    pad_after = [(0, 0)] * values.ndim
    pad_before[dimension] = (1, 0)
    pad_after[dimension] = (0, 1)
    return (jnp.pad(values, pad_after), jnp.pad(values, pad_before))

def blend_back(values, dimension, weight_at):
    first, second = pad_pair(values, dimension)
    return (1.0 - weight_at) * first + weight_at * second

def spread(values, dimension):
    first, second = pad_pair(values, dimension)
    return second - first

def element_forces(node_values, plastic, flow_dir, element_mask, offset):
    slopes = [[upper_part(node_values[c], d) - lower_part(node_values[c], d) for d in range(3)] for c in range(3)]
    totals = [[0.0, 0.0, 0.0] for c in range(3)]
    for i in range(2):
        for j in range(2):
            for k in range(2):
                point_x = GAUSS_POINTS[i]
                point_y = GAUSS_POINTS[j]
                point_z = GAUSS_POINTS[k]
                gradient = [[blend_at(blend_at(slopes[c][0], 1, point_y), 2, point_z), blend_at(blend_at(slopes[c][1], 0, point_x), 2, point_z), blend_at(blend_at(slopes[c][2], 0, point_x), 1, point_y)] for c in range(3)]
                strain = [[0.5 * (gradient[c][d] + gradient[d][c]) if c != d else gradient[c][c] for d in range(3)] for c in range(3)]
                trace_sum = strain[0][0] + strain[1][1] + strain[2][2]
                normal_part = flow_dir[0] * strain[0][0] + flow_dir[1] * strain[1][1] + flow_dir[2] * strain[2][2]
                normal_part = normal_part + 2.0 * (flow_dir[3] * strain[0][1] + flow_dir[4] * strain[1][2] + flow_dir[5] * strain[2][0])
                return_size = PLASTIC_GAIN * plastic[4 * i + 2 * j + k] * (normal_part - offset)
                scaling = POINT_WEIGHT * element_mask
                stress = [[None] * 3 for c in range(3)]
                for c in range(3):
                    for d in range(c, 3):
                        entry = 2.0 * SHEAR_MOD * strain[c][d] - return_size * flow_dir[FLOW_SLOT[c][d]]
                        if c == d:
                            entry = entry + LAME_FIRST * trace_sum
                        stress[c][d] = scaling * entry
                        stress[d][c] = stress[c][d]
                for c in range(3):
                    totals[c][0] = totals[c][0] + blend_back(blend_back(stress[c][0], 2, point_z), 1, point_y)
                    totals[c][1] = totals[c][1] + blend_back(blend_back(stress[c][1], 2, point_z), 0, point_x)
                    totals[c][2] = totals[c][2] + blend_back(blend_back(stress[c][2], 1, point_y), 0, point_x)
    return jnp.stack([spread(totals[c][0], 0) + spread(totals[c][1], 1) + spread(totals[c][2], 2) for c in range(3)])

def add_contact(result, field, active):
    return result.at[2, :, :, -1].add(CONTACT_STIFF * active * field[2, :, :, -1])

def reference(load, plastic_flags, flow_dir, contact_flags, die_depth):
    plastic = plastic_flags.astype(jnp.float32)
    active = contact_flags.astype(jnp.float32)

    def operate(field):
        node_values = jnp.pad(field, ((0, 0), (0, 1), (0, 1), (1, 0)))
        result = element_forces(node_values, plastic, flow_dir, 1.0, 0.0)[:, :-1, :-1, 1:]
        return add_contact(result, field, active)

    def conjugate(right):
        solution = jnp.zeros_like(right)
        remain = right
        direction = right
        norm_now = jnp.sum(remain * remain)
        for step in range(CG_STEPS):
            image = operate(direction)
            alpha = norm_now / jnp.sum(direction * image)
            solution = solution + alpha * direction
            remain = remain - alpha * image
            if step + 1 < CG_STEPS:
                norm_next = jnp.sum(remain * remain)
                direction = remain + norm_next / norm_now * direction
                norm_now = norm_next
        return solution
    zero_nodes = jnp.zeros((3, NX + 1, NY + 1, EZ + 1), jnp.float32)
    offset_force = element_forces(zero_nodes, plastic, flow_dir, 1.0, YIELD_OFFSET)[:, :-1, :-1, 1:]
    right_side = (load - offset_force).at[2, :, :, -1].add(CONTACT_STIFF * active * die_depth)
    displacement = jnp.zeros_like(load)
    for newton in range(NEWTON):
        if newton == 0:
            newton_residual = right_side
        else:
            newton_residual = right_side - operate(displacement)
        displacement = displacement + conjugate(newton_residual)
    return (displacement, right_side - operate(displacement))
```

```python
import math

import jax
import jax.numpy as jnp
from jax import lax
from jax.experimental import pallas as pl
from jax.experimental.pallas import tpu as pltpu
from jax.sharding import PartitionSpec as P

PLASTIC_GAIN = 6.0 / 3.1
YIELD_OFFSET = 0.05
CONTACT_STIFF = 4.0
CG_STEPS = 3
NEWTON = 2
ROOT_THIRD = 1.0 / math.sqrt(3.0)
THIRD = 1.0 / 3.0
SPAN = 10.0

HALO = 3
OX, OY, DZ = 9, 16, 128
WX = OX + 2 * HALO
WE = WX - 1
WY = 24
F32 = jnp.float32

FLOW_SENT = (0, 1, 3, 4, 5)
NEL = 14
CONTACT_AT = 13
ZZ_AT = 14


def lanes():
    return lax.broadcasted_iota(jnp.int32, (8, DZ), 1)


def z_pair(value, first_lane):
    low = jnp.where(first_lane, 0.0, pltpu.roll(value, 1, 1))
    return value + low, value - low


def z_merge(total, slope, last_lane):
    return total + slope + jnp.where(last_lane, 0.0, pltpu.roll(total - slope, DZ - 1, 1))


def to_points(s1, sx, sy, sz, syz, sxz, sxy):
    points = []
    for sign_x in (-1, 1):
        a0 = s1 + sx if sign_x > 0 else s1 - sx
        ay = sy + sxy if sign_x > 0 else sy - sxy
        az = sz + sxz if sign_x > 0 else sz - sxz
        for sign_y in (-1, 1):
            b0 = a0 + ay if sign_y > 0 else a0 - ay
            bz = az + syz if sign_y > 0 else az - syz
            points += [b0 - bz, b0 + bz]
    return points


def from_points(t):
    per_x = []
    for i in range(2):
        e0 = [t[4 * i + 2 * j + 1] + t[4 * i + 2 * j] for j in range(2)]
        ez = [t[4 * i + 2 * j + 1] - t[4 * i + 2 * j] for j in range(2)]
        per_x.append((e0[1] + e0[0], e0[1] - e0[0], ez[1] + ez[0], ez[1] - ez[0]))
    low, high = per_x
    t1, ty, tz, tyz = (high[m] + low[m] for m in range(4))
    tx, txy, txz = (high[m] - low[m] for m in range(3))
    return t1, tx, ty, tz, tyz, txz, txy


def plastic_forces(n, t):
    nxx, nyy, nzz, nxy, nyz, nzx = n
    t1, tx, ty, tz, tyz, txz, txy = t
    tx, ty, tz = tx * ROOT_THIRD, ty * ROOT_THIRD, tz * ROOT_THIRD
    tyz, txz, txy = tyz * THIRD, txz * THIRD, txy * THIRD
    a_xy, a_yz, a_zx = nxy * t1, nyz * t1, nzx * t1
    fx = [nxx * t1, a_xy, a_zx]
    fy = [a_xy, nyy * t1, a_yz]
    fz = [a_zx, a_yz, nzz * t1]
    xy_z, yz_x, zx_y = nxy * tz, nyz * tx, nzx * ty
    fxy = [nxx * ty + nxy * tx, nxy * ty + nyy * tx, zx_y + yz_x]
    fxz = [nxx * tz + nzx * tx, xy_z + yz_x, nzx * tz + nzz * tx]
    fyz = [xy_z + zx_y, nyy * tz + nyz * ty, nyz * tz + nzz * ty]
    fxyz = [
        nxx * tyz + nxy * txz + nzx * txy,
        nxy * tyz + nyy * txz + nyz * txy,
        nzx * tyz + nyz * txz + nzz * txy,
    ]
    return fx, fy, fz, fxy, fxz, fyz, fxyz


def element_core(modes, n, flags):
    ax, ay, az, axy, axz, ayz, axyz = modes
    nxx, nyy, nzz, nxy, nyz, nzx = n
    sh_xy, sh_yz, sh_zx = ax[1] + ay[0], ay[2] + az[1], az[0] + ax[2]
    k_x, k_y, k_z = axy[2] + axz[1], axy[2] + ayz[0], axz[1] + ayz[0]
    s1 = (nxx * ax[0] + nyy * ay[1] + nzz * az[2]) + (nxy * sh_xy + nyz * sh_yz + nzx * sh_zx)
    sx = (nxy * axy[0] + nyy * axy[1]) + (nyz * k_x + nzx * axz[0] + nzz * axz[2])
    sy = (nxx * axy[0] + nxy * axy[1]) + (nzx * k_y + nyz * ayz[1] + nzz * ayz[2])
    sz = (nxx * axz[0] + nxy * k_z) + (nzx * axz[2] + nyy * ayz[1] + nyz * ayz[2])
    syz = nxx * axyz[0] + nxy * axyz[1] + nzx * axyz[2]
    sxz = nxy * axyz[0] + nyy * axyz[1] + nyz * axyz[2]
    sxy = nzx * axyz[0] + nyz * axyz[1] + nzz * axyz[2]
    values = to_points(
        s1, sx * ROOT_THIRD, sy * ROOT_THIRD, sz * ROOT_THIRD, syz * THIRD, sxz * THIRD, sxy * THIRD
    )
    plastic = plastic_forces(n, from_points([value * flag for value, flag in zip(values, flags)]))
    trace = ax[0] + ay[1] + az[2]
    tr_x, tr_y, tr_z = (
        (axy[1] + axz[2]) * THIRD,
        (axy[0] + ayz[2]) * THIRD,
        (axz[0] + ayz[1]) * THIRD,
    )
    mixed = (k_x + ayz[0]) * THIRD
    elastic = (
        [trace + (ax[0] + ax[0]), sh_xy, sh_zx],
        [sh_xy, trace + (ay[1] + ay[1]), sh_yz],
        [sh_zx, sh_yz, trace + (az[2] + az[2])],
        [tr_y + axy[0], tr_x + axy[1], mixed + axy[2] * THIRD],
        [tr_z + axz[0], mixed + axz[1] * THIRD, tr_x + axz[2]],
        [mixed + ayz[0] * THIRD, tr_z + ayz[1], tr_y + ayz[2]],
        [axyz[c] * (5.0 / 9.0) for c in range(3)],
    )
    return [[elastic[m][c] + plastic[m][c] for c in range(3)] for m in range(7)]


def scatter_x(forces, behind):
    fx, fy, fz, fxy, fxz, fyz, fxyz = forces
    node, ahead = [], []
    for c in range(3):
        node += [
            behind[4 * c] - fx[c],
            behind[4 * c + 1] + (fy[c] - fxy[c]),
            behind[4 * c + 2] + (fz[c] - fxz[c]),
            behind[4 * c + 3] + (fyz[c] - fxyz[c]),
        ]
        ahead += [fx[c], fy[c] + fxy[c], fz[c] + fxz[c], fyz[c] + fxyz[c]]
    return node, ahead


def store_y(node, lower_ref, upper_ref, x, row, upper_keep=None):
    for c in range(3):
        ss, sd, ds, dd = node[4 * c : 4 * c + 4]
        lower_ref[2 * c, x, row : row + 8] = ss - sd
        lower_ref[2 * c + 1, x, row : row + 8] = ds - dd
        up_s, up_d = ss + sd, ds + dd
        if upper_keep is not None:
            up_s, up_d = jnp.where(upper_keep, up_s, 0.0), jnp.where(upper_keep, up_d, 0.0)
        upper_ref[2 * c, x, row + 8 : row + 16] = up_s
        upper_ref[2 * c + 1, x, row + 8 : row + 16] = up_d


def merge_yz(lower_ref, upper_ref, c, x, row, last_lane):
    total = lower_ref[2 * c, x, row : row + 8] + upper_ref[2 * c, x, row + 7 : row + 15]
    slope = lower_ref[2 * c + 1, x, row : row + 8] + upper_ref[2 * c + 1, x, row + 7 : row + 15]
    return z_merge(total, slope, last_lane)


def place():
    index_x, index_y = lax.axis_index("gx"), lax.axis_index("gy")
    return (
        index_x == 0,
        index_x == lax.axis_size("gx") - 1,
        index_y == 0,
        index_y == lax.axis_size("gy") - 1,
    )


def ask(flag):
    return jnp.where(flag, 0.0, 1.0).astype(F32)


def offset_kernel(load_ref, flags_ref, flow_ref, contact_ref, die_ref,
                  part_ref, right_ref, left_ref, up_ref, down_ref, lower_ref, upper_ref):
    lane = lanes()
    last_lane = lane == DZ - 1
    zero = jnp.zeros((8, DZ), F32)

    def clear(x, _):
        for m in range(6):
            lower_ref[m, x, 16:24] = zero
            upper_ref[m, x, 0:8] = zero
        return 0

    lax.fori_loop(0, OX + 1, clear, 0)
    for row in (0, 8):

        def element(x, behind):
            flags = [flags_ref[q, x, row : row + 8].astype(F32) * (0.5 * PLASTIC_GAIN * YIELD_OFFSET) for q in range(8)]
            n = [flow_ref[m, x, row : row + 8] for m in range(6)]
            node, ahead = scatter_x(plastic_forces(n, from_points(flags)), behind)
            store_y(node, lower_ref, upper_ref, x, row)
            return ahead

        behind = lax.fori_loop(0, OX, element, [zero] * 12)
        store_y(behind, lower_ref, upper_ref, OX, row)

    def finish(x, _):
        for c in range(3):
            for row in (0, 8, 16):
                part_ref[c, x, row : row + 8] = merge_yz(lower_ref, upper_ref, c, x, row, last_lane) * (-1.0 / 16.0)
        return 0

    lax.fori_loop(0, OX + 1, finish, 0)

    def add_load(x, _):
        for c in range(3):
            for row in (0, 8):
                value = part_ref[c, x, row : row + 8] + load_ref[c, x, row : row + 8]
                if c == 2:
                    value = value + die_ref[x, row : row + 8]
                part_ref[c, x, row : row + 8] = value
        return 0

    lax.fori_loop(0, OX, add_load, 0)

    def field(f, x, rows):
        if f < 8:
            return flags_ref[f, x, rows].astype(F32) * (-PLASTIC_GAIN / 8.0)
        if f < CONTACT_AT:
            return flow_ref[FLOW_SENT[f - 8], x, rows]
        return contact_ref[x, rows]

    whole = slice(0, OY)
    for f in range(NEL):
        for i in range(3):
            right_ref[3 * f + i] = field(f, 6 + i, whole)
        for i in range(2):
            left_ref[2 * f + i] = field(f, i, whole)
    for c in range(3):
        for i in range(4):
            right_ref[42 + 4 * c + i] = part_ref[c, 6 + i, 0:16]
            right_ref[54, 4 * c + i : 4 * c + i + 1] = part_ref[c, 6 + i, 16:17]
        for i in range(3):
            left_ref[28 + 3 * c + i] = part_ref[c, i, 0:16]
            left_ref[37, 3 * c + i : 3 * c + i + 1] = part_ref[c, i, 16:17]

    def slabs(x, _):
        for f in range(NEL):
            up_ref[x, 3 * f : 3 * f + 3] = field(f, x, slice(13, 16))
            down_ref[x, 2 * f : 2 * f + 2] = field(f, x, slice(0, 2))
        return 0

    lax.fori_loop(0, OX, slabs, 0)

    def part_slabs(x, _):
        for c in range(3):
            up_ref[x, 42 + 4 * c : 46 + 4 * c] = part_ref[c, x, 13:17]
            down_ref[x, 28 + 3 * c : 31 + 3 * c] = part_ref[c, x, 0:3]
        return 0

    lax.fori_loop(0, OX + 1, part_slabs, 0)


def three_steps(els_ref, basis, z_ref, lower_ref, upper_ref):
    at_first_x, at_last_x, at_first_y, at_last_y = place()
    lane = lanes()
    first_lane, last_lane = lane == 0, lane == DZ - 1
    rows = lax.broadcasted_iota(jnp.int32, (8, DZ), 0)
    keep_upper = jnp.logical_or(rows >= HALO, jnp.logical_not(at_first_y))
    keep_node = jnp.logical_or(rows < HALO, jnp.logical_not(at_last_y))
    zero = jnp.zeros((8, DZ), F32)

    def clear(x, _):
        for m in range(6):
            z_ref[m, x, 24:32] = zero
            upper_ref[m, x, 0:8] = zero
        return 0

    lax.fori_loop(0, WX, clear, 0)

    def first(x, _):
        for row in (0, 8, 16):
            for c in range(3):
                z_ref[2 * c, x, row : row + 8], z_ref[2 * c + 1, x, row : row + 8] = z_pair(
                    basis[0][c, x, row : row + 8], first_lane
                )
        return 0

    lax.fori_loop(0, WX, first, 0)

    for step in range(1, HALO + 1):
        start = jnp.where(at_first_x, HALO, step - 1)
        end = jnp.where(at_last_x, HALO + OX - 1, WX - 1 - step)
        for row in (0, 8, 16):

            def plane(x):
                values = []
                for m in range(6):
                    low, high = z_ref[m, x, row : row + 8], z_ref[m, x, row + 1 : row + 9]
                    values += [high + low, high - low]
                return values

            def element(x, carry):
                before, behind = carry
                after = plane(x + 1)
                p, q = before, after
                modes = (
                    [q[4 * c] - p[4 * c] for c in range(3)],
                    [q[4 * c + 1] + p[4 * c + 1] for c in range(3)],
                    [q[4 * c + 2] + p[4 * c + 2] for c in range(3)],
                    [q[4 * c + 1] - p[4 * c + 1] for c in range(3)],
                    [q[4 * c + 2] - p[4 * c + 2] for c in range(3)],
                    [q[4 * c + 3] + p[4 * c + 3] for c in range(3)],
                    [q[4 * c + 3] - p[4 * c + 3] for c in range(3)],
                )
                here = [els_ref[f, x, row : row + 8] for f in range(NEL + 1) if f != CONTACT_AT]
                n = (here[8], here[9], here[13], here[10], here[11], here[12])
                node, ahead = scatter_x(element_core(modes, n, here[:8]), behind)
                store_y(node, lower_ref, upper_ref, x, row, keep_upper if row == 0 else None)
                return after, ahead

            lax.fori_loop(start, end + 1, element, (plane(start), [zero] * 12))

        node_start = jnp.where(at_first_x, HALO, step)
        scale = (2.0 if step == 1 else 4.0) / SPAN

        def finish(x, _):
            for row in (0, 8, 16):
                for c in range(3):
                    here = basis[step - 1][c, x, row : row + 8]
                    value = merge_yz(lower_ref, upper_ref, c, x, row, last_lane) * (scale / 16.0)
                    if c == 2:
                        value = value + (els_ref[CONTACT_AT, x, row : row + 8] * scale) * here
                    if step == 1:
                        value = value - here
                    else:
                        value = value - (here + here) - basis[step - 2][c, x, row : row + 8]
                    if row == 16:
                        value = jnp.where(keep_node, value, 0.0)
                    basis[step][c, x, row : row + 8] = value
                    if step < HALO:
                        z_ref[2 * c, x, row : row + 8], z_ref[2 * c + 1, x, row : row + 8] = z_pair(value, first_lane)
            return 0

        lax.fori_loop(node_start, end + 1, finish, 0)


def sum_rows(values):
    return jnp.sum(values, axis=0, keepdims=True)


def first_kernel(flags_ref, flow_ref, contact_ref, part_ref, left_ref, right_ref, down_ref, up_ref, cl_ref, cr_ref,
                 els_ref, own_ref, dots_ref, right_out, left_out, up_out, down_out,
                 b0, b1, b2, b3, z_ref, lower_ref, upper_ref):
    at_first_x, at_last_x, at_first_y, at_last_y = place()
    has_l, has_r, has_d, has_u = ask(at_first_x), ask(at_last_x), ask(at_first_y), ask(at_last_y)
    zero = jnp.zeros((8, DZ), F32)
    low, high = slice(0, 3), slice(19, 21)
    mid = slice(HALO, HALO + OY)

    def clear(x, _):
        for f in range(NEL):
            els_ref[f, x, 16:24] = zero
        return 0

    lax.fori_loop(0, WE, clear, 0)

    def clear_start(x, _):
        for c in range(3):
            for row in (0, 8, 16):
                b0[c, x, row : row + 8] = zero
        return 0

    lax.fori_loop(0, WX, clear_start, 0)

    def own(x, _):
        w = x + HALO
        for f in range(NEL):
            if f < 8:
                value = flags_ref[f, x].astype(F32) * (-PLASTIC_GAIN / 8.0)
            elif f < CONTACT_AT:
                value = flow_ref[FLOW_SENT[f - 8], x]
            else:
                value = contact_ref[x]
            els_ref[f, w, mid] = value
            els_ref[f, w, low] = down_ref[x, 3 * f : 3 * f + 3]
            els_ref[f, w, high] = up_ref[x, 2 * f : 2 * f + 2]
        for c in range(3):
            b0[c, w, mid] = part_ref[c, x, 0:16]
            b0[c, w, 19:20] = part_ref[c, x, 16:17] * has_u
        return 0

    lax.fori_loop(0, OX, own, 0)
    for c in range(3):
        b0[c, 12, mid] = part_ref[c, OX, 0:16] * has_r
        b0[c, 12, 19:20] = part_ref[c, OX, 16:17] * (has_r * has_u)
    for i in range(3):
        for f in range(NEL):
            els_ref[f, i, mid] = left_ref[3 * f + i]
            els_ref[f, i, low] = cl_ref[i, 3 * f : 3 * f + 3]
            els_ref[f, i, high] = cl_ref[i, 56 + 2 * f : 58 + 2 * f]
    for i in range(2):
        for f in range(NEL):
            els_ref[f, 12 + i, mid] = right_ref[2 * f + i]
            els_ref[f, 12 + i, low] = cr_ref[i, 3 * f : 3 * f + 3]
            els_ref[f, 12 + i, high] = cr_ref[i, 56 + 2 * f : 58 + 2 * f]

    def zz(x, _):
        for row in (0, 8, 16):
            els_ref[ZZ_AT, x, row : row + 8] = -(els_ref[8, x, row : row + 8] + els_ref[9, x, row : row + 8])
        return 0

    lax.fori_loop(0, WE, zz, 0)

    for c in range(3):
        for i in range(4):
            b0[c, i, mid] += left_ref[42 + 4 * c + i] * has_l
            b0[c, i, 19:20] += left_ref[54, 4 * c + i : 4 * c + i + 1] * (has_l * has_u)
            b0[c, i, 0:4] += cl_ref[i, 42 + 4 * c : 46 + 4 * c] * (has_l * has_d)
            b0[c, i, 19:22] += cl_ref[i, 84 + 3 * c : 87 + 3 * c] * (has_l * has_u)
        for i in range(3):
            b0[c, 12 + i, mid] += right_ref[28 + 3 * c + i] * has_r
            b0[c, 12 + i, 19:20] += right_ref[37, 3 * c + i : 3 * c + i + 1] * (has_r * has_u)
            b0[c, 12 + i, 0:4] += cr_ref[i, 42 + 4 * c : 46 + 4 * c] * (has_r * has_d)
            b0[c, 12 + i, 19:22] += cr_ref[i, 84 + 3 * c : 87 + 3 * c] * (has_r * has_u)

    def edges(x, _):
        inside = jnp.where(x == OX, has_r, 1.0)
        for c in range(3):
            b0[c, x + HALO, 0:4] += down_ref[x, 42 + 4 * c : 46 + 4 * c] * (inside * has_d)
            b0[c, x + HALO, 19:22] += up_ref[x, 28 + 3 * c : 31 + 3 * c] * (inside * has_u)
        return 0

    lax.fori_loop(0, OX + 1, edges, 0)

    basis = (b0, b1, b2, b3)
    three_steps(els_ref, basis, z_ref, lower_ref, upper_ref)

    def collect(x, sums):
        sums = list(sums)
        for row in (0, 8):
            for c in range(3):
                v = [b[c, x + HALO, row + HALO : row + HALO + 8] for b in basis]
                for k in range(4):
                    own_ref[k, c, x, row : row + 8] = v[k]
                for k in range(7):
                    sums[k] = sums[k] + v[k // 2] * v[k - k // 2]
        return tuple(sums)

    sums = lax.fori_loop(0, OX, collect, (zero,) * 7)
    dots_ref[...] = zero
    for k in range(7):
        dots_ref[k : k + 1] = sum_rows(sums[k])

    for c in range(3):
        for i in range(3):
            right_out[3 * c + i] = b3[c, 9 + i, mid]
            left_out[3 * c + i] = b3[c, 3 + i, mid]

    def slabs(x, _):
        for c in range(3):
            up_out[x, 3 * c : 3 * c + 3] = b3[c, x + HALO, 16:19]
            down_out[x, 3 * c : 3 * c + 3] = b3[c, x + HALO, 3:6]
        return 0

    lax.fori_loop(0, OX, slabs, 0)


def second_kernel(els_ref, own_ref, left_ref, right_ref, down_ref, up_ref, cl_ref, cr_ref,
                  tail_ref, dots_ref, b0, b1, b2, b3, z_ref, lower_ref, upper_ref):
    _, at_last_x, _, at_last_y = place()
    has_r, has_u = ask(at_last_x), ask(at_last_y)
    zero = jnp.zeros((8, DZ), F32)
    mid = slice(HALO, HALO + OY)

    def own(x, _):
        w = x + HALO
        for c in range(3):
            b0[c, w, 16:24] = zero
            b0[c, w, mid] = own_ref[3, c, x]
            b0[c, w, 0:3] = down_ref[x, 3 * c : 3 * c + 3]
            b0[c, w, 19:22] = up_ref[x, 3 * c : 3 * c + 3] * has_u
        return 0

    lax.fori_loop(0, OX, own, 0)
    for c in range(3):
        for i in range(3):
            b0[c, i, 16:24] = zero
            b0[c, i, mid] = left_ref[3 * c + i]
            b0[c, i, 0:3] = cl_ref[i, 3 * c : 3 * c + 3]
            b0[c, i, 19:22] = cl_ref[i, 16 + 3 * c : 19 + 3 * c] * has_u
            b0[c, 12 + i, 16:24] = zero
            b0[c, 12 + i, mid] = right_ref[3 * c + i] * has_r
            b0[c, 12 + i, 0:3] = cr_ref[i, 3 * c : 3 * c + 3] * has_r
            b0[c, 12 + i, 19:22] = cr_ref[i, 16 + 3 * c : 19 + 3 * c] * (has_r * has_u)

    basis = (b0, b1, b2, b3)
    three_steps(els_ref, basis, z_ref, lower_ref, upper_ref)

    def collect(x, sums):
        sums = list(sums)
        for row in (0, 8):
            for c in range(3):
                v = [own_ref[3, c, x, row : row + 8]]
                for k in range(1, 4):
                    w = b_at(basis[k], c, x, row)
                    v.append((w + w) - own_ref[3 - k, c, x, row : row + 8])
                    tail_ref[k - 1, c, x, row : row + 8] = v[k]
                for k in range(1, 6):
                    sums[k - 1] = sums[k - 1] + v[k // 2] * v[k - k // 2]
        return tuple(sums)

    sums = lax.fori_loop(0, OX, collect, (zero,) * 5)
    dots_ref[...] = zero
    for k in range(5):
        dots_ref[k : k + 1] = sum_rows(sums[k])


def b_at(ref, c, x, row):
    return ref[c, x + HALO, row + HALO : row + HALO + 8]


def times_matrix(p):
    out = [None] * (len(p) + 1)

    def add(k, value):
        out[k] = value if out[k] is None else out[k] + value

    for k, value in enumerate(p):
        add(k, value * (SPAN / 2))
        if k == 0:
            add(1, value * (SPAN / 2))
        else:
            add(k + 1, value * (SPAN / 4))
            add(k - 1, value * (SPAN / 4))
    return out


def tree_sum(values):
    while len(values) > 1:
        values = [a + b for a, b in zip(values[::2], values[1::2])] + ([values[-1]] if len(values) % 2 else [])
    return values[0]


def combine(p, a, q):
    out = []
    for k in range(max(len(p), len(q))):
        term = a * q[k] if k < len(q) else None
        if k < len(p):
            term = p[k] if term is None else p[k] + term
        out.append(term)
    return out


def coefficients(mu):
    gram = [[0.5 * (mu[i + j] + mu[abs(i - j)]) if i + j < len(mu) else None for j in range(7)] for i in range(7)]

    def inner(p, q):
        return tree_sum([p[i] * tree_sum([gram[i][j] * q[j] for j in range(len(q))]) for i in range(len(p))])

    remain = [jnp.ones_like(mu[0])]
    total = []
    for newton in range(NEWTON):
        direction = remain
        norm = inner(remain, remain)
        for step in range(CG_STEPS):
            image = times_matrix(direction)
            alpha = norm / inner(direction, image)
            total = combine(total, alpha, direction)
            remain = combine(remain, -alpha, image)
            if step + 1 < CG_STEPS:
                norm_next = inner(remain, remain)
                direction = combine(remain, norm_next / norm, direction)
                norm = norm_next
    return total, remain


def last_kernel(dots_ref, own_ref, tail_ref, displacement_ref, residual_ref):
    sums = jnp.broadcast_to(jnp.sum(dots_ref[...], axis=1, keepdims=True), (16, DZ))
    dots = [sums[k : k + 1] for k in range(7)] + [sums[8 + k : 9 + k] for k in range(5)]
    mu = dots[:2]
    for k in range(2, 12):
        mu.append((dots[k] + dots[k]) - mu[k % 2])
    total, remain = coefficients(mu)
    total = [jnp.broadcast_to(value, (8, DZ)) for value in total]
    remain = [jnp.broadcast_to(value, (8, DZ)) for value in remain]

    def write(x, _):
        for row in (0, 8):
            for c in range(3):
                v = [own_ref[k, c, x, row : row + 8] for k in range(4)]
                v += [tail_ref[k, c, x, row : row + 8] for k in range(3)]
                displacement_ref[c, x, row : row + 8] = tree_sum([a * b for a, b in zip(total, v)])
                residual_ref[c, x, row : row + 8] = tree_sum([a * b for a, b in zip(remain, v)])
        return 0

    lax.fori_loop(0, OX, write, 0)


def shape(*dims):
    return jax.ShapeDtypeStruct(dims, F32)


def call(kernel, outs, scratch=()):
    return pl.pallas_call(
        kernel,
        out_shape=outs,
        scratch_shapes=[pltpu.VMEM(dims, F32) for dims in scratch],
        compiler_params=pltpu.CompilerParams(vmem_limit_bytes=48 * 1024 * 1024),
    )


STEP_SCRATCH = [(3, WX, WY, DZ)] * 4 + [(6, WX, WY + 8, DZ)] * 3


def rotate(value, axis, steps):
    count = lax.axis_size(axis)
    return lax.ppermute(value, axis, [(i, (i + steps) % count) for i in range(count)])


def exchange(right, left, up, down, top):
    from_left = rotate(right, "gx", 1)
    from_right = rotate(left, "gx", -1)
    from_down = rotate(up, "gy", 1)
    from_up = rotate(down, "gy", -1)
    corners = jnp.concatenate([from_down, from_up], axis=1)
    corner_left = rotate(corners[6:top], "gx", 1)
    corner_right = rotate(corners[0:3], "gx", -1)
    return from_left, from_right, from_down, from_up, corner_left, corner_right


def sum_everywhere(value):
    ring = [i ^ 1 for i in range(4)], [3 - i for i in range(4)]
    if (lax.axis_size("gx"), lax.axis_size("gy")) != (8, 16):
        return lax.psum(value, ("gx", "gy"))
    value = value + lax.ppermute(value, "gx", [(i, i ^ 1) for i in range(8)])
    for pairs in ring:
        value = value + lax.ppermute(value, "gx", [(2 * y + k, 2 * pairs[y] + k) for y in range(4) for k in range(2)])
    for pairs in ring:
        value = value + lax.ppermute(value, "gy", [(4 * x + z, 4 * x + pairs[z]) for x in range(4) for z in range(4)])
    for pairs in ring:
        value = value + lax.ppermute(value, "gy", [(4 * x + z, 4 * pairs[x] + z) for x in range(4) for z in range(4)])
    return value


def body(load, plastic_flags, flow_dir, contact_flags, die_depth):
    stiff = CONTACT_STIFF * contact_flags.astype(F32)
    at_top = lax.broadcasted_iota(jnp.int32, (OX, OY, DZ), 2) == DZ - 1
    contact = jnp.where(at_top, stiff[:, :, None], 0.0)
    die = jnp.where(at_top, (stiff * die_depth)[:, :, None], 0.0)

    part, right, left, up, down = call(
        offset_kernel,
        [shape(3, OX + 1, WY, DZ), shape(55, OY, DZ), shape(38, OY, DZ), shape(OX + 1, 56, DZ), shape(OX + 1, 40, DZ)],
        [(6, OX + 1, WY + 8, DZ)] * 2,
    )(load, plastic_flags, flow_dir, contact, die)
    halos = exchange(right, left, up, down, 10)
    els, own, dots, right, left, up, down = call(
        first_kernel,
        [shape(NEL + 1, WE, WY, DZ), shape(4, 3, OX, OY, DZ), shape(8, DZ), shape(9, OY, DZ), shape(9, OY, DZ),
         shape(OX, 16, DZ), shape(OX, 16, DZ)],
        STEP_SCRATCH,
    )(plastic_flags, flow_dir, contact, part, *halos)
    halos = exchange(right, left, up, down, 9)
    tail, dots_tail = call(
        second_kernel, [shape(3, 3, OX, OY, DZ), shape(8, DZ)], STEP_SCRATCH
    )(els, own, *halos)
    dots = sum_everywhere(jnp.concatenate([dots, dots_tail], axis=0))
    return tuple(call(last_kernel, [shape(3, OX, OY, DZ)] * 2)(dots, own, tail))


def solution(mesh):
    in_specs = (
        P(None, "gx", "gy", None),
        P(None, "gx", "gy", None),
        P(None, "gx", "gy", None),
        P("gx", "gy"),
        P("gx", "gy"),
    )
    out_specs = (P(None, "gx", "gy", None), P(None, "gx", "gy", None))
    return jax.shard_map(body, mesh=mesh, in_specs=in_specs, out_specs=out_specs, check_vma=False)
```

```python
import math

import jax
import jax.numpy as jnp
from jax import lax
from jax.experimental import pallas as pl
from jax.experimental.pallas import tpu as pltpu
from jax.sharding import PartitionSpec as P

PLASTIC_GAIN = 6.0 / 3.1
YIELD_OFFSET = 0.05
CONTACT_STIFF = 4.0
CG_STEPS = 3
NEWTON = 2
ROOT_THIRD = 1.0 / math.sqrt(3.0)
THIRD = 1.0 / 3.0
SPAN = 10.0

HALO = 3
OX, OY, DZ = 9, 16, 128
WX = OX + 2 * HALO
WE = WX - 1
WY = 24
F32 = jnp.float32

FLOW_SENT = (0, 1, 3, 4, 5)
NEL = 14
CONTACT_AT = 13
ZZ_AT = 14


def lanes():
    return lax.broadcasted_iota(jnp.int32, (8, DZ), 1)


def z_pair(value, first_lane):
    low = jnp.where(first_lane, 0.0, pltpu.roll(value, 1, 1))
    return value + low, value - low


def z_merge(total, slope, last_lane):
    return total + slope + jnp.where(last_lane, 0.0, pltpu.roll(total - slope, DZ - 1, 1))


def to_points(s1, sx, sy, sz, syz, sxz, sxy):
    points = []
    for sign_x in (-1, 1):
        a0 = s1 + sx if sign_x > 0 else s1 - sx
        ay = sy + sxy if sign_x > 0 else sy - sxy
        az = sz + sxz if sign_x > 0 else sz - sxz
        for sign_y in (-1, 1):
            b0 = a0 + ay if sign_y > 0 else a0 - ay
            bz = az + syz if sign_y > 0 else az - syz
            points += [b0 - bz, b0 + bz]
    return points


def from_points(t):
    per_x = []
    for i in range(2):
        e0 = [t[4 * i + 2 * j + 1] + t[4 * i + 2 * j] for j in range(2)]
        ez = [t[4 * i + 2 * j + 1] - t[4 * i + 2 * j] for j in range(2)]
        per_x.append((e0[1] + e0[0], e0[1] - e0[0], ez[1] + ez[0], ez[1] - ez[0]))
    low, high = per_x
    t1, ty, tz, tyz = (high[m] + low[m] for m in range(4))
    tx, txy, txz = (high[m] - low[m] for m in range(3))
    return t1, tx, ty, tz, tyz, txz, txy


def plastic_forces(n, t):
    nxx, nyy, nzz, nxy, nyz, nzx = n
    t1, tx, ty, tz, tyz, txz, txy = t
    tx, ty, tz = tx * ROOT_THIRD, ty * ROOT_THIRD, tz * ROOT_THIRD
    tyz, txz, txy = tyz * THIRD, txz * THIRD, txy * THIRD
    a_xy, a_yz, a_zx = nxy * t1, nyz * t1, nzx * t1
    fx = [nxx * t1, a_xy, a_zx]
    fy = [a_xy, nyy * t1, a_yz]
    fz = [a_zx, a_yz, nzz * t1]
    xy_z, yz_x, zx_y = nxy * tz, nyz * tx, nzx * ty
    fxy = [nxx * ty + nxy * tx, nxy * ty + nyy * tx, zx_y + yz_x]
    fxz = [nxx * tz + nzx * tx, xy_z + yz_x, nzx * tz + nzz * tx]
    fyz = [xy_z + zx_y, nyy * tz + nyz * ty, nyz * tz + nzz * ty]
    fxyz = [
        nxx * tyz + nxy * txz + nzx * txy,
        nxy * tyz + nyy * txz + nyz * txy,
        nzx * tyz + nyz * txz + nzz * txy,
    ]
    return fx, fy, fz, fxy, fxz, fyz, fxyz


def element_core(modes, n, flags):
    ax, ay, az, axy, axz, ayz, axyz = modes
    nxx, nyy, nzz, nxy, nyz, nzx = n
    sh_xy, sh_yz, sh_zx = ax[1] + ay[0], ay[2] + az[1], az[0] + ax[2]
    k_x, k_y, k_z = axy[2] + axz[1], axy[2] + ayz[0], axz[1] + ayz[0]
    s1 = (nxx * ax[0] + nyy * ay[1] + nzz * az[2]) + (nxy * sh_xy + nyz * sh_yz + nzx * sh_zx)
    sx = (nxy * axy[0] + nyy * axy[1]) + (nyz * k_x + nzx * axz[0] + nzz * axz[2])
    sy = (nxx * axy[0] + nxy * axy[1]) + (nzx * k_y + nyz * ayz[1] + nzz * ayz[2])
    sz = (nxx * axz[0] + nxy * k_z) + (nzx * axz[2] + nyy * ayz[1] + nyz * ayz[2])
    syz = nxx * axyz[0] + nxy * axyz[1] + nzx * axyz[2]
    sxz = nxy * axyz[0] + nyy * axyz[1] + nyz * axyz[2]
    sxy = nzx * axyz[0] + nyz * axyz[1] + nzz * axyz[2]
    values = to_points(
        s1, sx * ROOT_THIRD, sy * ROOT_THIRD, sz * ROOT_THIRD, syz * THIRD, sxz * THIRD, sxy * THIRD
    )
    plastic = plastic_forces(n, from_points([value * flag for value, flag in zip(values, flags)]))
    trace = ax[0] + ay[1] + az[2]
    tr_x, tr_y, tr_z = (
        (axy[1] + axz[2]) * THIRD,
        (axy[0] + ayz[2]) * THIRD,
        (axz[0] + ayz[1]) * THIRD,
    )
    mixed = (k_x + ayz[0]) * THIRD
    elastic = (
        [trace + (ax[0] + ax[0]), sh_xy, sh_zx],
        [sh_xy, trace + (ay[1] + ay[1]), sh_yz],
        [sh_zx, sh_yz, trace + (az[2] + az[2])],
        [tr_y + axy[0], tr_x + axy[1], mixed + axy[2] * THIRD],
        [tr_z + axz[0], mixed + axz[1] * THIRD, tr_x + axz[2]],
        [mixed + ayz[0] * THIRD, tr_z + ayz[1], tr_y + ayz[2]],
        [axyz[c] * (5.0 / 9.0) for c in range(3)],
    )
    return [[elastic[m][c] + plastic[m][c] for c in range(3)] for m in range(7)]


def scatter_x(forces, behind):
    fx, fy, fz, fxy, fxz, fyz, fxyz = forces
    node, ahead = [], []
    for c in range(3):
        node += [
            behind[4 * c] - fx[c],
            behind[4 * c + 1] + (fy[c] - fxy[c]),
            behind[4 * c + 2] + (fz[c] - fxz[c]),
            behind[4 * c + 3] + (fyz[c] - fxyz[c]),
        ]
        ahead += [fx[c], fy[c] + fxy[c], fz[c] + fxz[c], fyz[c] + fxyz[c]]
    return node, ahead


def store_y(node, lower_ref, upper_ref, x, row, upper_keep=None):
    for c in range(3):
        ss, sd, ds, dd = node[4 * c : 4 * c + 4]
        lower_ref[2 * c, x, row : row + 8] = ss - sd
        lower_ref[2 * c + 1, x, row : row + 8] = ds - dd
        up_s, up_d = ss + sd, ds + dd
        if upper_keep is not None:
            up_s, up_d = jnp.where(upper_keep, up_s, 0.0), jnp.where(upper_keep, up_d, 0.0)
        upper_ref[2 * c, x, row + 8 : row + 16] = up_s
        upper_ref[2 * c + 1, x, row + 8 : row + 16] = up_d


def merge_yz(lower_ref, upper_ref, c, x, row, last_lane):
    total = lower_ref[2 * c, x, row : row + 8] + upper_ref[2 * c, x, row + 7 : row + 15]
    slope = lower_ref[2 * c + 1, x, row : row + 8] + upper_ref[2 * c + 1, x, row + 7 : row + 15]
    return z_merge(total, slope, last_lane)


def place():
    index_x, index_y = lax.axis_index("gx"), lax.axis_index("gy")
    return (
        index_x == 0,
        index_x == lax.axis_size("gx") - 1,
        index_y == 0,
        index_y == lax.axis_size("gy") - 1,
    )


def ask(flag):
    return jnp.where(flag, 0.0, 1.0).astype(F32)


def offset_kernel(load_hbm, flags_hbm, flow_hbm, active_ref, die_ref,
                  part_ref, right_ref, left_ref, up_ref, down_ref, contact_ref,
                  lower_ref, upper_ref, load_ref, flags_ref, flow_ref, load_sem, flags_sem, flow_sem):
    copies = [
        [pltpu.make_async_copy(source.at[m], target.at[m], sem.at[m]) for m in range(source.shape[0])]
        for source, target, sem in (
            (flags_hbm, flags_ref, flags_sem), (flow_hbm, flow_ref, flow_sem), (load_hbm, load_ref, load_sem))
    ]
    for group in copies:
        for copy in group:
            copy.start()
    lane = lanes()
    last_lane = lane == DZ - 1
    zero = jnp.zeros((8, DZ), F32)
    last = lax.broadcasted_iota(jnp.int32, (OY, DZ), 1) == DZ - 1
    same = lax.broadcasted_iota(jnp.int32, (OY, OY), 0) == lax.broadcasted_iota(jnp.int32, (OY, OY), 1)

    def on_rows(row):
        return jnp.sum(jnp.where(same, jnp.broadcast_to(row, (OY, OY)), 0.0), axis=1, keepdims=True)

    die_rows = []
    for x in range(OX):
        stiff = CONTACT_STIFF * active_ref[x : x + 1].astype(F32)
        contact_ref[x] = jnp.where(last, on_rows(stiff), 0.0)
        die_rows.append(jnp.where(last, on_rows(stiff * die_ref[x : x + 1]), 0.0))

    def clear(x, _):
        for m in range(6):
            lower_ref[m, x, 16:24] = zero
            upper_ref[m, x, 0:8] = zero
        return 0

    lax.fori_loop(0, OX + 1, clear, 0)
    for group in copies[:2]:
        for copy in group:
            copy.wait()
    for row in (0, 8):

        def element(x, behind):
            flags = [flags_ref[q, x, row : row + 8].astype(F32) * (0.5 * PLASTIC_GAIN * YIELD_OFFSET) for q in range(8)]
            n = [flow_ref[m, x, row : row + 8] for m in range(6)]
            node, ahead = scatter_x(plastic_forces(n, from_points(flags)), behind)
            store_y(node, lower_ref, upper_ref, x, row)
            return ahead

        behind = lax.fori_loop(0, OX, element, [zero] * 12)
        store_y(behind, lower_ref, upper_ref, OX, row)

    def finish(x, _):
        for c in range(3):
            for row in (0, 8, 16):
                part_ref[c, x, row : row + 8] = merge_yz(lower_ref, upper_ref, c, x, row, last_lane) * (-1.0 / 16.0)
        return 0

    lax.fori_loop(0, OX + 1, finish, 0, unroll=2)
    for copy in copies[2]:
        copy.wait()
    for x in range(OX):
        for c in range(3):
            value = part_ref[c, x, 0:OY] + load_ref[c, x]
            part_ref[c, x, 0:OY] = value + die_rows[x] if c == 2 else value

    def field(f, x, rows):
        if f < 8:
            return flags_ref[f, x, rows].astype(F32) * (-PLASTIC_GAIN / 8.0)
        if f < CONTACT_AT:
            return flow_ref[FLOW_SENT[f - 8], x, rows]
        return contact_ref[x, rows]

    whole = slice(0, OY)
    for f in range(NEL):
        for i in range(3):
            right_ref[3 * f + i] = field(f, 6 + i, whole)
        for i in range(2):
            left_ref[2 * f + i] = field(f, i, whole)
    for c in range(3):
        for i in range(4):
            right_ref[42 + 4 * c + i] = part_ref[c, 6 + i, 0:16]
            right_ref[54, 4 * c + i : 4 * c + i + 1] = part_ref[c, 6 + i, 16:17]
        for i in range(3):
            left_ref[28 + 3 * c + i] = part_ref[c, i, 0:16]
            left_ref[37, 3 * c + i : 3 * c + i + 1] = part_ref[c, i, 16:17]

    def slabs(x, _):
        for f in range(NEL):
            up_ref[x, 3 * f : 3 * f + 3] = field(f, x, slice(13, 16))
            down_ref[x, 2 * f : 2 * f + 2] = field(f, x, slice(0, 2))
        return 0

    lax.fori_loop(0, OX, slabs, 0)

    def part_slabs(x, _):
        for c in range(3):
            up_ref[x, 42 + 4 * c : 46 + 4 * c] = part_ref[c, x, 13:17]
            down_ref[x, 28 + 3 * c : 31 + 3 * c] = part_ref[c, x, 0:3]
        return 0

    lax.fori_loop(0, OX + 1, part_slabs, 0)


def three_steps(els_ref, basis, z_ref, lower_ref, upper_ref):
    at_first_x, at_last_x, at_first_y, at_last_y = place()
    lane = lanes()
    first_lane, last_lane = lane == 0, lane == DZ - 1
    rows = lax.broadcasted_iota(jnp.int32, (8, DZ), 0)
    keep_upper = jnp.logical_or(rows >= HALO, jnp.logical_not(at_first_y))
    keep_node = jnp.logical_or(rows < HALO, jnp.logical_not(at_last_y))
    zero = jnp.zeros((8, DZ), F32)

    def clear(x, _):
        for m in range(6):
            z_ref[m, x, 24:32] = zero
            upper_ref[m, x, 0:8] = zero
        return 0

    lax.fori_loop(0, WX, clear, 0)

    def first(x, _):
        for row in (0, 8, 16):
            for c in range(3):
                z_ref[2 * c, x, row : row + 8], z_ref[2 * c + 1, x, row : row + 8] = z_pair(
                    basis[0][c, x, row : row + 8], first_lane
                )
        return 0

    lax.fori_loop(0, WX, first, 0, unroll=5)

    for step in range(1, HALO + 1):
        start, end = step - 1, WX - 1 - step
        scale = (2.0 if step == 1 else 4.0) / SPAN
        for row in (0, 8, 16):

            def plane(x):
                values = []
                for m in range(6):
                    low, high = z_ref[m, x, row : row + 8], z_ref[m, x, row + 1 : row + 9]
                    values += [high + low, high - low]
                return values

            def element(x, carry):
                before, behind = carry
                after = plane(x + 1)
                p, q = before, after
                modes = (
                    [q[4 * c] - p[4 * c] for c in range(3)],
                    [q[4 * c + 1] + p[4 * c + 1] for c in range(3)],
                    [q[4 * c + 2] + p[4 * c + 2] for c in range(3)],
                    [q[4 * c + 1] - p[4 * c + 1] for c in range(3)],
                    [q[4 * c + 2] - p[4 * c + 2] for c in range(3)],
                    [q[4 * c + 3] + p[4 * c + 3] for c in range(3)],
                    [q[4 * c + 3] - p[4 * c + 3] for c in range(3)],
                )
                here = [els_ref[f, x, row : row + 8] for f in range(NEL + 1) if f != CONTACT_AT]
                n = (here[8], here[9], here[13], here[10], here[11], here[12])
                node, ahead = scatter_x(element_core(modes, n, here[:8]), behind)
                store_y(node, lower_ref, upper_ref, x, row, keep_upper if row == 0 else None)
                return after, ahead

            carry = (plane(start), [zero] * 12)
            for x in range(start, HALO):
                carry = element(x, carry)
            carry = (carry[0], [jnp.where(at_first_x, 0.0, value) for value in carry[1]])
            first_pair = HALO + (end + 1 - HALO) % 2
            if first_pair > HALO:
                carry = element(HALO, carry)

            def pair(k, carry):
                x = first_pair + 2 * k
                return element(x + 1, element(x, carry))

            lax.fori_loop(0, (end + 1 - first_pair) // 2, pair, carry)

        for x in range(step, end + 1):
            for row in (0, 8, 16):
                for c in range(3):
                    here = basis[step - 1][c, x, row : row + 8]
                    value = merge_yz(lower_ref, upper_ref, c, x, row, last_lane) * (scale / 16.0)
                    if c == 2:
                        value = value + (els_ref[CONTACT_AT, x, row : row + 8] * scale) * here
                    if step == 1:
                        value = value - here
                    else:
                        value = value - (here + here) - basis[step - 2][c, x, row : row + 8]
                    if x >= HALO + OX:
                        value = jnp.where(at_last_x, 0.0, value)
                    if row == 16:
                        value = jnp.where(keep_node, value, 0.0)
                    basis[step][c, x, row : row + 8] = value
                    if step < HALO:
                        z_ref[2 * c, x, row : row + 8], z_ref[2 * c + 1, x, row : row + 8] = z_pair(value, first_lane)


def sum_rows(values):
    return jnp.sum(values, axis=0, keepdims=True)


def first_kernel(flags_ref, flow_ref, contact_ref, part_ref, left_ref, right_ref, down_ref, up_ref, cl_ref, cr_ref,
                 els_ref, own_ref, dots_ref, right_out, left_out, up_out, down_out,
                 b0, b1, b2, b3, z_ref, lower_ref, upper_ref):
    at_first_x, at_last_x, at_first_y, at_last_y = place()
    has_l, has_r, has_d, has_u = ask(at_first_x), ask(at_last_x), ask(at_first_y), ask(at_last_y)
    zero = jnp.zeros((8, DZ), F32)
    low, high = slice(0, 3), slice(19, 21)
    mid = slice(HALO, HALO + OY)

    def clear(x, _):
        for f in range(NEL):
            els_ref[f, x, 16:24] = zero
        return 0

    lax.fori_loop(0, WE, clear, 0)

    def clear_start(x, _):
        for c in range(3):
            for row in (0, 8, 16):
                b0[c, x, row : row + 8] = zero
        return 0

    lax.fori_loop(0, WX, clear_start, 0)

    def own(x, _):
        w = x + HALO
        for f in range(NEL):
            if f < 8:
                value = flags_ref[f, x].astype(F32) * (-PLASTIC_GAIN / 8.0)
            elif f < CONTACT_AT:
                value = flow_ref[FLOW_SENT[f - 8], x]
            else:
                value = contact_ref[x]
            els_ref[f, w, mid] = value
            els_ref[f, w, low] = down_ref[x, 3 * f : 3 * f + 3]
            els_ref[f, w, high] = up_ref[x, 2 * f : 2 * f + 2]
        for c in range(3):
            b0[c, w, mid] = part_ref[c, x, 0:16]
            b0[c, w, 19:20] = part_ref[c, x, 16:17] * has_u
        return 0

    lax.fori_loop(0, OX, own, 0)
    for c in range(3):
        b0[c, 12, mid] = part_ref[c, OX, 0:16] * has_r
        b0[c, 12, 19:20] = part_ref[c, OX, 16:17] * (has_r * has_u)
    for i in range(3):
        for f in range(NEL):
            els_ref[f, i, mid] = left_ref[3 * f + i]
            els_ref[f, i, low] = cl_ref[i, 3 * f : 3 * f + 3]
            els_ref[f, i, high] = cl_ref[i, 56 + 2 * f : 58 + 2 * f]
    for i in range(2):
        for f in range(NEL):
            els_ref[f, 12 + i, mid] = right_ref[2 * f + i]
            els_ref[f, 12 + i, low] = cr_ref[i, 3 * f : 3 * f + 3]
            els_ref[f, 12 + i, high] = cr_ref[i, 56 + 2 * f : 58 + 2 * f]

    def zz(x, _):
        for row in (0, 8, 16):
            els_ref[ZZ_AT, x, row : row + 8] = -(els_ref[8, x, row : row + 8] + els_ref[9, x, row : row + 8])
        return 0

    lax.fori_loop(0, WE, zz, 0)

    for c in range(3):
        for i in range(4):
            b0[c, i, mid] += left_ref[42 + 4 * c + i] * has_l
            b0[c, i, 19:20] += left_ref[54, 4 * c + i : 4 * c + i + 1] * (has_l * has_u)
            b0[c, i, 0:4] += cl_ref[i, 42 + 4 * c : 46 + 4 * c] * (has_l * has_d)
            b0[c, i, 19:22] += cl_ref[i, 84 + 3 * c : 87 + 3 * c] * (has_l * has_u)
        for i in range(3):
            b0[c, 12 + i, mid] += right_ref[28 + 3 * c + i] * has_r
            b0[c, 12 + i, 19:20] += right_ref[37, 3 * c + i : 3 * c + i + 1] * (has_r * has_u)
            b0[c, 12 + i, 0:4] += cr_ref[i, 42 + 4 * c : 46 + 4 * c] * (has_r * has_d)
            b0[c, 12 + i, 19:22] += cr_ref[i, 84 + 3 * c : 87 + 3 * c] * (has_r * has_u)

    def edges(x, _):
        inside = jnp.where(x == OX, has_r, 1.0)
        for c in range(3):
            b0[c, x + HALO, 0:4] += down_ref[x, 42 + 4 * c : 46 + 4 * c] * (inside * has_d)
            b0[c, x + HALO, 19:22] += up_ref[x, 28 + 3 * c : 31 + 3 * c] * (inside * has_u)
        return 0

    lax.fori_loop(0, OX + 1, edges, 0)

    basis = (b0, b1, b2, b3)
    three_steps(els_ref, basis, z_ref, lower_ref, upper_ref)

    def collect(x, sums):
        sums = list(sums)
        for row in (0, 8):
            for c in range(3):
                v = [b[c, x + HALO, row + HALO : row + HALO + 8] for b in basis]
                for k in range(4):
                    own_ref[k, c, x, row : row + 8] = v[k]
                for k in range(7):
                    sums[k] = sums[k] + v[k // 2] * v[k - k // 2]
        return tuple(sums)

    sums = lax.fori_loop(0, OX, collect, (zero,) * 7)
    dots_ref[...] = zero
    for k in range(7):
        dots_ref[k : k + 1] = sum_rows(sums[k])

    for i in range(3):
        for c in range(3):
            for out, x in ((right_out, 9 + i), (left_out, 3 + i)):
                out[3 * c + i] = b3[c, x, mid]
                out[9 + i, 3 * c : 3 * c + 3] = b3[c, x, 16:19]
                out[12 + i, 3 * c : 3 * c + 3] = b3[c, x, 3:6]

    def slabs(x, _):
        for c in range(3):
            up_out[x, 3 * c : 3 * c + 3] = b3[c, x + HALO, 16:19]
            down_out[x, 3 * c : 3 * c + 3] = b3[c, x + HALO, 3:6]
        return 0

    lax.fori_loop(0, OX, slabs, 0)


def second_kernel(els_ref, own_ref, dots_ref, left_ref, right_ref, down_ref, up_ref,
                  tail_ref, row_ref, b0, b1, b2, b3, z_ref, lower_ref, upper_ref):
    _, at_last_x, _, at_last_y = place()
    has_r, has_u = ask(at_last_x), ask(at_last_y)
    zero = jnp.zeros((8, DZ), F32)
    mid = slice(HALO, HALO + OY)

    def own(x, _):
        for c in range(3):
            b0[c, x + HALO, mid] = own_ref[3, c, x]
        return 0

    def edges(x, _):
        inside = jnp.where(x >= HALO + OX, has_r, 1.0)
        for c in range(3):
            b0[c, x, 16:24] = zero
            b0[c, x, 0:3] = down_ref[x, 3 * c : 3 * c + 3] * inside
            b0[c, x, 19:22] = up_ref[x, 3 * c : 3 * c + 3] * (inside * has_u)
        return 0

    lax.fori_loop(0, WX, edges, 0)
    lax.fori_loop(0, OX, own, 0)
    for c in range(3):
        for i in range(3):
            b0[c, i, mid] = left_ref[3 * c + i]
            b0[c, 12 + i, mid] = right_ref[3 * c + i] * has_r

    basis = (b0, b1, b2, b3)
    three_steps(els_ref, basis, z_ref, lower_ref, upper_ref)

    def collect(x, sums):
        sums = list(sums)
        for row in (0, 8):
            for c in range(3):
                v = [own_ref[3, c, x, row : row + 8]]
                for k in range(1, 4):
                    w = b_at(basis[k], c, x, row)
                    v.append((w + w) - own_ref[3 - k, c, x, row : row + 8])
                    tail_ref[k - 1, c, x, row : row + 8] = v[k]
                for k in range(1, 6):
                    sums[k - 1] = sums[k - 1] + v[k // 2] * v[k - k // 2]
        return tuple(sums)

    sums = lax.fori_loop(0, OX, collect, (zero,) * 5)
    lane = lax.broadcasted_iota(jnp.int32, (1, DZ), 1)
    line = jnp.zeros((1, DZ), F32)
    for k in range(12):
        dot = dots_ref[k : k + 1] if k < 7 else sum_rows(sums[k - 7])
        line = jnp.where(lane == k, jnp.sum(dot, axis=1, keepdims=True), line)
    row_ref[...] = jnp.broadcast_to(line, row_ref.shape)


def b_at(ref, c, x, row):
    return ref[c, x + HALO, row + HALO : row + HALO + 8]


def times_matrix(p):
    out = [None] * (len(p) + 1)

    def add(k, value):
        out[k] = value if out[k] is None else out[k] + value

    for k, value in enumerate(p):
        add(k, value * (SPAN / 2))
        if k == 0:
            add(1, value * (SPAN / 2))
        else:
            add(k + 1, value * (SPAN / 4))
            add(k - 1, value * (SPAN / 4))
    return out


def tree_sum(values):
    while len(values) > 1:
        values = [a + b for a, b in zip(values[::2], values[1::2])] + ([values[-1]] if len(values) % 2 else [])
    return values[0]


def combine(p, a, q):
    out = []
    for k in range(max(len(p), len(q))):
        term = a * q[k] if k < len(q) else None
        if k < len(p):
            term = p[k] if term is None else p[k] + term
        out.append(term)
    return out


def coefficients(mu):
    gram = [[0.5 * (mu[i + j] + mu[abs(i - j)]) if i + j < len(mu) else None for j in range(7)] for i in range(7)]

    def inner(p, q):
        return tree_sum([p[i] * tree_sum([gram[i][j] * q[j] for j in range(len(q))]) for i in range(len(p))])

    remain = [jnp.ones_like(mu[0])]
    total = []
    for newton in range(NEWTON):
        direction = remain
        norm = inner(remain, remain)
        for step in range(CG_STEPS):
            image = times_matrix(direction)
            alpha = norm / inner(direction, image)
            total = combine(total, alpha, direction)
            remain = combine(remain, -alpha, image)
            if step + 1 < CG_STEPS:
                norm_next = inner(remain, remain)
                direction = combine(remain, norm_next / norm, direction)
                norm = norm_next
    return total, remain


def last_kernel(dots_ref, own_ref, tail_ref, displacement_ref, residual_ref):
    sums = jnp.sum(dots_ref[...], axis=0, keepdims=True)
    dots = [jnp.broadcast_to(sums[:, k : k + 1], (1, DZ)) for k in range(12)]
    mu = dots[:2]
    for k in range(2, 12):
        mu.append((dots[k] + dots[k]) - mu[k % 2])
    total, remain = coefficients(mu)
    total = [jnp.broadcast_to(value, (8, DZ)) for value in total]
    remain = [jnp.broadcast_to(value, (8, DZ)) for value in remain]

    def write(x, _):
        for row in (0, 8):
            for c in range(3):
                v = [own_ref[k, c, x, row : row + 8] for k in range(4)]
                v += [tail_ref[k, c, x, row : row + 8] for k in range(3)]
                displacement_ref[c, x, row : row + 8] = tree_sum([a * b for a, b in zip(total, v)])
                residual_ref[c, x, row : row + 8] = tree_sum([a * b for a, b in zip(remain, v)])
        return 0

    lax.fori_loop(0, OX, write, 0)


def shape(*dims):
    return jax.ShapeDtypeStruct(dims, F32)


def call(kernel, outs, scratch=(), mebibytes=24, **more):
    return pl.pallas_call(
        kernel,
        out_shape=outs,
        scratch_shapes=[pltpu.VMEM(dims, F32) if isinstance(dims, tuple) else dims for dims in scratch],
        compiler_params=pltpu.CompilerParams(vmem_limit_bytes=mebibytes * 1024 * 1024),
        **more,
    )


STEP_SCRATCH = [(3, WX, WY, DZ)] * 4 + [(6, WX, WY + 8, DZ)] * 3


def rotate(value, axis, steps):
    count = lax.axis_size(axis)
    return lax.ppermute(value, axis, [(i, (i + steps) % count) for i in range(count)])


def exchange(right, left, up, down, top):
    from_left = rotate(right, "gx", 1)
    from_right = rotate(left, "gx", -1)
    from_down = rotate(up, "gy", 1)
    from_up = rotate(down, "gy", -1)
    corners = jnp.concatenate([from_down, from_up], axis=1)
    corner_left = rotate(corners[6:top], "gx", 1)
    corner_right = rotate(corners[0:3], "gx", -1)
    return from_left, from_right, from_down, from_up, corner_left, corner_right


def exchange_in_turn(right, left, up, down):
    from_left = rotate(right, "gx", 1)
    from_right = rotate(left, "gx", -1)
    up = jnp.concatenate([from_left[9:12], up, from_right[9:12]], axis=0)
    down = jnp.concatenate([from_left[12:15], down, from_right[12:15]], axis=0)
    return from_left, from_right, rotate(up, "gy", 1), rotate(down, "gy", -1)


def body(load, plastic_flags, flow_dir, contact_flags, die_depth):
    hbm, vmem = pl.BlockSpec(memory_space=pltpu.HBM), pl.BlockSpec(memory_space=pltpu.VMEM)
    part, right, left, up, down, contact = call(
        offset_kernel,
        [shape(3, OX + 1, WY, DZ), shape(55, OY, DZ), shape(38, OY, DZ), shape(OX + 1, 56, DZ),
         shape(OX + 1, 40, DZ), shape(OX, OY, DZ)],
        [(6, OX + 1, WY + 8, DZ)] * 2
        + [(3, OX, OY, DZ), pltpu.VMEM((8, OX, OY, DZ), jnp.int32), (6, OX, OY, DZ)]
        + [pltpu.SemaphoreType.DMA((count,)) for count in (3, 8, 6)],
        in_specs=[hbm, hbm, hbm, vmem, vmem],
    )(load, plastic_flags, flow_dir, contact_flags, die_depth)
    halos = exchange(right, left, up, down, 10)
    els, own, dots, right, left, up, down = call(
        first_kernel,
        [shape(NEL + 1, WE, WY, DZ), shape(4, 3, OX, OY, DZ), shape(8, DZ), shape(15, OY, DZ), shape(15, OY, DZ),
         shape(OX, 16, DZ), shape(OX, 16, DZ)],
        STEP_SCRATCH,
    )(plastic_flags, flow_dir, contact, part, *halos)
    halos = exchange_in_turn(right, left, up, down)
    count = lax.axis_size("gx") * lax.axis_size("gy")
    tail, line = call(
        second_kernel, [shape(3, 3, OX, OY, DZ), shape(count, DZ)], STEP_SCRATCH
    )(els, own, dots, *halos)
    lines = lax.all_to_all(line, ("gx", "gy"), 0, 0, tiled=True)
    return tuple(call(last_kernel, [shape(3, OX, OY, DZ)] * 2)(lines, own, tail))


def solution(mesh):
    in_specs = (
        P(None, "gx", "gy", None),
        P(None, "gx", "gy", None),
        P(None, "gx", "gy", None),
        P("gx", "gy"),
        P("gx", "gy"),
    )
    out_specs = (P(None, "gx", "gy", None), P(None, "gx", "gy", None))
    return jax.shard_map(body, mesh=mesh, in_specs=in_specs, out_specs=out_specs, check_vma=False)
```

```python
import math

import jax
import jax.numpy as jnp
from jax import lax
from jax.experimental import pallas as pl
from jax.experimental.pallas import tpu as pltpu
from jax.sharding import PartitionSpec as P

PLASTIC_GAIN = 6.0 / 3.1
YIELD_OFFSET = 0.05
CONTACT_STIFF = 4.0
CG_STEPS = 3
NEWTON = 2
ROOT_THIRD = 1.0 / math.sqrt(3.0)
THIRD = 1.0 / 3.0
SPAN = 10.0

HALO = 3
OX, OY, DZ = 9, 16, 128
WX = OX + 2 * HALO
WE = WX - 1
WY = 24
F32 = jnp.float32

FLOW_SENT = (0, 1, 3, 4, 5)
NEL = 14
CONTACT_AT = 13
ZZ_AT = 14


def lanes():
    return lax.broadcasted_iota(jnp.int32, (8, DZ), 1)


def z_pair(value, first_lane):
    low = jnp.where(first_lane, 0.0, pltpu.roll(value, 1, 1))
    return value + low, value - low


def z_merge(total, slope, last_lane):
    return total + slope + jnp.where(last_lane, 0.0, pltpu.roll(total - slope, DZ - 1, 1))


def to_points(s1, sx, sy, sz, syz, sxz, sxy):
    points = []
    for sign_x in (-1, 1):
        a0 = s1 + sx if sign_x > 0 else s1 - sx
        ay = sy + sxy if sign_x > 0 else sy - sxy
        az = sz + sxz if sign_x > 0 else sz - sxz
        for sign_y in (-1, 1):
            b0 = a0 + ay if sign_y > 0 else a0 - ay
            bz = az + syz if sign_y > 0 else az - syz
            points += [b0 - bz, b0 + bz]
    return points


def from_points(t):
    per_x = []
    for i in range(2):
        e0 = [t[4 * i + 2 * j + 1] + t[4 * i + 2 * j] for j in range(2)]
        ez = [t[4 * i + 2 * j + 1] - t[4 * i + 2 * j] for j in range(2)]
        per_x.append((e0[1] + e0[0], e0[1] - e0[0], ez[1] + ez[0], ez[1] - ez[0]))
    low, high = per_x
    t1, ty, tz, tyz = (high[m] + low[m] for m in range(4))
    tx, txy, txz = (high[m] - low[m] for m in range(3))
    return t1, tx, ty, tz, tyz, txz, txy


def plastic_forces(n, t):
    nxx, nyy, nzz, nxy, nyz, nzx = n
    t1, tx, ty, tz, tyz, txz, txy = t
    tx, ty, tz = tx * ROOT_THIRD, ty * ROOT_THIRD, tz * ROOT_THIRD
    tyz, txz, txy = tyz * THIRD, txz * THIRD, txy * THIRD
    a_xy, a_yz, a_zx = nxy * t1, nyz * t1, nzx * t1
    fx = [nxx * t1, a_xy, a_zx]
    fy = [a_xy, nyy * t1, a_yz]
    fz = [a_zx, a_yz, nzz * t1]
    xy_z, yz_x, zx_y = nxy * tz, nyz * tx, nzx * ty
    fxy = [nxx * ty + nxy * tx, nxy * ty + nyy * tx, zx_y + yz_x]
    fxz = [nxx * tz + nzx * tx, xy_z + yz_x, nzx * tz + nzz * tx]
    fyz = [xy_z + zx_y, nyy * tz + nyz * ty, nyz * tz + nzz * ty]
    fxyz = [
        nxx * tyz + nxy * txz + nzx * txy,
        nxy * tyz + nyy * txz + nyz * txy,
        nzx * tyz + nyz * txz + nzz * txy,
    ]
    return fx, fy, fz, fxy, fxz, fyz, fxyz


def element_core(modes, n, flags):
    ax, ay, az, axy, axz, ayz, axyz = modes
    nxx, nyy, nzz, nxy, nyz, nzx = n
    sh_xy, sh_yz, sh_zx = ax[1] + ay[0], ay[2] + az[1], az[0] + ax[2]
    k_x, k_y, k_z = axy[2] + axz[1], axy[2] + ayz[0], axz[1] + ayz[0]
    s1 = (nxx * ax[0] + nyy * ay[1] + nzz * az[2]) + (nxy * sh_xy + nyz * sh_yz + nzx * sh_zx)
    sx = (nxy * axy[0] + nyy * axy[1]) + (nyz * k_x + nzx * axz[0] + nzz * axz[2])
    sy = (nxx * axy[0] + nxy * axy[1]) + (nzx * k_y + nyz * ayz[1] + nzz * ayz[2])
    sz = (nxx * axz[0] + nxy * k_z) + (nzx * axz[2] + nyy * ayz[1] + nyz * ayz[2])
    syz = nxx * axyz[0] + nxy * axyz[1] + nzx * axyz[2]
    sxz = nxy * axyz[0] + nyy * axyz[1] + nyz * axyz[2]
    sxy = nzx * axyz[0] + nyz * axyz[1] + nzz * axyz[2]
    values = to_points(
        s1, sx * ROOT_THIRD, sy * ROOT_THIRD, sz * ROOT_THIRD, syz * THIRD, sxz * THIRD, sxy * THIRD
    )
    plastic = plastic_forces(n, from_points([value * flag for value, flag in zip(values, flags)]))
    trace = ax[0] + ay[1] + az[2]
    tr_x, tr_y, tr_z = (
        (axy[1] + axz[2]) * THIRD,
        (axy[0] + ayz[2]) * THIRD,
        (axz[0] + ayz[1]) * THIRD,
    )
    mixed = (k_x + ayz[0]) * THIRD
    elastic = (
        [trace + (ax[0] + ax[0]), sh_xy, sh_zx],
        [sh_xy, trace + (ay[1] + ay[1]), sh_yz],
        [sh_zx, sh_yz, trace + (az[2] + az[2])],
        [tr_y + axy[0], tr_x + axy[1], mixed + axy[2] * THIRD],
        [tr_z + axz[0], mixed + axz[1] * THIRD, tr_x + axz[2]],
        [mixed + ayz[0] * THIRD, tr_z + ayz[1], tr_y + ayz[2]],
        [axyz[c] * (5.0 / 9.0) for c in range(3)],
    )
    return [[elastic[m][c] + plastic[m][c] for c in range(3)] for m in range(7)]


def scatter_x(forces, behind):
    fx, fy, fz, fxy, fxz, fyz, fxyz = forces
    node, ahead = [], []
    for c in range(3):
        node += [
            behind[4 * c] - fx[c],
            behind[4 * c + 1] + (fy[c] - fxy[c]),
            behind[4 * c + 2] + (fz[c] - fxz[c]),
            behind[4 * c + 3] + (fyz[c] - fxyz[c]),
        ]
        ahead += [fx[c], fy[c] + fxy[c], fz[c] + fxz[c], fyz[c] + fxyz[c]]
    return node, ahead


def store_y(node, lower_ref, upper_ref, x, row, upper_keep=None):
    for c in range(3):
        ss, sd, ds, dd = node[4 * c : 4 * c + 4]
        lower_ref[2 * c, x, row : row + 8] = ss - sd
        lower_ref[2 * c + 1, x, row : row + 8] = ds - dd
        up_s, up_d = ss + sd, ds + dd
        if upper_keep is not None:
            up_s, up_d = jnp.where(upper_keep, up_s, 0.0), jnp.where(upper_keep, up_d, 0.0)
        upper_ref[2 * c, x, row + 8 : row + 16] = up_s
        upper_ref[2 * c + 1, x, row + 8 : row + 16] = up_d


def merge_yz(lower_ref, upper_ref, c, x, row, last_lane):
    total = lower_ref[2 * c, x, row : row + 8] + upper_ref[2 * c, x, row + 7 : row + 15]
    slope = lower_ref[2 * c + 1, x, row : row + 8] + upper_ref[2 * c + 1, x, row + 7 : row + 15]
    return z_merge(total, slope, last_lane)


def place():
    index_x, index_y = lax.axis_index("gx"), lax.axis_index("gy")
    return (
        index_x == 0,
        index_x == lax.axis_size("gx") - 1,
        index_y == 0,
        index_y == lax.axis_size("gy") - 1,
    )


def odd():
    return lax.rem(lax.axis_index("gx"), 2)


def ask(flag):
    return jnp.where(flag, 0.0, 1.0).astype(F32)


def top_fields(active_ref, die_ref):
    last = lax.broadcasted_iota(jnp.int32, (OY, DZ), 1) == DZ - 1
    same = lax.broadcasted_iota(jnp.int32, (OY, OY), 0) == lax.broadcasted_iota(jnp.int32, (OY, OY), 1)

    def on_rows(row):
        turned = jnp.sum(jnp.where(same, jnp.broadcast_to(row, (OY, OY)), 0.0), axis=1, keepdims=True)
        return jnp.where(last, turned, 0.0)

    contact, die = [], []
    for x in range(OX):
        stiff = CONTACT_STIFF * active_ref[x : x + 1].astype(F32)
        contact.append(on_rows(stiff))
        die.append(on_rows(stiff * die_ref[x : x + 1]))
    return contact, die


def own_part(flags_ref, flow_ref, part_ref, lower_ref, upper_ref):
    last_lane = lanes() == DZ - 1
    zero = jnp.zeros((8, DZ), F32)

    def clear(x, _):
        for m in range(6):
            lower_ref[m, x, 16:24] = zero
            upper_ref[m, x, 0:8] = zero
        return 0

    lax.fori_loop(0, OX + 1, clear, 0)
    for row in (0, 8):

        def element(x, behind):
            flags = [flags_ref[q, x, row : row + 8].astype(F32) * (0.5 * PLASTIC_GAIN * YIELD_OFFSET) for q in range(8)]
            n = [flow_ref[m, x, row : row + 8] for m in range(6)]
            node, ahead = scatter_x(plastic_forces(n, from_points(flags)), behind)
            store_y(node, lower_ref, upper_ref, x, row)
            return ahead

        behind = lax.fori_loop(0, OX, element, [zero] * 12)
        store_y(behind, lower_ref, upper_ref, OX, row)
    for x in range(OX + 1):
        for c in range(3):
            for row in (0, 8, 16):
                part_ref[c, x, row : row + 8] = merge_yz(lower_ref, upper_ref, c, x, row, last_lane) * (-1.0 / 16.0)


def add_load(part_ref, load_ref, die):
    for x in range(OX):
        for c in range(3):
            value = part_ref[c, x, 0:OY] + load_ref[c, x]
            part_ref[c, x, 0:OY] = value + die[x] if c == 2 else value


def part_kernel(load_ref, flags_ref, flow_ref, active_ref, die_ref, part_ref, contact_ref, lower_ref, upper_ref):
    contact, die = top_fields(active_ref, die_ref)
    for x in range(OX):
        contact_ref[x] = contact[x]
    own_part(flags_ref, flow_ref, part_ref, lower_ref, upper_ref)
    add_load(part_ref, load_ref, die)


def slab_kernel(load_hbm, flags_hbm, flow_hbm, active_hbm, die_hbm, right_hbm, left_hbm, first_hbm, second_hbm,
                right_ref, left_ref, rows_ref, part_ref, contact_ref, lower_ref, upper_ref,
                load_ref, flags_ref, flow_ref, active_ref, die_ref, load_sem, flags_sem, flow_sem, top_sem, out_sem):
    small = [
        pltpu.make_async_copy(active_hbm, active_ref, top_sem.at[0]),
        pltpu.make_async_copy(die_hbm, die_ref, top_sem.at[1]),
    ]
    large = [
        [pltpu.make_async_copy(source.at[m], target.at[m], sem.at[m]) for m in range(source.shape[0])]
        for source, target, sem in (
            (flags_hbm, flags_ref, flags_sem), (flow_hbm, flow_ref, flow_sem), (load_hbm, load_ref, load_sem))
    ]
    for group in (small, *large):
        for copy in group:
            copy.start()
    for copy in small:
        copy.wait()
    contact, die = top_fields(active_ref, die_ref)
    for x in range(OX):
        contact_ref[x] = contact[x]
    for group in large[:2]:
        for copy in group:
            copy.wait()

    def field(f, x, rows):
        if f < 8:
            return flags_ref[f, x, rows].astype(F32) * (-PLASTIC_GAIN / 8.0)
        if f < CONTACT_AT:
            return flow_ref[FLOW_SENT[f - 8], x, rows]
        return contact_ref[x, rows]

    whole = slice(0, OY)
    for f in range(NEL):
        for i in range(3):
            right_ref[3 * f + i] = field(f, 6 + i, whole)
        for i in range(2):
            left_ref[2 * f + i] = field(f, i, whole)
    outs = [
        pltpu.make_async_copy(right_ref.at[0:42], right_hbm.at[0:42], out_sem.at[0]),
        pltpu.make_async_copy(left_ref.at[0:28], left_hbm.at[0:28], out_sem.at[1]),
    ]
    for copy in outs:
        copy.start()

    def slabs(x, _):
        for f in range(NEL):
            rows_ref[0, x, 3 * f : 3 * f + 3] = field(f, x, slice(13, 16))
            rows_ref[1, x, 2 * f : 2 * f + 2] = field(f, x, slice(0, 2))
        return 0

    lax.fori_loop(0, OX, slabs, 0)
    own_part(flags_ref, flow_ref, part_ref, lower_ref, upper_ref)
    for copy in large[2]:
        copy.wait()
    add_load(part_ref, load_ref, die)

    def part_slabs(x, _):
        for c in range(3):
            rows_ref[0, x, 42 + 4 * c : 46 + 4 * c] = part_ref[c, x, 13:17]
            rows_ref[1, x, 28 + 3 * c : 31 + 3 * c] = part_ref[c, x, 0:3]
        return 0

    lax.fori_loop(0, OX + 1, part_slabs, 0)
    outs += [
        pltpu.make_async_copy(rows_ref.at[odd()], first_hbm, out_sem.at[2]),
        pltpu.make_async_copy(rows_ref.at[1 - odd()], second_hbm, out_sem.at[3]),
    ]
    for copy in outs[2:]:
        copy.start()
    for c in range(3):
        for i in range(4):
            right_ref[42 + 4 * c + i] = part_ref[c, 6 + i, 0:16]
            right_ref[54, 4 * c + i : 4 * c + i + 1] = part_ref[c, 6 + i, 16:17]
        for i in range(3):
            left_ref[28 + 3 * c + i] = part_ref[c, i, 0:16]
            left_ref[37, 3 * c + i : 3 * c + i + 1] = part_ref[c, i, 16:17]
    outs += [
        pltpu.make_async_copy(right_ref.at[42:55], right_hbm.at[42:55], out_sem.at[4]),
        pltpu.make_async_copy(left_ref.at[28:38], left_hbm.at[28:38], out_sem.at[5]),
    ]
    for copy in outs[4:]:
        copy.start()
    for copy in outs:
        copy.wait()


def three_steps(els_ref, basis, z_ref, lower_ref, upper_ref):
    at_first_x, at_last_x, at_first_y, at_last_y = place()
    lane = lanes()
    first_lane, last_lane = lane == 0, lane == DZ - 1
    rows = lax.broadcasted_iota(jnp.int32, (8, DZ), 0)
    keep_upper = jnp.logical_or(rows >= HALO, jnp.logical_not(at_first_y))
    keep_node = jnp.logical_or(rows < HALO, jnp.logical_not(at_last_y))
    zero = jnp.zeros((8, DZ), F32)

    def clear(x, _):
        for m in range(6):
            z_ref[m, x, 24:32] = zero
            upper_ref[m, x, 0:8] = zero
        return 0

    lax.fori_loop(0, WX, clear, 0)

    def first(x, _):
        for row in (0, 8, 16):
            for c in range(3):
                z_ref[2 * c, x, row : row + 8], z_ref[2 * c + 1, x, row : row + 8] = z_pair(
                    basis[0][c, x, row : row + 8], first_lane
                )
        return 0

    lax.fori_loop(0, WX, first, 0, unroll=5)

    for step in range(1, HALO + 1):
        start, end = step - 1, WX - 1 - step
        scale = (2.0 if step == 1 else 4.0) / SPAN
        for row in (0, 8, 16):

            def plane(x):
                values = []
                for m in range(6):
                    low, high = z_ref[m, x, row : row + 8], z_ref[m, x, row + 1 : row + 9]
                    values += [high + low, high - low]
                return values

            def element(x, carry):
                before, behind = carry
                after = plane(x + 1)
                p, q = before, after
                modes = (
                    [q[4 * c] - p[4 * c] for c in range(3)],
                    [q[4 * c + 1] + p[4 * c + 1] for c in range(3)],
                    [q[4 * c + 2] + p[4 * c + 2] for c in range(3)],
                    [q[4 * c + 1] - p[4 * c + 1] for c in range(3)],
                    [q[4 * c + 2] - p[4 * c + 2] for c in range(3)],
                    [q[4 * c + 3] + p[4 * c + 3] for c in range(3)],
                    [q[4 * c + 3] - p[4 * c + 3] for c in range(3)],
                )
                here = [els_ref[f, x, row : row + 8] for f in range(NEL + 1) if f != CONTACT_AT]
                n = (here[8], here[9], here[13], here[10], here[11], here[12])
                node, ahead = scatter_x(element_core(modes, n, here[:8]), behind)
                store_y(node, lower_ref, upper_ref, x, row, keep_upper if row == 0 else None)
                return after, ahead

            carry = (plane(start), [zero] * 12)
            for x in range(start, HALO):
                carry = element(x, carry)
            carry = (carry[0], [jnp.where(at_first_x, 0.0, value) for value in carry[1]])
            first_pair = HALO + (end + 1 - HALO) % 2
            if first_pair > HALO:
                carry = element(HALO, carry)

            def pair(k, carry):
                x = first_pair + 2 * k
                return element(x + 1, element(x, carry))

            lax.fori_loop(0, (end + 1 - first_pair) // 2, pair, carry)

        for x in range(step, end + 1):
            for row in (0, 8, 16):
                for c in range(3):
                    here = basis[step - 1][c, x, row : row + 8]
                    value = merge_yz(lower_ref, upper_ref, c, x, row, last_lane) * (scale / 16.0)
                    if c == 2:
                        value = value + (els_ref[CONTACT_AT, x, row : row + 8] * scale) * here
                    if step == 1:
                        value = value - here
                    else:
                        value = value - (here + here) - basis[step - 2][c, x, row : row + 8]
                    if x >= HALO + OX:
                        value = jnp.where(at_last_x, 0.0, value)
                    if row == 16:
                        value = jnp.where(keep_node, value, 0.0)
                    basis[step][c, x, row : row + 8] = value
                    if step < HALO:
                        z_ref[2 * c, x, row : row + 8], z_ref[2 * c + 1, x, row : row + 8] = z_pair(value, first_lane)


def sum_rows(values):
    return jnp.sum(values, axis=0, keepdims=True)


def first_kernel(flags_ref, flow_ref, contact_ref, part_ref, left_ref, right_ref, rows_ref, cl_ref, cr_ref,
                 els_ref, own_ref, dots_ref, right_out, left_out, first_out, second_out,
                 b0, b1, b2, b3, z_ref, lower_ref, upper_ref):
    at_first_x, at_last_x, at_first_y, at_last_y = place()
    has_l, has_r, has_d, has_u = ask(at_first_x), ask(at_last_x), ask(at_first_y), ask(at_last_y)
    below = odd()
    above = 1 - below
    zero = jnp.zeros((8, DZ), F32)
    low, high = slice(0, 3), slice(19, 21)
    mid = slice(HALO, HALO + OY)

    def clear(x, _):
        for f in range(NEL):
            els_ref[f, x, 16:24] = zero
        return 0

    lax.fori_loop(0, WE, clear, 0)

    def clear_start(x, _):
        for c in range(3):
            for row in (0, 8, 16):
                b0[c, x, row : row + 8] = zero
        return 0

    lax.fori_loop(0, WX, clear_start, 0)

    def own(x, _):
        w = x + HALO
        for f in range(NEL):
            if f < 8:
                value = flags_ref[f, x].astype(F32) * (-PLASTIC_GAIN / 8.0)
            elif f < CONTACT_AT:
                value = flow_ref[FLOW_SENT[f - 8], x]
            else:
                value = contact_ref[x]
            els_ref[f, w, mid] = value
            els_ref[f, w, low] = rows_ref[x, below, 3 * f : 3 * f + 3]
            els_ref[f, w, high] = rows_ref[x, above, 2 * f : 2 * f + 2]
        for c in range(3):
            b0[c, w, mid] = part_ref[c, x, 0:16]
            b0[c, w, 19:20] = part_ref[c, x, 16:17] * has_u
        return 0

    lax.fori_loop(0, OX, own, 0)
    for c in range(3):
        b0[c, 12, mid] = part_ref[c, OX, 0:16] * has_r
        b0[c, 12, 19:20] = part_ref[c, OX, 16:17] * (has_r * has_u)
    for i in range(3):
        for f in range(NEL):
            els_ref[f, i, mid] = left_ref[3 * f + i]
            els_ref[f, i, low] = cl_ref[i, above, 3 * f : 3 * f + 3]
            els_ref[f, i, high] = cl_ref[i, below, 2 * f : 2 * f + 2]
    for i in range(2):
        for f in range(NEL):
            els_ref[f, 12 + i, mid] = right_ref[2 * f + i]
            els_ref[f, 12 + i, low] = cr_ref[i, above, 3 * f : 3 * f + 3]
            els_ref[f, 12 + i, high] = cr_ref[i, below, 2 * f : 2 * f + 2]

    def zz(x, _):
        for row in (0, 8, 16):
            els_ref[ZZ_AT, x, row : row + 8] = -(els_ref[8, x, row : row + 8] + els_ref[9, x, row : row + 8])
        return 0

    lax.fori_loop(0, WE, zz, 0)

    for c in range(3):
        for i in range(4):
            b0[c, i, mid] += left_ref[42 + 4 * c + i] * has_l
            b0[c, i, 19:20] += left_ref[54, 4 * c + i : 4 * c + i + 1] * (has_l * has_u)
            b0[c, i, 0:4] += cl_ref[i, above, 42 + 4 * c : 46 + 4 * c] * (has_l * has_d)
            b0[c, i, 19:22] += cl_ref[i, below, 28 + 3 * c : 31 + 3 * c] * (has_l * has_u)
        for i in range(3):
            b0[c, 12 + i, mid] += right_ref[28 + 3 * c + i] * has_r
            b0[c, 12 + i, 19:20] += right_ref[37, 3 * c + i : 3 * c + i + 1] * (has_r * has_u)
            b0[c, 12 + i, 0:4] += cr_ref[i, above, 42 + 4 * c : 46 + 4 * c] * (has_r * has_d)
            b0[c, 12 + i, 19:22] += cr_ref[i, below, 28 + 3 * c : 31 + 3 * c] * (has_r * has_u)

    def edges(x, _):
        inside = jnp.where(x == OX, has_r, 1.0)
        for c in range(3):
            b0[c, x + HALO, 0:4] += rows_ref[x, below, 42 + 4 * c : 46 + 4 * c] * (inside * has_d)
            b0[c, x + HALO, 19:22] += rows_ref[x, above, 28 + 3 * c : 31 + 3 * c] * (inside * has_u)
        return 0

    lax.fori_loop(0, OX + 1, edges, 0)

    basis = (b0, b1, b2, b3)
    three_steps(els_ref, basis, z_ref, lower_ref, upper_ref)

    def collect(x, sums):
        sums = list(sums)
        for row in (0, 8):
            for c in range(3):
                v = [b[c, x + HALO, row + HALO : row + HALO + 8] for b in basis]
                for k in range(4):
                    own_ref[k, c, x, row : row + 8] = v[k]
                for k in range(7):
                    sums[k] = sums[k] + v[k // 2] * v[k - k // 2]
        return tuple(sums)

    sums = lax.fori_loop(0, OX, collect, (zero,) * 7)
    dots_ref[...] = zero
    for k in range(7):
        dots_ref[k : k + 1] = sum_rows(sums[k])

    def edge_rows(c, x):
        last, start = b3[c, x, 16:19], b3[c, x, 3:6]
        return jnp.where(below == 0, last, start), jnp.where(below == 0, start, last)

    for i in range(3):
        for c in range(3):
            for out, x in ((right_out, 9 + i), (left_out, 3 + i)):
                out[3 * c + i] = b3[c, x, mid]
                first, second = edge_rows(c, x)
                out[9 + i, 3 * c : 3 * c + 3] = second
                out[12 + i, 3 * c : 3 * c + 3] = first

    def slabs(x, _):
        for c in range(3):
            first, second = edge_rows(c, x + HALO)
            first_out[x, 3 * c : 3 * c + 3] = first
            second_out[x, 3 * c : 3 * c + 3] = second
        return 0

    lax.fori_loop(0, OX, slabs, 0)


def second_kernel(els_ref, own_ref, dots_ref, left_ref, right_ref, first_ref, second_ref,
                  tail_ref, row_ref, b0, b1, b2, b3, z_ref, lower_ref, upper_ref):
    _, at_last_x, _, at_last_y = place()
    has_r, has_u = ask(at_last_x), ask(at_last_y)
    below = odd()
    zero = jnp.zeros((8, DZ), F32)
    mid = slice(HALO, HALO + OY)

    def own(x, _):
        for c in range(3):
            b0[c, x + HALO, mid] = own_ref[3, c, x]
        return 0

    def edges(x, _):
        inside = jnp.where(x >= HALO + OX, has_r, 1.0)
        for c in range(3):
            b0[c, x, 16:24] = zero
            one, two = first_ref[x, 3 * c : 3 * c + 3] * inside, second_ref[x, 3 * c : 3 * c + 3] * inside
            b0[c, x, 0:3] = jnp.where(below == 0, one, two)
            b0[c, x, 19:22] = jnp.where(below == 0, two, one) * has_u
        return 0

    lax.fori_loop(0, WX, edges, 0)
    lax.fori_loop(0, OX, own, 0)
    for c in range(3):
        for i in range(3):
            b0[c, i, mid] = left_ref[3 * c + i]
            b0[c, 12 + i, mid] = right_ref[3 * c + i] * has_r

    basis = (b0, b1, b2, b3)
    three_steps(els_ref, basis, z_ref, lower_ref, upper_ref)

    def collect(x, sums):
        sums = list(sums)
        for row in (0, 8):
            for c in range(3):
                v = [own_ref[3, c, x, row : row + 8]]
                for k in range(1, 4):
                    w = b_at(basis[k], c, x, row)
                    v.append((w + w) - own_ref[3 - k, c, x, row : row + 8])
                    tail_ref[k - 1, c, x, row : row + 8] = v[k]
                for k in range(1, 6):
                    sums[k - 1] = sums[k - 1] + v[k // 2] * v[k - k // 2]
        return tuple(sums)

    sums = lax.fori_loop(0, OX, collect, (zero,) * 5)
    lane = lax.broadcasted_iota(jnp.int32, (1, DZ), 1)
    line = jnp.zeros((1, DZ), F32)
    for k in range(12):
        dot = dots_ref[k : k + 1] if k < 7 else sum_rows(sums[k - 7])
        line = jnp.where(lane == k, jnp.sum(dot, axis=1, keepdims=True), line)
    row_ref[...] = jnp.broadcast_to(line, row_ref.shape)


def b_at(ref, c, x, row):
    return ref[c, x + HALO, row + HALO : row + HALO + 8]


def times_matrix(p):
    out = [None] * (len(p) + 1)

    def add(k, value):
        out[k] = value if out[k] is None else out[k] + value

    for k, value in enumerate(p):
        add(k, value * (SPAN / 2))
        if k == 0:
            add(1, value * (SPAN / 2))
        else:
            add(k + 1, value * (SPAN / 4))
            add(k - 1, value * (SPAN / 4))
    return out


def tree_sum(values):
    while len(values) > 1:
        values = [a + b for a, b in zip(values[::2], values[1::2])] + ([values[-1]] if len(values) % 2 else [])
    return values[0]


def combine(p, a, q):
    out = []
    for k in range(max(len(p), len(q))):
        term = a * q[k] if k < len(q) else None
        if k < len(p):
            term = p[k] if term is None else p[k] + term
        out.append(term)
    return out


def coefficients(mu):
    gram = [[0.5 * (mu[i + j] + mu[abs(i - j)]) if i + j < len(mu) else None for j in range(7)] for i in range(7)]

    def inner(p, q):
        return tree_sum([p[i] * tree_sum([gram[i][j] * q[j] for j in range(len(q))]) for i in range(len(p))])

    remain = [jnp.ones_like(mu[0])]
    total = []
    for newton in range(NEWTON):
        direction = remain
        norm = inner(remain, remain)
        for step in range(CG_STEPS):
            image = times_matrix(direction)
            alpha = norm / inner(direction, image)
            total = combine(total, alpha, direction)
            remain = combine(remain, -alpha, image)
            if step + 1 < CG_STEPS:
                norm_next = inner(remain, remain)
                direction = combine(remain, norm_next / norm, direction)
                norm = norm_next
    return total, remain


def last_kernel(dots_ref, own_ref, tail_ref, displacement_ref, residual_ref):
    sums = jnp.sum(dots_ref[...], axis=0, keepdims=True)
    dots = [jnp.broadcast_to(sums[:, k : k + 1], (1, DZ)) for k in range(12)]
    mu = dots[:2]
    for k in range(2, 12):
        mu.append((dots[k] + dots[k]) - mu[k % 2])
    total, remain = coefficients(mu)
    total = [jnp.broadcast_to(value, (8, DZ)) for value in total]
    remain = [jnp.broadcast_to(value, (8, DZ)) for value in remain]

    def write(x, _):
        for row in (0, 8):
            for c in range(3):
                v = [own_ref[k, c, x, row : row + 8] for k in range(4)]
                v += [tail_ref[k, c, x, row : row + 8] for k in range(3)]
                displacement_ref[c, x, row : row + 8] = tree_sum([a * b for a, b in zip(total, v)])
                residual_ref[c, x, row : row + 8] = tree_sum([a * b for a, b in zip(remain, v)])
        return 0

    lax.fori_loop(0, OX, write, 0)


def shape(*dims):
    return jax.ShapeDtypeStruct(dims, F32)


def call(kernel, outs, scratch=(), mebibytes=24, **more):
    return pl.pallas_call(
        kernel,
        out_shape=outs,
        scratch_shapes=[pltpu.VMEM(dims, F32) if isinstance(dims, tuple) else dims for dims in scratch],
        compiler_params=pltpu.CompilerParams(vmem_limit_bytes=mebibytes * 1024 * 1024),
        **more,
    )


STEP_SCRATCH = [(3, WX, WY, DZ)] * 4 + [(6, WX, WY + 8, DZ)] * 3


def rotate(value, axis, steps):
    count = lax.axis_size(axis)
    return lax.ppermute(value, axis, [(i, (i + steps) % count) for i in range(count)])


def wind(value, forward):
    count_x, count_y = lax.axis_size("gx"), lax.axis_size("gy")
    pairs = []
    for x in range(count_x):
        for y in range(count_y):
            ahead = y + 1 if (x % 2 == 0) == forward else y - 1
            goal = (x, ahead) if 0 <= ahead < count_y else (x ^ 1, y)
            pairs.append((x * count_y + y, goal[0] * count_y + goal[1]))
    return lax.ppermute(value, ("gx", "gy"), pairs)


def exchange(right, left, first, second):
    from_left = rotate(right, "gx", 1)
    from_right = rotate(left, "gx", -1)
    rows = jnp.stack([wind(first, True), wind(second, False)], axis=1)
    corner_left = rotate(rows[6:10], "gx", 1)
    corner_right = rotate(rows[0:3], "gx", -1)
    return from_left, from_right, rows, corner_left, corner_right


def exchange_in_turn(right, left, first, second):
    from_left = rotate(right, "gx", 1)
    from_right = rotate(left, "gx", -1)
    first = jnp.concatenate([from_left[9:12], first, from_right[9:12]], axis=0)
    second = jnp.concatenate([from_left[12:15], second, from_right[12:15]], axis=0)
    return from_left, from_right, wind(first, True), wind(second, False)


def body(load, plastic_flags, flow_dir, contact_flags, die_depth):
    slabs = [(55, OY, DZ), (38, OY, DZ), (OX + 1, 56, DZ), (OX + 1, 56, DZ)]
    work = [(6, OX + 1, WY + 8, DZ)] * 2
    outside = pl.BlockSpec(memory_space=pl.ANY)
    inputs = (load, plastic_flags, flow_dir, contact_flags, die_depth)
    right, left, first, second = call(
        slab_kernel,
        [shape(*dims) for dims in slabs],
        slabs[:2] + [(2, OX + 1, 56, DZ), (3, OX + 1, WY, DZ), (OX, OY, DZ)] + work
        + [(3, OX, OY, DZ), pltpu.VMEM((8, OX, OY, DZ), jnp.int32), (6, OX, OY, DZ),
           pltpu.VMEM((OX, OY), jnp.int32), (OX, OY)]
        + [pltpu.SemaphoreType.DMA((count,)) for count in (3, 8, 6, 2, 6)],
        mebibytes=54,
        in_specs=[outside] * 5,
        out_specs=[outside] * 4,
    )(*inputs)
    part, contact = call(
        part_kernel, [shape(3, OX + 1, WY, DZ), shape(OX, OY, DZ)], work,
        cost_estimate=pl.CostEstimate(flops=4000000, bytes_accessed=2000000, transcendentals=0),
    )(*inputs)
    halos = exchange(right, left, first, second)
    els, own, dots, right, left, first, second = call(
        first_kernel,
        [shape(NEL + 1, WE, WY, DZ), shape(4, 3, OX, OY, DZ), shape(8, DZ), shape(15, OY, DZ), shape(15, OY, DZ),
         shape(OX, 16, DZ), shape(OX, 16, DZ)],
        STEP_SCRATCH,
    )(plastic_flags, flow_dir, contact, part, *halos)
    halos = exchange_in_turn(right, left, first, second)
    count = lax.axis_size("gx") * lax.axis_size("gy")
    tail, line = call(
        second_kernel, [shape(3, 3, OX, OY, DZ), shape(count, DZ)], STEP_SCRATCH
    )(els, own, dots, *halos)
    lines = lax.all_to_all(line, ("gx", "gy"), 0, 0, tiled=True)
    return tuple(call(last_kernel, [shape(3, OX, OY, DZ)] * 2)(lines, own, tail))


def solution(mesh):
    in_specs = (
        P(None, "gx", "gy", None),
        P(None, "gx", "gy", None),
        P(None, "gx", "gy", None),
        P("gx", "gy"),
        P("gx", "gy"),
    )
    out_specs = (P(None, "gx", "gy", None), P(None, "gx", "gy", None))
    return jax.shard_map(body, mesh=mesh, in_specs=in_specs, out_specs=out_specs, check_vma=False)
```

```python
import math

import jax
import jax.numpy as jnp
from jax import lax
from jax.experimental import pallas as pl
from jax.experimental.pallas import tpu as pltpu
from jax.sharding import PartitionSpec as P

PLASTIC_GAIN = 6.0 / 3.1
YIELD_OFFSET = 0.05
CONTACT_STIFF = 4.0
CG_STEPS = 3
NEWTON = 2
ROOT_THIRD = 1.0 / math.sqrt(3.0)
THIRD = 1.0 / 3.0
SPAN = 10.0

HALO = 3
OX, OY, DZ = 9, 16, 128
WX = OX + 2 * HALO
WE = WX - 1
WY = 24
F32 = jnp.float32

FLOW_SENT = (0, 1, 3, 4, 5)
NEL = 14
CONTACT_AT = 13
ZZ_AT = 14


ROW_AT = (0, 54, 108, 168, 222, 276, 336, 390, 444, 498)
SLAB_ROWS = 512
LOW_PART, HIGH_PART = slice(0, 168), slice(336, 512)


def up_rows(x, c):
    at = ROW_AT[x] + (42 if x < OX else 0) + 4 * c
    return slice(at, at + 4)


def down_rows(x, c):
    at = ROW_AT[x] + (28 if x < OX else 0) + 3 * c
    return slice(at, at + 3)


def moved(rows, by):
    return slice(rows.start - by, rows.stop - by)


def lanes():
    return lax.broadcasted_iota(jnp.int32, (8, DZ), 1)


def z_pair(value, first_lane):
    low = jnp.where(first_lane, 0.0, pltpu.roll(value, 1, 1))
    return value + low, value - low


def z_merge(total, slope, last_lane):
    return total + slope + jnp.where(last_lane, 0.0, pltpu.roll(total - slope, DZ - 1, 1))


def to_points(s1, sx, sy, sz, syz, sxz, sxy):
    points = []
    for sign_x in (-1, 1):
        a0 = s1 + sx if sign_x > 0 else s1 - sx
        ay = sy + sxy if sign_x > 0 else sy - sxy
        az = sz + sxz if sign_x > 0 else sz - sxz
        for sign_y in (-1, 1):
            b0 = a0 + ay if sign_y > 0 else a0 - ay
            bz = az + syz if sign_y > 0 else az - syz
            points += [b0 - bz, b0 + bz]
    return points


def from_points(t):
    per_x = []
    for i in range(2):
        e0 = [t[4 * i + 2 * j + 1] + t[4 * i + 2 * j] for j in range(2)]
        ez = [t[4 * i + 2 * j + 1] - t[4 * i + 2 * j] for j in range(2)]
        per_x.append((e0[1] + e0[0], e0[1] - e0[0], ez[1] + ez[0], ez[1] - ez[0]))
    low, high = per_x
    t1, ty, tz, tyz = (high[m] + low[m] for m in range(4))
    tx, txy, txz = (high[m] - low[m] for m in range(3))
    return t1, tx, ty, tz, tyz, txz, txy


def plastic_forces(n, t):
    nxx, nyy, nzz, nxy, nyz, nzx = n
    t1, tx, ty, tz, tyz, txz, txy = t
    tx, ty, tz = tx * ROOT_THIRD, ty * ROOT_THIRD, tz * ROOT_THIRD
    tyz, txz, txy = tyz * THIRD, txz * THIRD, txy * THIRD
    a_xy, a_yz, a_zx = nxy * t1, nyz * t1, nzx * t1
    fx = [nxx * t1, a_xy, a_zx]
    fy = [a_xy, nyy * t1, a_yz]
    fz = [a_zx, a_yz, nzz * t1]
    xy_z, yz_x, zx_y = nxy * tz, nyz * tx, nzx * ty
    fxy = [nxx * ty + nxy * tx, nxy * ty + nyy * tx, zx_y + yz_x]
    fxz = [nxx * tz + nzx * tx, xy_z + yz_x, nzx * tz + nzz * tx]
    fyz = [xy_z + zx_y, nyy * tz + nyz * ty, nyz * tz + nzz * ty]
    fxyz = [
        nxx * tyz + nxy * txz + nzx * txy,
        nxy * tyz + nyy * txz + nyz * txy,
        nzx * tyz + nyz * txz + nzz * txy,
    ]
    return fx, fy, fz, fxy, fxz, fyz, fxyz


def element_core(modes, n, flags):
    ax, ay, az, axy, axz, ayz, axyz = modes
    nxx, nyy, nzz, nxy, nyz, nzx = n
    sh_xy, sh_yz, sh_zx = ax[1] + ay[0], ay[2] + az[1], az[0] + ax[2]
    k_x, k_y, k_z = axy[2] + axz[1], axy[2] + ayz[0], axz[1] + ayz[0]
    s1 = (nxx * ax[0] + nyy * ay[1] + nzz * az[2]) + (nxy * sh_xy + nyz * sh_yz + nzx * sh_zx)
    sx = (nxy * axy[0] + nyy * axy[1]) + (nyz * k_x + nzx * axz[0] + nzz * axz[2])
    sy = (nxx * axy[0] + nxy * axy[1]) + (nzx * k_y + nyz * ayz[1] + nzz * ayz[2])
    sz = (nxx * axz[0] + nxy * k_z) + (nzx * axz[2] + nyy * ayz[1] + nyz * ayz[2])
    syz = nxx * axyz[0] + nxy * axyz[1] + nzx * axyz[2]
    sxz = nxy * axyz[0] + nyy * axyz[1] + nyz * axyz[2]
    sxy = nzx * axyz[0] + nyz * axyz[1] + nzz * axyz[2]
    values = to_points(
        s1, sx * ROOT_THIRD, sy * ROOT_THIRD, sz * ROOT_THIRD, syz * THIRD, sxz * THIRD, sxy * THIRD
    )
    plastic = plastic_forces(n, from_points([value * flag for value, flag in zip(values, flags)]))
    trace = ax[0] + ay[1] + az[2]
    tr_x, tr_y, tr_z = (
        (axy[1] + axz[2]) * THIRD,
        (axy[0] + ayz[2]) * THIRD,
        (axz[0] + ayz[1]) * THIRD,
    )
    mixed = (k_x + ayz[0]) * THIRD
    elastic = (
        [trace + (ax[0] + ax[0]), sh_xy, sh_zx],
        [sh_xy, trace + (ay[1] + ay[1]), sh_yz],
        [sh_zx, sh_yz, trace + (az[2] + az[2])],
        [tr_y + axy[0], tr_x + axy[1], mixed + axy[2] * THIRD],
        [tr_z + axz[0], mixed + axz[1] * THIRD, tr_x + axz[2]],
        [mixed + ayz[0] * THIRD, tr_z + ayz[1], tr_y + ayz[2]],
        [axyz[c] * (5.0 / 9.0) for c in range(3)],
    )
    return [[elastic[m][c] + plastic[m][c] for c in range(3)] for m in range(7)]


def scatter_x(forces, behind):
    fx, fy, fz, fxy, fxz, fyz, fxyz = forces
    node, ahead = [], []
    for c in range(3):
        node += [
            behind[4 * c] - fx[c],
            behind[4 * c + 1] + (fy[c] - fxy[c]),
            behind[4 * c + 2] + (fz[c] - fxz[c]),
            behind[4 * c + 3] + (fyz[c] - fxyz[c]),
        ]
        ahead += [fx[c], fy[c] + fxy[c], fz[c] + fxz[c], fyz[c] + fxyz[c]]
    return node, ahead


def store_y(node, lower_ref, upper_ref, x, row, upper_keep=None):
    for c in range(3):
        ss, sd, ds, dd = node[4 * c : 4 * c + 4]
        lower_ref[2 * c, x, row : row + 8] = ss - sd
        lower_ref[2 * c + 1, x, row : row + 8] = ds - dd
        up_s, up_d = ss + sd, ds + dd
        if upper_keep is not None:
            up_s, up_d = jnp.where(upper_keep, up_s, 0.0), jnp.where(upper_keep, up_d, 0.0)
        upper_ref[2 * c, x, row + 8 : row + 16] = up_s
        upper_ref[2 * c + 1, x, row + 8 : row + 16] = up_d


def merge_yz(lower_ref, upper_ref, c, x, row, last_lane):
    total = lower_ref[2 * c, x, row : row + 8] + upper_ref[2 * c, x, row + 7 : row + 15]
    slope = lower_ref[2 * c + 1, x, row : row + 8] + upper_ref[2 * c + 1, x, row + 7 : row + 15]
    return z_merge(total, slope, last_lane)


def place():
    index_x, index_y = lax.axis_index("gx"), lax.axis_index("gy")
    return (
        index_x == 0,
        index_x == lax.axis_size("gx") - 1,
        index_y == 0,
        index_y == lax.axis_size("gy") - 1,
    )


def odd():
    return lax.rem(lax.axis_index("gx"), 2)


def ask(flag):
    return jnp.where(flag, 0.0, 1.0).astype(F32)


def top_fields(active_ref, die_ref):
    last = lax.broadcasted_iota(jnp.int32, (OY, DZ), 1) == DZ - 1
    same = lax.broadcasted_iota(jnp.int32, (OY, OY), 0) == lax.broadcasted_iota(jnp.int32, (OY, OY), 1)

    def on_rows(row):
        turned = jnp.sum(jnp.where(same, jnp.broadcast_to(row, (OY, OY)), 0.0), axis=1, keepdims=True)
        return jnp.where(last, turned, 0.0)

    contact, die = [], []
    for x in range(OX):
        stiff = CONTACT_STIFF * active_ref[x : x + 1].astype(F32)
        contact.append(on_rows(stiff))
        die.append(on_rows(stiff * die_ref[x : x + 1]))
    return contact, die


def own_part(flags_ref, flow_ref, part_ref, lower_ref, upper_ref):
    last_lane = lanes() == DZ - 1
    zero = jnp.zeros((8, DZ), F32)

    def clear(x, _):
        for m in range(6):
            lower_ref[m, x, 16:24] = zero
            upper_ref[m, x, 0:8] = zero
        return 0

    lax.fori_loop(0, OX + 1, clear, 0)
    for row in (0, 8):

        def element(x, behind):
            flags = [flags_ref[q, x, row : row + 8].astype(F32) * (0.5 * PLASTIC_GAIN * YIELD_OFFSET) for q in range(8)]
            n = [flow_ref[m, x, row : row + 8] for m in range(6)]
            node, ahead = scatter_x(plastic_forces(n, from_points(flags)), behind)
            store_y(node, lower_ref, upper_ref, x, row)
            return ahead

        behind = lax.fori_loop(0, OX, element, [zero] * 12)
        store_y(behind, lower_ref, upper_ref, OX, row)
    for x in range(OX + 1):
        for c in range(3):
            for row in (0, 8, 16):
                part_ref[c, x, row : row + 8] = merge_yz(lower_ref, upper_ref, c, x, row, last_lane) * (-1.0 / 16.0)


def add_load(part_ref, load_ref, die):
    for x in range(OX):
        for c in range(3):
            value = part_ref[c, x, 0:OY] + load_ref[c, x]
            part_ref[c, x, 0:OY] = value + die[x] if c == 2 else value


def part_kernel(load_ref, flags_ref, flow_ref, active_ref, die_ref, part_ref, contact_ref, lower_ref, upper_ref):
    contact, die = top_fields(active_ref, die_ref)
    for x in range(OX):
        contact_ref[x] = contact[x]
    own_part(flags_ref, flow_ref, part_ref, lower_ref, upper_ref)
    add_load(part_ref, load_ref, die)


def slab_kernel(load_hbm, flags_hbm, flow_hbm, active_hbm, die_hbm, right_hbm, left_hbm, first_hbm, second_hbm,
                right_ref, left_ref, rows_ref, part_ref, contact_ref, lower_ref, upper_ref,
                load_ref, flags_ref, flow_ref, active_ref, die_ref, load_sem, flags_sem, flow_sem, top_sem, out_sem):
    small = [
        pltpu.make_async_copy(active_hbm, active_ref, top_sem.at[0]),
        pltpu.make_async_copy(die_hbm, die_ref, top_sem.at[1]),
    ]
    large = [
        [pltpu.make_async_copy(source.at[m : m + step], target.at[m : m + step], sem.at[m])
         for m in range(0, source.shape[0], step)]
        for source, target, sem, step in (
            (flags_hbm, flags_ref, flags_sem, 4), (flow_hbm, flow_ref, flow_sem, 3), (load_hbm, load_ref, load_sem, 3))
    ]
    for group in (small, *large):
        for copy in group:
            copy.start()
    for copy in small:
        copy.wait()
    contact, die = top_fields(active_ref, die_ref)
    for x in range(OX):
        contact_ref[x] = contact[x]
    for group in large[:2]:
        for copy in group:
            copy.wait()

    def field(f, x, rows):
        if f < 8:
            return flags_ref[f, x, rows].astype(F32) * (-PLASTIC_GAIN / 8.0)
        if f < CONTACT_AT:
            return flow_ref[FLOW_SENT[f - 8], x, rows]
        return contact_ref[x, rows]

    whole = slice(0, OY)
    for f in range(NEL):
        for i in range(3):
            right_ref[3 * f + i] = field(f, 6 + i, whole)
        for i in range(2):
            left_ref[2 * f + i] = field(f, i, whole)
    outs = [
        pltpu.make_async_copy(right_ref.at[0:42], right_hbm.at[0:42], out_sem.at[0]),
        pltpu.make_async_copy(left_ref.at[0:28], left_hbm.at[0:28], out_sem.at[1]),
    ]
    for copy in outs:
        copy.start()

    for x in range(OX):
        for f in range(NEL):
            rows_ref[0, ROW_AT[x] + 3 * f : ROW_AT[x] + 3 * f + 3] = field(f, x, slice(13, 16))
            rows_ref[1, ROW_AT[x] + 2 * f : ROW_AT[x] + 2 * f + 2] = field(f, x, slice(0, 2))
    own_part(flags_ref, flow_ref, part_ref, lower_ref, upper_ref)
    for copy in large[2]:
        copy.wait()
    add_load(part_ref, load_ref, die)

    for x in range(OX + 1):
        for c in range(3):
            rows_ref[0, up_rows(x, c)] = part_ref[c, x, 13:17]
            rows_ref[1, down_rows(x, c)] = part_ref[c, x, 0:3]
    outs += [
        pltpu.make_async_copy(rows_ref.at[odd()], first_hbm, out_sem.at[2]),
        pltpu.make_async_copy(rows_ref.at[1 - odd()], second_hbm, out_sem.at[3]),
    ]
    for copy in outs[2:]:
        copy.start()
    for c in range(3):
        for i in range(4):
            right_ref[42 + 4 * c + i] = part_ref[c, 6 + i, 0:16]
            right_ref[54, 4 * c + i : 4 * c + i + 1] = part_ref[c, 6 + i, 16:17]
        for i in range(3):
            left_ref[28 + 3 * c + i] = part_ref[c, i, 0:16]
            left_ref[37, 3 * c + i : 3 * c + i + 1] = part_ref[c, i, 16:17]
    outs += [
        pltpu.make_async_copy(right_ref.at[42:55], right_hbm.at[42:55], out_sem.at[4]),
        pltpu.make_async_copy(left_ref.at[28:38], left_hbm.at[28:38], out_sem.at[5]),
    ]
    for copy in outs[4:]:
        copy.start()
    for copy in outs:
        copy.wait()


def three_steps(els_ref, basis, z_ref, lower_ref, upper_ref):
    at_first_x, at_last_x, at_first_y, at_last_y = place()
    lane = lanes()
    first_lane, last_lane = lane == 0, lane == DZ - 1
    rows = lax.broadcasted_iota(jnp.int32, (8, DZ), 0)
    keep_upper = jnp.logical_or(rows >= HALO, jnp.logical_not(at_first_y))
    keep_node = jnp.logical_or(rows < HALO, jnp.logical_not(at_last_y))
    zero = jnp.zeros((8, DZ), F32)

    def clear(x, _):
        for m in range(6):
            z_ref[m, x, 24:32] = zero
            upper_ref[m, x, 0:8] = zero
        return 0

    lax.fori_loop(0, WX, clear, 0)

    def first(x, _):
        for row in (0, 8, 16):
            for c in range(3):
                z_ref[2 * c, x, row : row + 8], z_ref[2 * c + 1, x, row : row + 8] = z_pair(
                    basis[0][c, x, row : row + 8], first_lane
                )
        return 0

    lax.fori_loop(0, WX, first, 0, unroll=5)

    for step in range(1, HALO + 1):
        start, end = step - 1, WX - 1 - step
        scale = (2.0 if step == 1 else 4.0) / SPAN
        for row in (0, 8, 16):

            def plane(x):
                values = []
                for m in range(6):
                    low, high = z_ref[m, x, row : row + 8], z_ref[m, x, row + 1 : row + 9]
                    values += [high + low, high - low]
                return values

            def element(x, carry):
                before, behind = carry
                after = plane(x + 1)
                p, q = before, after
                modes = (
                    [q[4 * c] - p[4 * c] for c in range(3)],
                    [q[4 * c + 1] + p[4 * c + 1] for c in range(3)],
                    [q[4 * c + 2] + p[4 * c + 2] for c in range(3)],
                    [q[4 * c + 1] - p[4 * c + 1] for c in range(3)],
                    [q[4 * c + 2] - p[4 * c + 2] for c in range(3)],
                    [q[4 * c + 3] + p[4 * c + 3] for c in range(3)],
                    [q[4 * c + 3] - p[4 * c + 3] for c in range(3)],
                )
                here = [els_ref[f, x, row : row + 8] for f in range(NEL + 1) if f != CONTACT_AT]
                n = (here[8], here[9], here[13], here[10], here[11], here[12])
                node, ahead = scatter_x(element_core(modes, n, here[:8]), behind)
                store_y(node, lower_ref, upper_ref, x, row, keep_upper if row == 0 else None)
                return after, ahead

            carry = (plane(start), [zero] * 12)
            for x in range(start, HALO):
                carry = element(x, carry)
            carry = (carry[0], [jnp.where(at_first_x, 0.0, value) for value in carry[1]])
            first_pair = HALO + (end + 1 - HALO) % 2
            if first_pair > HALO:
                carry = element(HALO, carry)

            def pair(k, carry):
                x = first_pair + 2 * k
                return element(x + 1, element(x, carry))

            lax.fori_loop(0, (end + 1 - first_pair) // 2, pair, carry)

        for x in range(step, end + 1):
            for row in (0, 8, 16) if step < HALO else (HALO, HALO + 8):
                for c in range(3):
                    here = basis[step - 1][c, x, row : row + 8]
                    value = merge_yz(lower_ref, upper_ref, c, x, row, last_lane) * (scale / 16.0)
                    if c == 2:
                        value = value + (els_ref[CONTACT_AT, x, row : row + 8] * scale) * here
                    if step == 1:
                        value = value - here
                    else:
                        value = value - (here + here) - basis[step - 2][c, x, row : row + 8]
                    if x >= HALO + OX:
                        value = jnp.where(at_last_x, 0.0, value)
                    if row == 16:
                        value = jnp.where(keep_node, value, 0.0)
                    basis[step][c, x, row : row + 8] = value
                    if step < HALO:
                        z_ref[2 * c, x, row : row + 8], z_ref[2 * c + 1, x, row : row + 8] = z_pair(value, first_lane)


def sum_rows(values):
    return jnp.sum(values, axis=0, keepdims=True)


def first_kernel(flags_ref, flow_ref, contact_ref, part_ref, left_ref, right_ref, rows_ref, cl_ref, cr_ref,
                 els_ref, own_ref, dots_ref, right_out, left_out, first_out, second_out,
                 b0, b1, b2, b3, z_ref, lower_ref, upper_ref):
    at_first_x, at_last_x, at_first_y, at_last_y = place()
    has_l, has_r, has_u = ask(at_first_x), ask(at_last_x), ask(at_last_y)
    below = odd()
    above = 1 - below
    zero = jnp.zeros((8, DZ), F32)
    low, high = slice(0, 3), slice(19, 21)
    mid = slice(HALO, HALO + OY)

    def clear(x, _):
        for f in range(NEL):
            els_ref[f, x, 16:24] = zero
        return 0

    lax.fori_loop(0, WE, clear, 0)

    def clear_start(x, _):
        for c in range(3):
            for row in (0, 8, 16):
                b0[c, x, row : row + 8] = zero
        return 0

    lax.fori_loop(0, WX, clear_start, 0)

    def own(x, _):
        w = x + HALO
        for f in range(NEL):
            if f < 8:
                value = flags_ref[f, x].astype(F32) * (-PLASTIC_GAIN / 8.0)
            elif f < CONTACT_AT:
                value = flow_ref[FLOW_SENT[f - 8], x]
            else:
                value = contact_ref[x]
            els_ref[f, w, mid] = value
        for c in range(3):
            b0[c, w, mid] = part_ref[c, x, 0:16]
            b0[c, w, 19:20] = part_ref[c, x, 16:17] * has_u
        return 0

    lax.fori_loop(0, OX, own, 0)
    for x in range(OX):
        for f in range(NEL):
            els_ref[f, x + HALO, low] = rows_ref[below, ROW_AT[x] + 3 * f : ROW_AT[x] + 3 * f + 3]
            els_ref[f, x + HALO, high] = rows_ref[above, ROW_AT[x] + 2 * f : ROW_AT[x] + 2 * f + 2]
    for c in range(3):
        b0[c, 12, mid] = part_ref[c, OX, 0:16] * has_r
        b0[c, 12, 19:20] = part_ref[c, OX, 16:17] * (has_r * has_u)
    for i in range(3):
        for f in range(NEL):
            els_ref[f, i, mid] = left_ref[3 * f + i]
            els_ref[f, i, low] = cl_ref[above, ROW_AT[i] + 3 * f : ROW_AT[i] + 3 * f + 3]
            els_ref[f, i, high] = cl_ref[below, ROW_AT[i] + 2 * f : ROW_AT[i] + 2 * f + 2]
    for i in range(2):
        for f in range(NEL):
            els_ref[f, 12 + i, mid] = right_ref[2 * f + i]
            els_ref[f, 12 + i, low] = cr_ref[above, ROW_AT[i] + 3 * f : ROW_AT[i] + 3 * f + 3]
            els_ref[f, 12 + i, high] = cr_ref[below, ROW_AT[i] + 2 * f : ROW_AT[i] + 2 * f + 2]

    def zz(x, _):
        for row in (0, 8, 16):
            els_ref[ZZ_AT, x, row : row + 8] = -(els_ref[8, x, row : row + 8] + els_ref[9, x, row : row + 8])
        return 0

    lax.fori_loop(0, WE, zz, 0)

    def from_below(piece):
        return jnp.where(at_first_y, 0.0, piece)

    for c in range(3):
        for i in range(4):
            b0[c, i, mid] += left_ref[42 + 4 * c + i] * has_l
            b0[c, i, 19:20] += left_ref[54, 4 * c + i : 4 * c + i + 1] * (has_l * has_u)
            b0[c, i, 0:4] += from_below(cl_ref[above, moved(up_rows(6 + i, c), HIGH_PART.start)]) * has_l
            b0[c, i, 19:22] += cl_ref[below, moved(down_rows(6 + i, c), HIGH_PART.start)] * (has_l * has_u)
        for i in range(3):
            b0[c, 12 + i, mid] += right_ref[28 + 3 * c + i] * has_r
            b0[c, 12 + i, 19:20] += right_ref[37, 3 * c + i : 3 * c + i + 1] * (has_r * has_u)
            b0[c, 12 + i, 0:4] += from_below(cr_ref[above, up_rows(i, c)]) * has_r
            b0[c, 12 + i, 19:22] += cr_ref[below, down_rows(i, c)] * (has_r * has_u)

    for x in range(OX + 1):
        inside = has_r if x == OX else 1.0
        for c in range(3):
            b0[c, x + HALO, 0:4] += from_below(rows_ref[below, up_rows(x, c)]) * inside
            b0[c, x + HALO, 19:22] += rows_ref[above, down_rows(x, c)] * (inside * has_u)

    basis = (b0, b1, b2, b3)
    three_steps(els_ref, basis, z_ref, lower_ref, upper_ref)

    def collect(x, sums):
        sums = list(sums)
        for row in (0, 8):
            for c in range(3):
                v = [b[c, x + HALO, row + HALO : row + HALO + 8] for b in basis]
                for k in range(4):
                    own_ref[k, c, x, row : row + 8] = v[k]
                for k in range(7):
                    sums[k] = sums[k] + v[k // 2] * v[k - k // 2]
        return tuple(sums)

    sums = lax.fori_loop(0, OX, collect, (zero,) * 7)
    dots_ref[...] = zero
    for k in range(7):
        dots_ref[k : k + 1] = sum_rows(sums[k])

    def edge_rows(c, x):
        last, start = b3[c, x, 16:19], b3[c, x, 3:6]
        return jnp.where(below == 0, last, start), jnp.where(below == 0, start, last)

    for i in range(3):
        for c in range(3):
            for out, x in ((right_out, 9 + i), (left_out, 3 + i)):
                out[16 * (3 * c + i) : 16 * (3 * c + i) + 16] = b3[c, x, mid]
                first, second = edge_rows(c, x)
                at = 9 * i + 3 * c
                out[144 + at : 147 + at] = second
                out[176 + at : 179 + at] = first
    for x in range(OX):
        for c in range(3):
            first, second = edge_rows(c, x + HALO)
            at = 9 * x + 3 * c
            first_out[at : at + 3] = first
            second_out[at : at + 3] = second


def second_kernel(els_ref, own_ref, dots_ref, left_ref, right_ref, first_ref, second_ref,
                  tail_ref, row_ref, b0, b1, b2, b3, z_ref, lower_ref, upper_ref):
    _, at_last_x, _, at_last_y = place()
    has_r, has_u = ask(at_last_x), ask(at_last_y)
    below = odd()
    zero = jnp.zeros((8, DZ), F32)
    mid = slice(HALO, HALO + OY)

    def own(x, _):
        for c in range(3):
            b0[c, x + HALO, mid] = own_ref[3, c, x]
        return 0

    for x in range(WX):
        inside = has_r if x >= HALO + OX else 1.0
        for c in range(3):
            b0[c, x, 16:24] = zero
            at = 88 + 9 * x if x < HALO else 9 * (x - HALO) if x < HALO + OX else 120 + 9 * (x - HALO - OX)
            rows = slice(at + 3 * c, at + 3 * c + 3)
            one, two = first_ref[rows] * inside, second_ref[rows] * inside
            b0[c, x, 0:3] = jnp.where(below == 0, one, two)
            b0[c, x, 19:22] = jnp.where(below == 0, two, one) * has_u
    lax.fori_loop(0, OX, own, 0)
    for c in range(3):
        for i in range(3):
            block = slice(16 * (3 * c + i), 16 * (3 * c + i) + 16)
            b0[c, i, mid] = left_ref[block]
            b0[c, 12 + i, mid] = right_ref[block] * has_r

    basis = (b0, b1, b2, b3)
    three_steps(els_ref, basis, z_ref, lower_ref, upper_ref)

    def collect(x, sums):
        sums = list(sums)
        for row in (0, 8):
            for c in range(3):
                v = [own_ref[3, c, x, row : row + 8]]
                for k in range(1, 4):
                    w = b_at(basis[k], c, x, row)
                    v.append((w + w) - own_ref[3 - k, c, x, row : row + 8])
                    tail_ref[k - 1, c, x, row : row + 8] = v[k]
                for k in range(1, 6):
                    sums[k - 1] = sums[k - 1] + v[k // 2] * v[k - k // 2]
        return tuple(sums)

    sums = lax.fori_loop(0, OX, collect, (zero,) * 5)
    lane = lax.broadcasted_iota(jnp.int32, (1, DZ), 1)
    line = jnp.zeros((1, DZ), F32)
    for k in range(12):
        dot = dots_ref[k : k + 1] if k < 7 else sum_rows(sums[k - 7])
        line = jnp.where(lane == k, jnp.sum(dot, axis=1, keepdims=True), line)
    row_ref[...] = jnp.broadcast_to(line, row_ref.shape)


def b_at(ref, c, x, row):
    return ref[c, x + HALO, row + HALO : row + HALO + 8]


def times_matrix(p):
    out = [None] * (len(p) + 1)

    def add(k, value):
        out[k] = value if out[k] is None else out[k] + value

    for k, value in enumerate(p):
        add(k, value * (SPAN / 2))
        if k == 0:
            add(1, value * (SPAN / 2))
        else:
            add(k + 1, value * (SPAN / 4))
            add(k - 1, value * (SPAN / 4))
    return out


def tree_sum(values):
    while len(values) > 1:
        values = [a + b for a, b in zip(values[::2], values[1::2])] + ([values[-1]] if len(values) % 2 else [])
    return values[0]


def combine(p, a, q):
    out = []
    for k in range(max(len(p), len(q))):
        term = a * q[k] if k < len(q) else None
        if k < len(p):
            term = p[k] if term is None else p[k] + term
        out.append(term)
    return out


def coefficients(mu):
    gram = [[0.5 * (mu[i + j] + mu[abs(i - j)]) if i + j < len(mu) else None for j in range(7)] for i in range(7)]

    def inner(p, q):
        return tree_sum([p[i] * tree_sum([gram[i][j] * q[j] for j in range(len(q))]) for i in range(len(p))])

    remain = [jnp.ones_like(mu[0])]
    total = []
    for newton in range(NEWTON):
        direction = remain
        norm = inner(remain, remain)
        for step in range(CG_STEPS):
            image = times_matrix(direction)
            alpha = norm / inner(direction, image)
            total = combine(total, alpha, direction)
            remain = combine(remain, -alpha, image)
            if step + 1 < CG_STEPS:
                norm_next = inner(remain, remain)
                direction = combine(remain, norm_next / norm, direction)
                norm = norm_next
    return total, remain


def last_kernel(dots_ref, own_ref, tail_ref, displacement_ref, residual_ref):
    sums = jnp.sum(dots_ref[...], axis=0, keepdims=True)
    dots = [jnp.broadcast_to(sums[:, k : k + 1], (1, DZ)) for k in range(12)]
    mu = dots[:2]
    for k in range(2, 12):
        mu.append((dots[k] + dots[k]) - mu[k % 2])
    total, remain = coefficients(mu)
    total = [jnp.broadcast_to(value, (8, DZ)) for value in total]
    remain = [jnp.broadcast_to(value, (8, DZ)) for value in remain]

    def write(x, _):
        for row in (0, 8):
            for c in range(3):
                v = [own_ref[k, c, x, row : row + 8] for k in range(4)]
                v += [tail_ref[k, c, x, row : row + 8] for k in range(3)]
                displacement_ref[c, x, row : row + 8] = tree_sum([a * b for a, b in zip(total, v)])
                residual_ref[c, x, row : row + 8] = tree_sum([a * b for a, b in zip(remain, v)])
        return 0

    lax.fori_loop(0, OX, write, 0)


def shape(*dims):
    return jax.ShapeDtypeStruct(dims, F32)


def call(kernel, outs, scratch=(), mebibytes=24, **more):
    return pl.pallas_call(
        kernel,
        out_shape=outs,
        scratch_shapes=[pltpu.VMEM(dims, F32) if isinstance(dims, tuple) else dims for dims in scratch],
        compiler_params=pltpu.CompilerParams(vmem_limit_bytes=mebibytes * 1024 * 1024),
        **more,
    )


STEP_SCRATCH = [(3, WX, WY, DZ)] * 4 + [(6, WX, WY + 8, DZ)] * 3


def rotate(value, axis, steps):
    count = lax.axis_size(axis)
    return lax.ppermute(value, axis, [(i, (i + steps) % count) for i in range(count)])


def wind(value, forward):
    count_x, count_y = lax.axis_size("gx"), lax.axis_size("gy")
    pairs = []
    for x in range(count_x):
        for y in range(count_y):
            ahead = y + 1 if (x % 2 == 0) == forward else y - 1
            goal = (x, ahead) if 0 <= ahead < count_y else (x ^ 1, y)
            pairs.append((x * count_y + y, goal[0] * count_y + goal[1]))
    return lax.ppermute(value, ("gx", "gy"), pairs)


def exchange(right, left, first, second):
    from_left = rotate(right, "gx", 1)
    from_right = rotate(left, "gx", -1)
    rows = jnp.stack([wind(first, True), wind(second, False)])
    corner_left = rotate(rows[:, HIGH_PART], "gx", 1)
    corner_right = rotate(rows[:, LOW_PART], "gx", -1)
    return from_left, from_right, rows, corner_left, corner_right


def exchange_in_turn(right, left, first, second):
    from_left = rotate(right, "gx", 1)
    from_right = rotate(left, "gx", -1)
    first = jnp.concatenate([first, from_left[144:176], from_right[144:176]], axis=0)
    second = jnp.concatenate([second, from_left[176:208], from_right[176:208]], axis=0)
    return from_left, from_right, wind(first, True), wind(second, False)


def body(load, plastic_flags, flow_dir, contact_flags, die_depth):
    slabs = [(55, OY, DZ), (38, OY, DZ), (SLAB_ROWS, DZ), (SLAB_ROWS, DZ)]
    work = [(6, OX + 1, WY + 8, DZ)] * 2
    outside = pl.BlockSpec(memory_space=pl.ANY)
    inputs = (load, plastic_flags, flow_dir, contact_flags, die_depth)
    right, left, first, second = call(
        slab_kernel,
        [shape(*dims) for dims in slabs],
        slabs[:2] + [(2, SLAB_ROWS, DZ), (3, OX + 1, WY, DZ), (OX, OY, DZ)] + work
        + [(3, OX, OY, DZ), pltpu.VMEM((8, OX, OY, DZ), jnp.int32), (6, OX, OY, DZ),
           pltpu.VMEM((OX, OY), jnp.int32), (OX, OY)]
        + [pltpu.SemaphoreType.DMA((count,)) for count in (3, 8, 6, 2, 6)],
        mebibytes=54,
        in_specs=[outside] * 5,
        out_specs=[outside] * 4,
    )(*inputs)
    part, contact = call(
        part_kernel, [shape(3, OX + 1, WY, DZ), shape(OX, OY, DZ)], work,
        cost_estimate=pl.CostEstimate(flops=4000000, bytes_accessed=2000000, transcendentals=0),
    )(*inputs)
    halos = exchange(right, left, first, second)
    els, own, dots, right, left, first, second = call(
        first_kernel,
        [shape(NEL + 1, WE, WY, DZ), shape(4, 3, OX, OY, DZ), shape(8, DZ), shape(208, DZ), shape(208, DZ), shape(88, DZ), shape(88, DZ)],
        STEP_SCRATCH,
    )(plastic_flags, flow_dir, contact, part, *halos)
    halos = exchange_in_turn(right, left, first, second)
    count = lax.axis_size("gx") * lax.axis_size("gy")
    tail, line = call(
        second_kernel, [shape(3, 3, OX, OY, DZ), shape(count, DZ)], STEP_SCRATCH
    )(els, own, dots, *halos)
    lines = lax.all_to_all(line, ("gx", "gy"), 0, 0, tiled=True)
    return tuple(call(last_kernel, [shape(3, OX, OY, DZ)] * 2)(lines, own, tail))


def solution(mesh):
    in_specs = (
        P(None, "gx", "gy", None),
        P(None, "gx", "gy", None),
        P(None, "gx", "gy", None),
        P("gx", "gy"),
        P("gx", "gy"),
    )
    out_specs = (P(None, "gx", "gy", None), P(None, "gx", "gy", None))
    return jax.shard_map(body, mesh=mesh, in_specs=in_specs, out_specs=out_specs, check_vma=False)
```

```python
import math

import jax
import jax.numpy as jnp
from jax import lax
from jax.experimental import pallas as pl
from jax.experimental.pallas import tpu as pltpu
from jax.sharding import PartitionSpec as P

PLASTIC_GAIN = 6.0 / 3.1
YIELD_OFFSET = 0.05
CONTACT_STIFF = 4.0
CG_STEPS = 3
NEWTON = 2
ROOT_THIRD = 1.0 / math.sqrt(3.0)
THIRD = 1.0 / 3.0
SPAN = 10.0

HALO = 3
OX, OY, DZ = 9, 16, 128
WX = OX + 2 * HALO
WE = WX - 1
WY = 24
F32 = jnp.float32

FLOW_SENT = (0, 1, 3, 4, 5)
NEL = 14
CONTACT_AT = 13
ZZ_AT = 14


UP_AT = (0, 54, 108, 168, 222, 276, 336, 390, 444, 498)
DOWN_AT = (0, 37, 74, 112, 149, 186, 224, 261, 298, 335)
UP_ROWS, DOWN_ROWS = 512, 344
UP_LOW, UP_HIGH = slice(0, 168), slice(336, 512)
DOWN_LOW, DOWN_HIGH = slice(0, 112), slice(224, 344)


def up_rows(x, c):
    at = UP_AT[x] + (42 if x < OX else 0) + 4 * c
    return slice(at, at + 4)


def down_rows(x, c):
    at = DOWN_AT[x] + (28 if x < OX else 0) + 3 * c
    return slice(at, at + 3)


def moved(rows, by):
    return slice(rows.start - by, rows.stop - by)


def lanes():
    return lax.broadcasted_iota(jnp.int32, (8, DZ), 1)


def z_pair(value, first_lane):
    low = jnp.where(first_lane, 0.0, pltpu.roll(value, 1, 1))
    return value + low, value - low


def z_merge(total, slope, last_lane):
    return total + slope + jnp.where(last_lane, 0.0, pltpu.roll(total - slope, DZ - 1, 1))


def to_points(s1, sx, sy, sz, syz, sxz, sxy):
    points = []
    for sign_x in (-1, 1):
        a0 = s1 + sx if sign_x > 0 else s1 - sx
        ay = sy + sxy if sign_x > 0 else sy - sxy
        az = sz + sxz if sign_x > 0 else sz - sxz
        for sign_y in (-1, 1):
            b0 = a0 + ay if sign_y > 0 else a0 - ay
            bz = az + syz if sign_y > 0 else az - syz
            points += [b0 - bz, b0 + bz]
    return points


def from_points(t):
    per_x = []
    for i in range(2):
        e0 = [t[4 * i + 2 * j + 1] + t[4 * i + 2 * j] for j in range(2)]
        ez = [t[4 * i + 2 * j + 1] - t[4 * i + 2 * j] for j in range(2)]
        per_x.append((e0[1] + e0[0], e0[1] - e0[0], ez[1] + ez[0], ez[1] - ez[0]))
    low, high = per_x
    t1, ty, tz, tyz = (high[m] + low[m] for m in range(4))
    tx, txy, txz = (high[m] - low[m] for m in range(3))
    return t1, tx, ty, tz, tyz, txz, txy


def plastic_forces(n, t):
    nxx, nyy, nzz, nxy, nyz, nzx = n
    t1, tx, ty, tz, tyz, txz, txy = t
    tx, ty, tz = tx * ROOT_THIRD, ty * ROOT_THIRD, tz * ROOT_THIRD
    tyz, txz, txy = tyz * THIRD, txz * THIRD, txy * THIRD
    a_xy, a_yz, a_zx = nxy * t1, nyz * t1, nzx * t1
    fx = [nxx * t1, a_xy, a_zx]
    fy = [a_xy, nyy * t1, a_yz]
    fz = [a_zx, a_yz, nzz * t1]
    xy_z, yz_x, zx_y = nxy * tz, nyz * tx, nzx * ty
    fxy = [nxx * ty + nxy * tx, nxy * ty + nyy * tx, zx_y + yz_x]
    fxz = [nxx * tz + nzx * tx, xy_z + yz_x, nzx * tz + nzz * tx]
    fyz = [xy_z + zx_y, nyy * tz + nyz * ty, nyz * tz + nzz * ty]
    fxyz = [
        nxx * tyz + nxy * txz + nzx * txy,
        nxy * tyz + nyy * txz + nyz * txy,
        nzx * tyz + nyz * txz + nzz * txy,
    ]
    return fx, fy, fz, fxy, fxz, fyz, fxyz


def element_core(modes, n, flags):
    ax, ay, az, axy, axz, ayz, axyz = modes
    nxx, nyy, nzz, nxy, nyz, nzx = n
    sh_xy, sh_yz, sh_zx = ax[1] + ay[0], ay[2] + az[1], az[0] + ax[2]
    k_x, k_y, k_z = axy[2] + axz[1], axy[2] + ayz[0], axz[1] + ayz[0]
    s1 = (nxx * ax[0] + nyy * ay[1] + nzz * az[2]) + (nxy * sh_xy + nyz * sh_yz + nzx * sh_zx)
    sx = (nxy * axy[0] + nyy * axy[1]) + (nyz * k_x + nzx * axz[0] + nzz * axz[2])
    sy = (nxx * axy[0] + nxy * axy[1]) + (nzx * k_y + nyz * ayz[1] + nzz * ayz[2])
    sz = (nxx * axz[0] + nxy * k_z) + (nzx * axz[2] + nyy * ayz[1] + nyz * ayz[2])
    syz = nxx * axyz[0] + nxy * axyz[1] + nzx * axyz[2]
    sxz = nxy * axyz[0] + nyy * axyz[1] + nyz * axyz[2]
    sxy = nzx * axyz[0] + nyz * axyz[1] + nzz * axyz[2]
    values = to_points(
        s1, sx * ROOT_THIRD, sy * ROOT_THIRD, sz * ROOT_THIRD, syz * THIRD, sxz * THIRD, sxy * THIRD
    )
    plastic = plastic_forces(n, from_points([value * flag for value, flag in zip(values, flags)]))
    trace = ax[0] + ay[1] + az[2]
    tr_x, tr_y, tr_z = (
        (axy[1] + axz[2]) * THIRD,
        (axy[0] + ayz[2]) * THIRD,
        (axz[0] + ayz[1]) * THIRD,
    )
    mixed = (k_x + ayz[0]) * THIRD
    elastic = (
        [trace + (ax[0] + ax[0]), sh_xy, sh_zx],
        [sh_xy, trace + (ay[1] + ay[1]), sh_yz],
        [sh_zx, sh_yz, trace + (az[2] + az[2])],
        [tr_y + axy[0], tr_x + axy[1], mixed + axy[2] * THIRD],
        [tr_z + axz[0], mixed + axz[1] * THIRD, tr_x + axz[2]],
        [mixed + ayz[0] * THIRD, tr_z + ayz[1], tr_y + ayz[2]],
        [axyz[c] * (5.0 / 9.0) for c in range(3)],
    )
    return [[elastic[m][c] + plastic[m][c] for c in range(3)] for m in range(7)]


def scatter_x(forces, behind):
    fx, fy, fz, fxy, fxz, fyz, fxyz = forces
    node, ahead = [], []
    for c in range(3):
        node += [
            behind[4 * c] - fx[c],
            behind[4 * c + 1] + (fy[c] - fxy[c]),
            behind[4 * c + 2] + (fz[c] - fxz[c]),
            behind[4 * c + 3] + (fyz[c] - fxyz[c]),
        ]
        ahead += [fx[c], fy[c] + fxy[c], fz[c] + fxz[c], fyz[c] + fxyz[c]]
    return node, ahead


def store_y(node, lower_ref, upper_ref, x, row, upper_keep=None):
    for c in range(3):
        ss, sd, ds, dd = node[4 * c : 4 * c + 4]
        lower_ref[2 * c, x, row : row + 8] = ss - sd
        lower_ref[2 * c + 1, x, row : row + 8] = ds - dd
        up_s, up_d = ss + sd, ds + dd
        if upper_keep is not None:
            up_s, up_d = jnp.where(upper_keep, up_s, 0.0), jnp.where(upper_keep, up_d, 0.0)
        upper_ref[2 * c, x, row + 8 : row + 16] = up_s
        upper_ref[2 * c + 1, x, row + 8 : row + 16] = up_d


def merge_yz(lower_ref, upper_ref, c, x, row, last_lane):
    total = lower_ref[2 * c, x, row : row + 8] + upper_ref[2 * c, x, row + 7 : row + 15]
    slope = lower_ref[2 * c + 1, x, row : row + 8] + upper_ref[2 * c + 1, x, row + 7 : row + 15]
    return z_merge(total, slope, last_lane)


def place():
    index_x, index_y = lax.axis_index("gx"), lax.axis_index("gy")
    return (
        index_x == 0,
        index_x == lax.axis_size("gx") - 1,
        index_y == 0,
        index_y == lax.axis_size("gy") - 1,
    )


def odd():
    return lax.rem(lax.axis_index("gx"), 2)


def ask(flag):
    return jnp.where(flag, 0.0, 1.0).astype(F32)


def top_fields(active_ref, die_ref):
    last = lax.broadcasted_iota(jnp.int32, (OY, DZ), 1) == DZ - 1
    same = lax.broadcasted_iota(jnp.int32, (OY, OY), 0) == lax.broadcasted_iota(jnp.int32, (OY, OY), 1)

    def on_rows(row):
        turned = jnp.sum(jnp.where(same, jnp.broadcast_to(row, (OY, OY)), 0.0), axis=1, keepdims=True)
        return jnp.where(last, turned, 0.0)

    contact, die = [], []
    for x in range(OX):
        stiff = CONTACT_STIFF * active_ref[x : x + 1].astype(F32)
        contact.append(on_rows(stiff))
        die.append(on_rows(stiff * die_ref[x : x + 1]))
    return contact, die


def own_part(flags_ref, flow_ref, part_ref, lower_ref, upper_ref):
    last_lane = lanes() == DZ - 1
    zero = jnp.zeros((8, DZ), F32)

    def clear(x, _):
        for m in range(6):
            lower_ref[m, x, 16:24] = zero
            upper_ref[m, x, 0:8] = zero
        return 0

    lax.fori_loop(0, OX + 1, clear, 0)
    for row in (0, 8):

        def element(x, behind):
            flags = [flags_ref[q, x, row : row + 8].astype(F32) * (0.5 * PLASTIC_GAIN * YIELD_OFFSET) for q in range(8)]
            n = [flow_ref[m, x, row : row + 8] for m in range(6)]
            node, ahead = scatter_x(plastic_forces(n, from_points(flags)), behind)
            store_y(node, lower_ref, upper_ref, x, row)
            return ahead

        behind = lax.fori_loop(0, OX, element, [zero] * 12)
        store_y(behind, lower_ref, upper_ref, OX, row)
    for x in range(OX + 1):
        for c in range(3):
            for row in (0, 8, 16):
                part_ref[c, x, row : row + 8] = merge_yz(lower_ref, upper_ref, c, x, row, last_lane) * (-1.0 / 16.0)


def add_load(part_ref, load_ref, die):
    for x in range(OX):
        for c in range(3):
            value = part_ref[c, x, 0:OY] + load_ref[c, x]
            part_ref[c, x, 0:OY] = value + die[x] if c == 2 else value


def part_kernel(load_ref, flags_ref, flow_ref, active_ref, die_ref, part_ref, contact_ref, lower_ref, upper_ref):
    contact, die = top_fields(active_ref, die_ref)
    for x in range(OX):
        contact_ref[x] = contact[x]
    own_part(flags_ref, flow_ref, part_ref, lower_ref, upper_ref)
    add_load(part_ref, load_ref, die)


def slab_kernel(load_hbm, flags_hbm, flow_hbm, active_hbm, die_hbm, right_hbm, left_hbm, up_hbm, down_hbm,
                right_ref, left_ref, up_ref, down_ref, part_ref, contact_ref, lower_ref, upper_ref,
                load_ref, flags_ref, flow_ref, active_ref, die_ref, load_sem, flags_sem, flow_sem, top_sem, out_sem):
    small = [
        pltpu.make_async_copy(active_hbm, active_ref, top_sem.at[0]),
        pltpu.make_async_copy(die_hbm, die_ref, top_sem.at[1]),
    ]
    large = [
        [pltpu.make_async_copy(source.at[m : m + step], target.at[m : m + step], sem.at[m])
         for m in range(0, source.shape[0], step)]
        for source, target, sem, step in (
            (flags_hbm, flags_ref, flags_sem, 4), (flow_hbm, flow_ref, flow_sem, 3), (load_hbm, load_ref, load_sem, 3))
    ]
    for group in (small, *large):
        for copy in group:
            copy.start()
    for copy in small:
        copy.wait()
    contact, die = top_fields(active_ref, die_ref)
    for x in range(OX):
        contact_ref[x] = contact[x]
    for group in large[:2]:
        for copy in group:
            copy.wait()

    def field(f, x, rows):
        if f < 8:
            return flags_ref[f, x, rows].astype(F32) * (-PLASTIC_GAIN / 8.0)
        if f < CONTACT_AT:
            return flow_ref[FLOW_SENT[f - 8], x, rows]
        return contact_ref[x, rows]

    whole = slice(0, OY)
    for f in range(NEL):
        for i in range(3):
            right_ref[3 * f + i] = field(f, 6 + i, whole)
        for i in range(2):
            left_ref[2 * f + i] = field(f, i, whole)
    outs = [
        pltpu.make_async_copy(right_ref.at[0:42], right_hbm.at[0:42], out_sem.at[0]),
        pltpu.make_async_copy(left_ref.at[0:28], left_hbm.at[0:28], out_sem.at[1]),
    ]
    for copy in outs:
        copy.start()

    for x in range(OX):
        for f in range(NEL):
            up_ref[UP_AT[x] + 3 * f : UP_AT[x] + 3 * f + 3] = field(f, x, slice(13, 16))
            down_ref[DOWN_AT[x] + 2 * f : DOWN_AT[x] + 2 * f + 2] = field(f, x, slice(0, 2))
    own_part(flags_ref, flow_ref, part_ref, lower_ref, upper_ref)
    for copy in large[2]:
        copy.wait()
    add_load(part_ref, load_ref, die)

    for x in range(OX + 1):
        for c in range(3):
            up_ref[up_rows(x, c)] = part_ref[c, x, 13:17]
            down_ref[down_rows(x, c)] = part_ref[c, x, 0:3]
    outs += [
        pltpu.make_async_copy(up_ref, up_hbm, out_sem.at[2]),
        pltpu.make_async_copy(down_ref, down_hbm, out_sem.at[3]),
    ]
    for copy in outs[2:]:
        copy.start()
    for c in range(3):
        for i in range(4):
            right_ref[42 + 4 * c + i] = part_ref[c, 6 + i, 0:16]
            right_ref[54, 4 * c + i : 4 * c + i + 1] = part_ref[c, 6 + i, 16:17]
        for i in range(3):
            left_ref[28 + 3 * c + i] = part_ref[c, i, 0:16]
            left_ref[37, 3 * c + i : 3 * c + i + 1] = part_ref[c, i, 16:17]
    outs += [
        pltpu.make_async_copy(right_ref.at[42:55], right_hbm.at[42:55], out_sem.at[4]),
        pltpu.make_async_copy(left_ref.at[28:38], left_hbm.at[28:38], out_sem.at[5]),
    ]
    for copy in outs[4:]:
        copy.start()
    for copy in outs:
        copy.wait()


def three_steps(els_ref, basis, z_ref, lower_ref, upper_ref):
    at_first_x, at_last_x, at_first_y, at_last_y = place()
    lane = lanes()
    first_lane, last_lane = lane == 0, lane == DZ - 1
    rows = lax.broadcasted_iota(jnp.int32, (8, DZ), 0)
    keep_upper = jnp.logical_or(rows >= HALO, jnp.logical_not(at_first_y))
    keep_node = jnp.logical_or(rows < HALO, jnp.logical_not(at_last_y))
    zero = jnp.zeros((8, DZ), F32)

    def clear(x, _):
        for m in range(6):
            z_ref[m, x, 24:32] = zero
            upper_ref[m, x, 0:8] = zero
        return 0

    lax.fori_loop(0, WX, clear, 0)

    def first(x, _):
        for row in (0, 8, 16):
            for c in range(3):
                z_ref[2 * c, x, row : row + 8], z_ref[2 * c + 1, x, row : row + 8] = z_pair(
                    basis[0][c, x, row : row + 8], first_lane
                )
        return 0

    lax.fori_loop(0, WX, first, 0, unroll=5)

    for step in range(1, HALO + 1):
        start, end = step - 1, WX - 1 - step
        scale = (2.0 if step == 1 else 4.0) / SPAN
        for row in (0, 8, 16):

            def plane(x):
                values = []
                for m in range(6):
                    low, high = z_ref[m, x, row : row + 8], z_ref[m, x, row + 1 : row + 9]
                    values += [high + low, high - low]
                return values

            def element(x, carry):
                before, behind = carry
                after = plane(x + 1)
                p, q = before, after
                modes = (
                    [q[4 * c] - p[4 * c] for c in range(3)],
                    [q[4 * c + 1] + p[4 * c + 1] for c in range(3)],
                    [q[4 * c + 2] + p[4 * c + 2] for c in range(3)],
                    [q[4 * c + 1] - p[4 * c + 1] for c in range(3)],
                    [q[4 * c + 2] - p[4 * c + 2] for c in range(3)],
                    [q[4 * c + 3] + p[4 * c + 3] for c in range(3)],
                    [q[4 * c + 3] - p[4 * c + 3] for c in range(3)],
                )
                here = [els_ref[f, x, row : row + 8] for f in range(NEL + 1) if f != CONTACT_AT]
                n = (here[8], here[9], here[13], here[10], here[11], here[12])
                node, ahead = scatter_x(element_core(modes, n, here[:8]), behind)
                store_y(node, lower_ref, upper_ref, x, row, keep_upper if row == 0 else None)
                return after, ahead

            carry = (plane(start), [zero] * 12)
            for x in range(start, HALO):
                carry = element(x, carry)
            carry = (carry[0], [jnp.where(at_first_x, 0.0, value) for value in carry[1]])
            first_pair = HALO + (end + 1 - HALO) % 2
            if first_pair > HALO:
                carry = element(HALO, carry)

            def pair(k, carry):
                x = first_pair + 2 * k
                return element(x + 1, element(x, carry))

            lax.fori_loop(0, (end + 1 - first_pair) // 2, pair, carry)

        for x in range(step, end + 1):
            for row in (0, 8, 16) if step < HALO else (HALO, HALO + 8):
                for c in range(3):
                    here = basis[step - 1][c, x, row : row + 8]
                    value = merge_yz(lower_ref, upper_ref, c, x, row, last_lane) * (scale / 16.0)
                    if c == 2:
                        value = value + (els_ref[CONTACT_AT, x, row : row + 8] * scale) * here
                    if step == 1:
                        value = value - here
                    else:
                        value = value - (here + here) - basis[step - 2][c, x, row : row + 8]
                    if x >= HALO + OX:
                        value = jnp.where(at_last_x, 0.0, value)
                    if row == 16:
                        value = jnp.where(keep_node, value, 0.0)
                    basis[step][c, x, row : row + 8] = value
                    if step < HALO:
                        z_ref[2 * c, x, row : row + 8], z_ref[2 * c + 1, x, row : row + 8] = z_pair(value, first_lane)


def sum_rows(values):
    return jnp.sum(values, axis=0, keepdims=True)


def first_kernel(flags_ref, flow_ref, contact_ref, part_ref, left_ref, right_ref, up_ref, down_ref, cl_ref, cr_ref,
                 els_ref, own_ref, dots_ref, right_out, left_out, first_out, second_out,
                 b0, b1, b2, b3, z_ref, lower_ref, upper_ref):
    at_first_x, at_last_x, at_first_y, at_last_y = place()
    has_l, has_r, has_u = ask(at_first_x), ask(at_last_x), ask(at_last_y)
    zero = jnp.zeros((8, DZ), F32)
    low, high = slice(0, 3), slice(19, 21)
    mid = slice(HALO, HALO + OY)

    def clear(x, _):
        for f in range(NEL):
            els_ref[f, x, 16:24] = zero
        return 0

    lax.fori_loop(0, WE, clear, 0)

    def clear_start(x, _):
        for c in range(3):
            for row in (0, 8, 16):
                b0[c, x, row : row + 8] = zero
        return 0

    lax.fori_loop(0, WX, clear_start, 0)

    def own(x, _):
        w = x + HALO
        for f in range(NEL):
            if f < 8:
                value = flags_ref[f, x].astype(F32) * (-PLASTIC_GAIN / 8.0)
            elif f < CONTACT_AT:
                value = flow_ref[FLOW_SENT[f - 8], x]
            else:
                value = contact_ref[x]
            els_ref[f, w, mid] = value
        for c in range(3):
            b0[c, w, mid] = part_ref[c, x, 0:16]
            b0[c, w, 19:20] = part_ref[c, x, 16:17] * has_u
        return 0

    lax.fori_loop(0, OX, own, 0)
    for x in range(OX):
        for f in range(NEL):
            els_ref[f, x + HALO, low] = up_ref[UP_AT[x] + 3 * f : UP_AT[x] + 3 * f + 3]
            els_ref[f, x + HALO, high] = down_ref[DOWN_AT[x] + 2 * f : DOWN_AT[x] + 2 * f + 2]
    for c in range(3):
        b0[c, 12, mid] = part_ref[c, OX, 0:16] * has_r
        b0[c, 12, 19:20] = part_ref[c, OX, 16:17] * (has_r * has_u)
    for i in range(3):
        for f in range(NEL):
            els_ref[f, i, mid] = left_ref[3 * f + i]
            els_ref[f, i, low] = cl_ref[UP_AT[i] + 3 * f : UP_AT[i] + 3 * f + 3]
            els_ref[f, i, high] = cl_ref[176 + DOWN_AT[i] + 2 * f : 176 + DOWN_AT[i] + 2 * f + 2]
    for i in range(2):
        for f in range(NEL):
            els_ref[f, 12 + i, mid] = right_ref[2 * f + i]
            els_ref[f, 12 + i, low] = cr_ref[UP_AT[i] + 3 * f : UP_AT[i] + 3 * f + 3]
            els_ref[f, 12 + i, high] = cr_ref[168 + DOWN_AT[i] + 2 * f : 168 + DOWN_AT[i] + 2 * f + 2]

    def zz(x, _):
        for row in (0, 8, 16):
            els_ref[ZZ_AT, x, row : row + 8] = -(els_ref[8, x, row : row + 8] + els_ref[9, x, row : row + 8])
        return 0

    lax.fori_loop(0, WE, zz, 0)

    def from_below(piece):
        return jnp.where(at_first_y, 0.0, piece)

    for c in range(3):
        for i in range(4):
            b0[c, i, mid] += left_ref[42 + 4 * c + i] * has_l
            b0[c, i, 19:20] += left_ref[54, 4 * c + i : 4 * c + i + 1] * (has_l * has_u)
            b0[c, i, 0:4] += from_below(cl_ref[moved(up_rows(6 + i, c), UP_HIGH.start)]) * has_l
            b0[c, i, 19:22] += cl_ref[moved(down_rows(6 + i, c), DOWN_HIGH.start - 176)] * (has_l * has_u)
        for i in range(3):
            b0[c, 12 + i, mid] += right_ref[28 + 3 * c + i] * has_r
            b0[c, 12 + i, 19:20] += right_ref[37, 3 * c + i : 3 * c + i + 1] * (has_r * has_u)
            b0[c, 12 + i, 0:4] += from_below(cr_ref[up_rows(i, c)]) * has_r
            b0[c, 12 + i, 19:22] += cr_ref[moved(down_rows(i, c), -168)] * (has_r * has_u)

    for x in range(OX + 1):
        inside = has_r if x == OX else 1.0
        for c in range(3):
            b0[c, x + HALO, 0:4] += from_below(up_ref[up_rows(x, c)]) * inside
            b0[c, x + HALO, 19:22] += down_ref[down_rows(x, c)] * (inside * has_u)

    basis = (b0, b1, b2, b3)
    three_steps(els_ref, basis, z_ref, lower_ref, upper_ref)

    def collect(x, sums):
        sums = list(sums)
        for row in (0, 8):
            for c in range(3):
                v = [b[c, x + HALO, row + HALO : row + HALO + 8] for b in basis]
                for k in range(4):
                    own_ref[k, c, x, row : row + 8] = v[k]
                for k in range(7):
                    sums[k] = sums[k] + v[k // 2] * v[k - k // 2]
        return tuple(sums)

    sums = lax.fori_loop(0, OX, collect, (zero,) * 7, unroll=3)
    dots_ref[...] = zero
    for k in range(7):
        dots_ref[k : k + 1] = sum_rows(sums[k])

    def edge_rows(c, x):
        last, start, goes_up = b3[c, x, 16:19], b3[c, x, 3:6], odd() == 0
        return jnp.where(goes_up, last, start), jnp.where(goes_up, start, last)

    for i in range(3):
        for c in range(3):
            for out, x in ((right_out, 9 + i), (left_out, 3 + i)):
                out[16 * (3 * c + i) : 16 * (3 * c + i) + 16] = b3[c, x, mid]
                first, second = edge_rows(c, x)
                at = 9 * i + 3 * c
                out[144 + at : 147 + at] = second
                out[176 + at : 179 + at] = first
    for x in range(OX):
        for c in range(3):
            first, second = edge_rows(c, x + HALO)
            at = 9 * x + 3 * c
            first_out[at : at + 3] = first
            second_out[at : at + 3] = second


def second_kernel(els_ref, own_ref, dots_ref, left_ref, right_ref, first_ref, second_ref,
                  tail_ref, row_ref, b0, b1, b2, b3, z_ref, lower_ref, upper_ref):
    _, at_last_x, _, at_last_y = place()
    has_r, has_u = ask(at_last_x), ask(at_last_y)
    below = odd()
    zero = jnp.zeros((8, DZ), F32)
    mid = slice(HALO, HALO + OY)

    def own(x, _):
        for c in range(3):
            b0[c, x + HALO, mid] = own_ref[3, c, x]
        return 0

    for x in range(WX):
        inside = has_r if x >= HALO + OX else 1.0
        for c in range(3):
            b0[c, x, 16:24] = zero
            at = 88 + 9 * x if x < HALO else 9 * (x - HALO) if x < HALO + OX else 120 + 9 * (x - HALO - OX)
            rows = slice(at + 3 * c, at + 3 * c + 3)
            one, two = first_ref[rows] * inside, second_ref[rows] * inside
            b0[c, x, 0:3] = jnp.where(below == 0, one, two)
            b0[c, x, 19:22] = jnp.where(below == 0, two, one) * has_u
    lax.fori_loop(0, OX, own, 0)
    for c in range(3):
        for i in range(3):
            block = slice(16 * (3 * c + i), 16 * (3 * c + i) + 16)
            b0[c, i, mid] = left_ref[block]
            b0[c, 12 + i, mid] = right_ref[block] * has_r

    basis = (b0, b1, b2, b3)
    three_steps(els_ref, basis, z_ref, lower_ref, upper_ref)

    def collect(x, sums):
        sums = list(sums)
        for row in (0, 8):
            for c in range(3):
                v = [own_ref[3, c, x, row : row + 8]]
                for k in range(1, 4):
                    w = b_at(basis[k], c, x, row)
                    v.append((w + w) - own_ref[3 - k, c, x, row : row + 8])
                    tail_ref[k - 1, c, x, row : row + 8] = v[k]
                for k in range(1, 6):
                    sums[k - 1] = sums[k - 1] + v[k // 2] * v[k - k // 2]
        return tuple(sums)

    sums = lax.fori_loop(0, OX, collect, (zero,) * 5, unroll=3)
    lane = lax.broadcasted_iota(jnp.int32, (1, DZ), 1)
    line = jnp.zeros((1, DZ), F32)
    for k in range(12):
        dot = dots_ref[k : k + 1] if k < 7 else sum_rows(sums[k - 7])
        line = jnp.where(lane == k, jnp.sum(dot, axis=1, keepdims=True), line)
    row_ref[...] = jnp.broadcast_to(line, row_ref.shape)


def b_at(ref, c, x, row):
    return ref[c, x + HALO, row + HALO : row + HALO + 8]


def times_matrix(p):
    out = [None] * (len(p) + 1)

    def add(k, value):
        out[k] = value if out[k] is None else out[k] + value

    for k, value in enumerate(p):
        add(k, value * (SPAN / 2))
        if k == 0:
            add(1, value * (SPAN / 2))
        else:
            add(k + 1, value * (SPAN / 4))
            add(k - 1, value * (SPAN / 4))
    return out


def tree_sum(values):
    while len(values) > 1:
        values = [a + b for a, b in zip(values[::2], values[1::2])] + ([values[-1]] if len(values) % 2 else [])
    return values[0]


def combine(p, a, q):
    out = []
    for k in range(max(len(p), len(q))):
        term = a * q[k] if k < len(q) else None
        if k < len(p):
            term = p[k] if term is None else p[k] + term
        out.append(term)
    return out


def coefficients(mu):
    gram = [[0.5 * (mu[i + j] + mu[abs(i - j)]) if i + j < len(mu) else None for j in range(7)] for i in range(7)]

    def inner(p, q):
        return tree_sum([p[i] * tree_sum([gram[i][j] * q[j] for j in range(len(q))]) for i in range(len(p))])

    remain = [jnp.ones_like(mu[0])]
    total = []
    for newton in range(NEWTON):
        direction = remain
        norm = inner(remain, remain)
        for step in range(CG_STEPS):
            image = times_matrix(direction)
            alpha = norm / inner(direction, image)
            total = combine(total, alpha, direction)
            remain = combine(remain, -alpha, image)
            if step + 1 < CG_STEPS:
                norm_next = inner(remain, remain)
                direction = combine(remain, norm_next / norm, direction)
                norm = norm_next
    return total, remain


def last_kernel(dots_ref, own_ref, tail_ref, displacement_hbm, residual_hbm, displacement_ref, residual_ref, sems):
    sums = jnp.sum(dots_ref[...], axis=0, keepdims=True)
    dots = [jnp.broadcast_to(sums[:, k : k + 1], (1, DZ)) for k in range(12)]
    mu = dots[:2]
    for k in range(2, 12):
        mu.append((dots[k] + dots[k]) - mu[k % 2])
    total, remain = coefficients(mu)
    total = [jnp.broadcast_to(value, (8, DZ)) for value in total]
    remain = [jnp.broadcast_to(value, (8, DZ)) for value in remain]
    copies = []
    for c in range(3):

        def write(x, _):
            for row in (0, 8):
                v = [own_ref[k, c, x, row : row + 8] for k in range(4)]
                v += [tail_ref[k, c, x, row : row + 8] for k in range(3)]
                displacement_ref[c, x, row : row + 8] = tree_sum([a * b for a, b in zip(total, v)])
                residual_ref[c, x, row : row + 8] = tree_sum([a * b for a, b in zip(remain, v)])
            return 0

        lax.fori_loop(0, OX, write, 0, unroll=3)
        for m, (source, target) in enumerate(((displacement_ref, displacement_hbm), (residual_ref, residual_hbm))):
            copies.append(pltpu.make_async_copy(source.at[c], target.at[c], sems.at[m, c]))
            copies[-1].start()
    for copy in copies:
        copy.wait()


def shape(*dims):
    return jax.ShapeDtypeStruct(dims, F32)


def call(kernel, outs, scratch=(), mebibytes=24, **more):
    return pl.pallas_call(
        kernel,
        out_shape=outs,
        scratch_shapes=[pltpu.VMEM(dims, F32) if isinstance(dims, tuple) else dims for dims in scratch],
        compiler_params=pltpu.CompilerParams(vmem_limit_bytes=mebibytes * 1024 * 1024),
        **more,
    )


STEP_SCRATCH = [(3, WX, WY, DZ)] * 4 + [(6, WX, WY + 8, DZ)] * 3


def rotate(value, axis, steps):
    count = lax.axis_size(axis)
    return lax.ppermute(value, axis, [(i, (i + steps) % count) for i in range(count)])


def wind(value, forward):
    count_x, count_y = lax.axis_size("gx"), lax.axis_size("gy")
    pairs = []
    for x in range(count_x):
        for y in range(count_y):
            ahead = y + 1 if (x % 2 == 0) == forward else y - 1
            goal = (x, ahead) if 0 <= ahead < count_y else (x ^ 1, y)
            pairs.append((x * count_y + y, goal[0] * count_y + goal[1]))
    return lax.ppermute(value, ("gx", "gy"), pairs)


def exchange(right, left, up, down):
    from_left = rotate(right, "gx", 1)
    from_right = rotate(left, "gx", -1)
    from_below = rotate(up, "gy", 1)
    from_above = rotate(down, "gy", -1)
    corner_left = rotate(jnp.concatenate([from_below[UP_HIGH], from_above[DOWN_HIGH]]), "gx", 1)
    corner_right = rotate(jnp.concatenate([from_below[UP_LOW], from_above[DOWN_LOW]]), "gx", -1)
    return from_left, from_right, from_below, from_above, corner_left, corner_right


def exchange_in_turn(right, left, first, second):
    from_left = rotate(right, "gx", 1)
    from_right = rotate(left, "gx", -1)
    first = jnp.concatenate([first, from_left[144:176], from_right[144:176]], axis=0)
    second = jnp.concatenate([second, from_left[176:208], from_right[176:208]], axis=0)
    return from_left, from_right, wind(first, True), wind(second, False)


def body(load, plastic_flags, flow_dir, contact_flags, die_depth):
    slabs = [(55, OY, DZ), (38, OY, DZ), (UP_ROWS, DZ), (DOWN_ROWS, DZ)]
    work = [(6, OX + 1, WY + 8, DZ)] * 2
    outside = pl.BlockSpec(memory_space=pl.ANY)
    inputs = (load, plastic_flags, flow_dir, contact_flags, die_depth)
    right, left, up, down = call(
        slab_kernel,
        [shape(*dims) for dims in slabs],
        slabs + [(3, OX + 1, WY, DZ), (OX, OY, DZ)] + work
        + [(3, OX, OY, DZ), pltpu.VMEM((8, OX, OY, DZ), jnp.int32), (6, OX, OY, DZ),
           pltpu.VMEM((OX, OY), jnp.int32), (OX, OY)]
        + [pltpu.SemaphoreType.DMA((count,)) for count in (3, 8, 6, 2, 6)],
        mebibytes=54,
        in_specs=[outside] * 5,
        out_specs=[outside] * 4,
    )(*inputs)
    part, contact = call(
        part_kernel, [shape(3, OX + 1, WY, DZ), shape(OX, OY, DZ)], work,
        cost_estimate=pl.CostEstimate(flops=400000, bytes_accessed=1000, transcendentals=0),
    )(*inputs)
    halos = exchange(right, left, up, down)
    els, own, dots, right, left, first, second = call(
        first_kernel,
        [shape(NEL + 1, WE, WY, DZ), shape(4, 3, OX, OY, DZ), shape(8, DZ), shape(208, DZ), shape(208, DZ), shape(88, DZ), shape(88, DZ)],
        STEP_SCRATCH,
    )(plastic_flags, flow_dir, contact, part, *halos)
    halos = exchange_in_turn(right, left, first, second)
    count = lax.axis_size("gx") * lax.axis_size("gy")
    tail, line = call(
        second_kernel, [shape(3, 3, OX, OY, DZ), shape(count, DZ)], STEP_SCRATCH
    )(els, own, dots, *halos)
    lines = lax.all_to_all(line, ("gx", "gy"), 0, 0, tiled=True)
    return tuple(
        call(
            last_kernel,
            [shape(3, OX, OY, DZ)] * 2,
            [(3, OX, OY, DZ)] * 2 + [pltpu.SemaphoreType.DMA((2, 3))],
            out_specs=[outside] * 2,
        )(lines, own, tail)
    )


def solution(mesh):
    in_specs = (
        P(None, "gx", "gy", None),
        P(None, "gx", "gy", None),
        P(None, "gx", "gy", None),
        P("gx", "gy"),
        P("gx", "gy"),
    )
    out_specs = (P(None, "gx", "gy", None), P(None, "gx", "gy", None))
    return jax.shard_map(body, mesh=mesh, in_specs=in_specs, out_specs=out_specs, check_vma=False)
```

```python
import math

import jax
import jax.numpy as jnp
from jax import lax
from jax.experimental import pallas as pl
from jax.experimental.pallas import tpu as pltpu
from jax.sharding import PartitionSpec as P

PLASTIC_GAIN = 6.0 / 3.1
YIELD_OFFSET = 0.05
CONTACT_STIFF = 4.0
CG_STEPS = 3
NEWTON = 2
ROOT_THIRD = 1.0 / math.sqrt(3.0)
THIRD = 1.0 / 3.0
SPAN = 10.0

HALO = 3
OX, OY, DZ = 9, 16, 128
WX = OX + 2 * HALO
WE = WX - 1
WY = 24
F32 = jnp.float32

FLOW_SENT = (0, 1, 3, 4, 5)
NEL = 14
CONTACT_AT = 13
ZZ_AT = 14


UP_AT = (0, 54, 108, 168, 222, 276, 336, 390, 444, 498)
DOWN_AT = (0, 37, 74, 112, 149, 186, 224, 261, 298, 335)
UP_ROWS, DOWN_ROWS = 512, 344
UP_LOW, UP_HIGH = slice(0, 168), slice(336, 512)
DOWN_LOW, DOWN_HIGH = slice(0, 112), slice(224, 344)


def up_rows(x, c):
    at = UP_AT[x] + (42 if x < OX else 0) + 4 * c
    return slice(at, at + 4)


def down_rows(x, c):
    at = DOWN_AT[x] + (28 if x < OX else 0) + 3 * c
    return slice(at, at + 3)


def moved(rows, by):
    return slice(rows.start - by, rows.stop - by)


def lanes():
    return lax.broadcasted_iota(jnp.int32, (8, DZ), 1)


def z_pair(value, first_lane):
    low = jnp.where(first_lane, 0.0, pltpu.roll(value, 1, 1))
    return value + low, value - low


def z_merge(total, slope, last_lane):
    return total + slope + jnp.where(last_lane, 0.0, pltpu.roll(total - slope, DZ - 1, 1))


def to_points(s1, sx, sy, sz, syz, sxz, sxy):
    points = []
    for sign_x in (-1, 1):
        a0 = s1 + sx if sign_x > 0 else s1 - sx
        ay = sy + sxy if sign_x > 0 else sy - sxy
        az = sz + sxz if sign_x > 0 else sz - sxz
        for sign_y in (-1, 1):
            b0 = a0 + ay if sign_y > 0 else a0 - ay
            bz = az + syz if sign_y > 0 else az - syz
            points += [b0 - bz, b0 + bz]
    return points


def from_points(t):
    per_x = []
    for i in range(2):
        e0 = [t[4 * i + 2 * j + 1] + t[4 * i + 2 * j] for j in range(2)]
        ez = [t[4 * i + 2 * j + 1] - t[4 * i + 2 * j] for j in range(2)]
        per_x.append((e0[1] + e0[0], e0[1] - e0[0], ez[1] + ez[0], ez[1] - ez[0]))
    low, high = per_x
    t1, ty, tz, tyz = (high[m] + low[m] for m in range(4))
    tx, txy, txz = (high[m] - low[m] for m in range(3))
    return t1, tx, ty, tz, tyz, txz, txy


def plastic_forces(n, t):
    nxx, nyy, nzz, nxy, nyz, nzx = n
    t1, tx, ty, tz, tyz, txz, txy = t
    tx, ty, tz = tx * ROOT_THIRD, ty * ROOT_THIRD, tz * ROOT_THIRD
    tyz, txz, txy = tyz * THIRD, txz * THIRD, txy * THIRD
    a_xy, a_yz, a_zx = nxy * t1, nyz * t1, nzx * t1
    fx = [nxx * t1, a_xy, a_zx]
    fy = [a_xy, nyy * t1, a_yz]
    fz = [a_zx, a_yz, nzz * t1]
    xy_z, yz_x, zx_y = nxy * tz, nyz * tx, nzx * ty
    fxy = [nxx * ty + nxy * tx, nxy * ty + nyy * tx, zx_y + yz_x]
    fxz = [nxx * tz + nzx * tx, xy_z + yz_x, nzx * tz + nzz * tx]
    fyz = [xy_z + zx_y, nyy * tz + nyz * ty, nyz * tz + nzz * ty]
    fxyz = [
        nxx * tyz + nxy * txz + nzx * txy,
        nxy * tyz + nyy * txz + nyz * txy,
        nzx * tyz + nyz * txz + nzz * txy,
    ]
    return fx, fy, fz, fxy, fxz, fyz, fxyz


def element_core(modes, n, flags):
    ax, ay, az, axy, axz, ayz, axyz = modes
    nxx, nyy, nzz, nxy, nyz, nzx = n
    sh_xy, sh_yz, sh_zx = ax[1] + ay[0], ay[2] + az[1], az[0] + ax[2]
    k_x, k_y, k_z = axy[2] + axz[1], axy[2] + ayz[0], axz[1] + ayz[0]
    s1 = (nxx * ax[0] + nyy * ay[1] + nzz * az[2]) + (nxy * sh_xy + nyz * sh_yz + nzx * sh_zx)
    sx = (nxy * axy[0] + nyy * axy[1]) + (nyz * k_x + nzx * axz[0] + nzz * axz[2])
    sy = (nxx * axy[0] + nxy * axy[1]) + (nzx * k_y + nyz * ayz[1] + nzz * ayz[2])
    sz = (nxx * axz[0] + nxy * k_z) + (nzx * axz[2] + nyy * ayz[1] + nyz * ayz[2])
    syz = nxx * axyz[0] + nxy * axyz[1] + nzx * axyz[2]
    sxz = nxy * axyz[0] + nyy * axyz[1] + nyz * axyz[2]
    sxy = nzx * axyz[0] + nyz * axyz[1] + nzz * axyz[2]
    values = to_points(
        s1, sx * ROOT_THIRD, sy * ROOT_THIRD, sz * ROOT_THIRD, syz * THIRD, sxz * THIRD, sxy * THIRD
    )
    plastic = plastic_forces(n, from_points([value * flag for value, flag in zip(values, flags)]))
    trace = ax[0] + ay[1] + az[2]
    tr_x, tr_y, tr_z = (
        (axy[1] + axz[2]) * THIRD,
        (axy[0] + ayz[2]) * THIRD,
        (axz[0] + ayz[1]) * THIRD,
    )
    mixed = (k_x + ayz[0]) * THIRD
    elastic = (
        [trace + (ax[0] + ax[0]), sh_xy, sh_zx],
        [sh_xy, trace + (ay[1] + ay[1]), sh_yz],
        [sh_zx, sh_yz, trace + (az[2] + az[2])],
        [tr_y + axy[0], tr_x + axy[1], mixed + axy[2] * THIRD],
        [tr_z + axz[0], mixed + axz[1] * THIRD, tr_x + axz[2]],
        [mixed + ayz[0] * THIRD, tr_z + ayz[1], tr_y + ayz[2]],
        [axyz[c] * (5.0 / 9.0) for c in range(3)],
    )
    return [[elastic[m][c] + plastic[m][c] for c in range(3)] for m in range(7)]


def scatter_x(forces, behind):
    fx, fy, fz, fxy, fxz, fyz, fxyz = forces
    node, ahead = [], []
    for c in range(3):
        node += [
            behind[4 * c] - fx[c],
            behind[4 * c + 1] + (fy[c] - fxy[c]),
            behind[4 * c + 2] + (fz[c] - fxz[c]),
            behind[4 * c + 3] + (fyz[c] - fxyz[c]),
        ]
        ahead += [fx[c], fy[c] + fxy[c], fz[c] + fxz[c], fyz[c] + fxyz[c]]
    return node, ahead


def store_y(node, lower_ref, upper_ref, x, row, upper_keep=None):
    for c in range(3):
        ss, sd, ds, dd = node[4 * c : 4 * c + 4]
        lower_ref[2 * c, x, row : row + 8] = ss - sd
        lower_ref[2 * c + 1, x, row : row + 8] = ds - dd
        up_s, up_d = ss + sd, ds + dd
        if upper_keep is not None:
            up_s, up_d = jnp.where(upper_keep, up_s, 0.0), jnp.where(upper_keep, up_d, 0.0)
        upper_ref[2 * c, x, row + 8 : row + 16] = up_s
        upper_ref[2 * c + 1, x, row + 8 : row + 16] = up_d


def merge_yz(lower_ref, upper_ref, c, x, row, last_lane):
    total = lower_ref[2 * c, x, row : row + 8] + upper_ref[2 * c, x, row + 7 : row + 15]
    slope = lower_ref[2 * c + 1, x, row : row + 8] + upper_ref[2 * c + 1, x, row + 7 : row + 15]
    return z_merge(total, slope, last_lane)


def place():
    index_x, index_y = lax.axis_index("gx"), lax.axis_index("gy")
    return (
        index_x == 0,
        index_x == lax.axis_size("gx") - 1,
        index_y == 0,
        index_y == lax.axis_size("gy") - 1,
    )


def odd():
    return lax.rem(lax.axis_index("gx"), 2)


def ask(flag):
    return jnp.where(flag, 0.0, 1.0).astype(F32)


def top_fields(active_ref, die_ref):
    last = lax.broadcasted_iota(jnp.int32, (OY, DZ), 1) == DZ - 1
    same = lax.broadcasted_iota(jnp.int32, (OY, OY), 0) == lax.broadcasted_iota(jnp.int32, (OY, OY), 1)

    def on_rows(row):
        turned = jnp.sum(jnp.where(same, jnp.broadcast_to(row, (OY, OY)), 0.0), axis=1, keepdims=True)
        return jnp.where(last, turned, 0.0)

    contact, die = [], []
    for x in range(OX):
        stiff = CONTACT_STIFF * active_ref[x : x + 1].astype(F32)
        contact.append(on_rows(stiff))
        die.append(on_rows(stiff * die_ref[x : x + 1]))
    return contact, die


def own_part(flags_ref, flow_ref, part_ref, lower_ref, upper_ref):
    last_lane = lanes() == DZ - 1
    zero = jnp.zeros((8, DZ), F32)

    def clear(x, _):
        for m in range(6):
            lower_ref[m, x, 16:24] = zero
            upper_ref[m, x, 0:8] = zero
        return 0

    lax.fori_loop(0, OX + 1, clear, 0)
    for row in (0, 8):

        def element(x, behind):
            flags = [flags_ref[q, x, row : row + 8].astype(F32) * (0.5 * PLASTIC_GAIN * YIELD_OFFSET) for q in range(8)]
            n = [flow_ref[m, x, row : row + 8] for m in range(6)]
            node, ahead = scatter_x(plastic_forces(n, from_points(flags)), behind)
            store_y(node, lower_ref, upper_ref, x, row)
            return ahead

        behind = lax.fori_loop(0, OX, element, [zero] * 12, unroll=3)
        store_y(behind, lower_ref, upper_ref, OX, row)
    for x in range(OX + 1):
        for c in range(3):
            for row in (0, 8, 16):
                part_ref[c, x, row : row + 8] = merge_yz(lower_ref, upper_ref, c, x, row, last_lane) * (-1.0 / 16.0)


def add_load(part_ref, load_ref, die):
    for x in range(OX):
        for c in range(3):
            value = part_ref[c, x, 0:OY] + load_ref[c, x]
            part_ref[c, x, 0:OY] = value + die[x] if c == 2 else value


def part_kernel(load_ref, flags_ref, flow_ref, active_ref, die_ref, part_ref, contact_ref, lower_ref, upper_ref):
    contact, die = top_fields(active_ref, die_ref)
    for x in range(OX):
        contact_ref[x] = contact[x]
    own_part(flags_ref, flow_ref, part_ref, lower_ref, upper_ref)
    add_load(part_ref, load_ref, die)


def slab_kernel(load_hbm, flags_hbm, flow_hbm, active_hbm, die_hbm, right_hbm, left_hbm, up_hbm, down_hbm,
                right_ref, left_ref, up_ref, down_ref, part_ref, contact_ref, lower_ref, upper_ref,
                load_ref, flags_ref, flow_ref, active_ref, die_ref, load_sem, flags_sem, flow_sem, top_sem, out_sem):
    small = [
        pltpu.make_async_copy(active_hbm, active_ref, top_sem.at[0]),
        pltpu.make_async_copy(die_hbm, die_ref, top_sem.at[1]),
    ]
    large = [
        [pltpu.make_async_copy(source.at[m : m + step], target.at[m : m + step], sem.at[m])
         for m in range(0, source.shape[0], step)]
        for source, target, sem, step in (
            (flags_hbm, flags_ref, flags_sem, 4), (flow_hbm, flow_ref, flow_sem, 3), (load_hbm, load_ref, load_sem, 3))
    ]
    for group in (small, *large):
        for copy in group:
            copy.start()
    for copy in small:
        copy.wait()
    contact, die = top_fields(active_ref, die_ref)
    for x in range(OX):
        contact_ref[x] = contact[x]

    def field(f, x, rows):
        if f < 8:
            return flags_ref[f, x, rows].astype(F32) * (-PLASTIC_GAIN / 8.0)
        if f < CONTACT_AT:
            return flow_ref[FLOW_SENT[f - 8], x, rows]
        return contact_ref[x, rows]

    whole = slice(0, OY)
    arrived = {0: large[0][0], 4: large[0][1], 8: large[1][0], 10: large[1][1]}
    for f in range(NEL):
        if f in arrived:
            arrived[f].wait()
        for i in range(3):
            right_ref[3 * f + i] = field(f, 6 + i, whole)
        for i in range(2):
            left_ref[2 * f + i] = field(f, i, whole)
        for x in range(OX):
            up_ref[UP_AT[x] + 3 * f : UP_AT[x] + 3 * f + 3] = field(f, x, slice(13, 16))
            down_ref[DOWN_AT[x] + 2 * f : DOWN_AT[x] + 2 * f + 2] = field(f, x, slice(0, 2))
    outs = [
        pltpu.make_async_copy(right_ref.at[0:42], right_hbm.at[0:42], out_sem.at[0]),
        pltpu.make_async_copy(left_ref.at[0:28], left_hbm.at[0:28], out_sem.at[1]),
    ]
    for copy in outs:
        copy.start()
    own_part(flags_ref, flow_ref, part_ref, lower_ref, upper_ref)
    for copy in large[2]:
        copy.wait()
    add_load(part_ref, load_ref, die)

    for x in range(OX + 1):
        for c in range(3):
            up_ref[up_rows(x, c)] = part_ref[c, x, 13:17]
            down_ref[down_rows(x, c)] = part_ref[c, x, 0:3]
    outs += [
        pltpu.make_async_copy(up_ref, up_hbm, out_sem.at[2]),
        pltpu.make_async_copy(down_ref, down_hbm, out_sem.at[3]),
    ]
    for copy in outs[2:]:
        copy.start()
    for c in range(3):
        for i in range(4):
            right_ref[42 + 4 * c + i] = part_ref[c, 6 + i, 0:16]
            right_ref[54, 4 * c + i : 4 * c + i + 1] = part_ref[c, 6 + i, 16:17]
        for i in range(3):
            left_ref[28 + 3 * c + i] = part_ref[c, i, 0:16]
            left_ref[37, 3 * c + i : 3 * c + i + 1] = part_ref[c, i, 16:17]
    outs += [
        pltpu.make_async_copy(right_ref.at[42:55], right_hbm.at[42:55], out_sem.at[4]),
        pltpu.make_async_copy(left_ref.at[28:38], left_hbm.at[28:38], out_sem.at[5]),
    ]
    for copy in outs[4:]:
        copy.start()
    for copy in outs:
        copy.wait()


def three_steps(els_ref, basis, z_ref, lower_ref, upper_ref):
    at_first_x, at_last_x, at_first_y, at_last_y = place()
    lane = lanes()
    first_lane, last_lane = lane == 0, lane == DZ - 1
    rows = lax.broadcasted_iota(jnp.int32, (8, DZ), 0)
    keep_upper = jnp.logical_or(rows >= HALO, jnp.logical_not(at_first_y))
    keep_node = jnp.logical_or(rows < HALO, jnp.logical_not(at_last_y))
    zero = jnp.zeros((8, DZ), F32)

    def clear(x, _):
        for m in range(6):
            z_ref[m, x, 24:32] = zero
            upper_ref[m, x, 0:8] = zero
        return 0

    lax.fori_loop(0, WX, clear, 0)

    def first(x, _):
        for row in (0, 8, 16):
            for c in range(3):
                z_ref[2 * c, x, row : row + 8], z_ref[2 * c + 1, x, row : row + 8] = z_pair(
                    basis[0][c, x, row : row + 8], first_lane
                )
        return 0

    lax.fori_loop(0, WX, first, 0, unroll=5)

    for step in range(1, HALO + 1):
        start, end = step - 1, WX - 1 - step
        scale = (2.0 if step == 1 else 4.0) / SPAN
        for row in (0, 8, 16):

            def plane(x):
                values = []
                for m in range(6):
                    low, high = z_ref[m, x, row : row + 8], z_ref[m, x, row + 1 : row + 9]
                    values += [high + low, high - low]
                return values

            def element(x, carry):
                before, behind = carry
                after = plane(x + 1)
                p, q = before, after
                modes = (
                    [q[4 * c] - p[4 * c] for c in range(3)],
                    [q[4 * c + 1] + p[4 * c + 1] for c in range(3)],
                    [q[4 * c + 2] + p[4 * c + 2] for c in range(3)],
                    [q[4 * c + 1] - p[4 * c + 1] for c in range(3)],
                    [q[4 * c + 2] - p[4 * c + 2] for c in range(3)],
                    [q[4 * c + 3] + p[4 * c + 3] for c in range(3)],
                    [q[4 * c + 3] - p[4 * c + 3] for c in range(3)],
                )
                here = [els_ref[f, x, row : row + 8] for f in range(NEL + 1) if f != CONTACT_AT]
                n = (here[8], here[9], here[13], here[10], here[11], here[12])
                node, ahead = scatter_x(element_core(modes, n, here[:8]), behind)
                store_y(node, lower_ref, upper_ref, x, row, keep_upper if row == 0 else None)
                return after, ahead

            carry = (plane(start), [zero] * 12)
            for x in range(start, HALO):
                carry = element(x, carry)
            carry = (carry[0], [jnp.where(at_first_x, 0.0, value) for value in carry[1]])
            first_pair = HALO + (end + 1 - HALO) % 2
            if first_pair > HALO:
                carry = element(HALO, carry)

            def pair(k, carry):
                x = first_pair + 2 * k
                return element(x + 1, element(x, carry))

            lax.fori_loop(0, (end + 1 - first_pair) // 2, pair, carry)

        for x in range(step, end + 1):
            for row in (0, 8, 16) if step < HALO else (HALO, HALO + 8):
                for c in range(3):
                    here = basis[step - 1][c, x, row : row + 8]
                    value = merge_yz(lower_ref, upper_ref, c, x, row, last_lane) * (scale / 16.0)
                    if c == 2:
                        value = value + (els_ref[CONTACT_AT, x, row : row + 8] * scale) * here
                    if step == 1:
                        value = value - here
                    else:
                        value = value - (here + here) - basis[step - 2][c, x, row : row + 8]
                    if x >= HALO + OX:
                        value = jnp.where(at_last_x, 0.0, value)
                    if row == 16:
                        value = jnp.where(keep_node, value, 0.0)
                    basis[step][c, x, row : row + 8] = value
                    if step < HALO:
                        z_ref[2 * c, x, row : row + 8], z_ref[2 * c + 1, x, row : row + 8] = z_pair(value, first_lane)


def sum_rows(values):
    return jnp.sum(values, axis=0, keepdims=True)


def first_kernel(flags_ref, flow_ref, contact_ref, part_ref, left_ref, right_ref, up_ref, down_ref, cl_ref, cr_ref,
                 els_ref, own_ref, dots_ref, right_out, left_out, first_out, second_out,
                 b0, b1, b2, b3, z_ref, lower_ref, upper_ref):
    at_first_x, at_last_x, at_first_y, at_last_y = place()
    has_l, has_r, has_u = ask(at_first_x), ask(at_last_x), ask(at_last_y)
    zero = jnp.zeros((8, DZ), F32)
    low, high = slice(0, 3), slice(19, 21)
    mid = slice(HALO, HALO + OY)

    def clear(x, _):
        for f in range(NEL):
            els_ref[f, x, 16:24] = zero
        return 0

    lax.fori_loop(0, WE, clear, 0)

    def clear_start(x, _):
        for c in range(3):
            for row in (0, 8, 16):
                b0[c, x, row : row + 8] = zero
        return 0

    lax.fori_loop(0, WX, clear_start, 0)

    def own(x, _):
        w = x + HALO
        for f in range(NEL):
            if f < 8:
                value = flags_ref[f, x].astype(F32) * (-PLASTIC_GAIN / 8.0)
            elif f < CONTACT_AT:
                value = flow_ref[FLOW_SENT[f - 8], x]
            else:
                value = contact_ref[x]
            els_ref[f, w, mid] = value
        for c in range(3):
            b0[c, w, mid] = part_ref[c, x, 0:16]
            b0[c, w, 19:20] = part_ref[c, x, 16:17] * has_u
        return 0

    lax.fori_loop(0, OX, own, 0)
    for x in range(OX):
        for f in range(NEL):
            els_ref[f, x + HALO, low] = up_ref[UP_AT[x] + 3 * f : UP_AT[x] + 3 * f + 3]
            els_ref[f, x + HALO, high] = down_ref[DOWN_AT[x] + 2 * f : DOWN_AT[x] + 2 * f + 2]
    for c in range(3):
        b0[c, 12, mid] = part_ref[c, OX, 0:16] * has_r
        b0[c, 12, 19:20] = part_ref[c, OX, 16:17] * (has_r * has_u)
    for i in range(3):
        for f in range(NEL):
            els_ref[f, i, mid] = left_ref[3 * f + i]
            els_ref[f, i, low] = cl_ref[UP_AT[i] + 3 * f : UP_AT[i] + 3 * f + 3]
            els_ref[f, i, high] = cl_ref[176 + DOWN_AT[i] + 2 * f : 176 + DOWN_AT[i] + 2 * f + 2]
    for i in range(2):
        for f in range(NEL):
            els_ref[f, 12 + i, mid] = right_ref[2 * f + i]
            els_ref[f, 12 + i, low] = cr_ref[UP_AT[i] + 3 * f : UP_AT[i] + 3 * f + 3]
            els_ref[f, 12 + i, high] = cr_ref[168 + DOWN_AT[i] + 2 * f : 168 + DOWN_AT[i] + 2 * f + 2]

    def zz(x, _):
        for row in (0, 8, 16):
            els_ref[ZZ_AT, x, row : row + 8] = -(els_ref[8, x, row : row + 8] + els_ref[9, x, row : row + 8])
        return 0

    lax.fori_loop(0, WE, zz, 0)

    def from_below(piece):
        return jnp.where(at_first_y, 0.0, piece)

    for c in range(3):
        for i in range(4):
            b0[c, i, mid] += left_ref[42 + 4 * c + i] * has_l
            b0[c, i, 19:20] += left_ref[54, 4 * c + i : 4 * c + i + 1] * (has_l * has_u)
            b0[c, i, 0:4] += from_below(cl_ref[moved(up_rows(6 + i, c), UP_HIGH.start)]) * has_l
            b0[c, i, 19:22] += cl_ref[moved(down_rows(6 + i, c), DOWN_HIGH.start - 176)] * (has_l * has_u)
        for i in range(3):
            b0[c, 12 + i, mid] += right_ref[28 + 3 * c + i] * has_r
            b0[c, 12 + i, 19:20] += right_ref[37, 3 * c + i : 3 * c + i + 1] * (has_r * has_u)
            b0[c, 12 + i, 0:4] += from_below(cr_ref[up_rows(i, c)]) * has_r
            b0[c, 12 + i, 19:22] += cr_ref[moved(down_rows(i, c), -168)] * (has_r * has_u)

    for x in range(OX + 1):
        inside = has_r if x == OX else 1.0
        for c in range(3):
            b0[c, x + HALO, 0:4] += from_below(up_ref[up_rows(x, c)]) * inside
            b0[c, x + HALO, 19:22] += down_ref[down_rows(x, c)] * (inside * has_u)

    basis = (b0, b1, b2, b3)
    three_steps(els_ref, basis, z_ref, lower_ref, upper_ref)

    def collect(x, sums):
        sums = list(sums)
        for row in (0, 8):
            for c in range(3):
                v = [b[c, x + HALO, row + HALO : row + HALO + 8] for b in basis]
                for k in range(4):
                    own_ref[k, c, x, row : row + 8] = v[k]
                for k in range(7):
                    sums[k] = sums[k] + v[k // 2] * v[k - k // 2]
        return tuple(sums)

    sums = lax.fori_loop(0, OX, collect, (zero,) * 7, unroll=3)
    dots_ref[...] = zero
    for k in range(7):
        dots_ref[k : k + 1] = sum_rows(sums[k])

    def edge_rows(c, x):
        last, start, goes_up = b3[c, x, 16:19], b3[c, x, 3:6], odd() == 0
        return jnp.where(goes_up, last, start), jnp.where(goes_up, start, last)

    for i in range(3):
        for c in range(3):
            for out, x in ((right_out, 9 + i), (left_out, 3 + i)):
                out[16 * (3 * c + i) : 16 * (3 * c + i) + 16] = b3[c, x, mid]
                first, second = edge_rows(c, x)
                at = 9 * i + 3 * c
                out[144 + at : 147 + at] = second
                out[176 + at : 179 + at] = first
    for x in range(OX):
        for c in range(3):
            first, second = edge_rows(c, x + HALO)
            at = 9 * x + 3 * c
            first_out[at : at + 3] = first
            second_out[at : at + 3] = second


def second_kernel(els_ref, own_ref, dots_ref, left_ref, right_ref, first_ref, second_ref,
                  tail_ref, row_ref, b0, b1, b2, b3, z_ref, lower_ref, upper_ref):
    _, at_last_x, _, at_last_y = place()
    has_r, has_u = ask(at_last_x), ask(at_last_y)
    below = odd()
    zero = jnp.zeros((8, DZ), F32)
    mid = slice(HALO, HALO + OY)

    def own(x, _):
        for c in range(3):
            b0[c, x + HALO, mid] = own_ref[3, c, x]
        return 0

    for x in range(WX):
        inside = has_r if x >= HALO + OX else 1.0
        for c in range(3):
            b0[c, x, 16:24] = zero
            at = 88 + 9 * x if x < HALO else 9 * (x - HALO) if x < HALO + OX else 120 + 9 * (x - HALO - OX)
            rows = slice(at + 3 * c, at + 3 * c + 3)
            one, two = first_ref[rows] * inside, second_ref[rows] * inside
            b0[c, x, 0:3] = jnp.where(below == 0, one, two)
            b0[c, x, 19:22] = jnp.where(below == 0, two, one) * has_u
    lax.fori_loop(0, OX, own, 0)
    for c in range(3):
        for i in range(3):
            block = slice(16 * (3 * c + i), 16 * (3 * c + i) + 16)
            b0[c, i, mid] = left_ref[block]
            b0[c, 12 + i, mid] = right_ref[block] * has_r

    basis = (b0, b1, b2, b3)
    three_steps(els_ref, basis, z_ref, lower_ref, upper_ref)

    def collect(x, sums):
        sums = list(sums)
        for row in (0, 8):
            for c in range(3):
                v = [own_ref[3, c, x, row : row + 8]]
                for k in range(1, 4):
                    w = b_at(basis[k], c, x, row)
                    v.append((w + w) - own_ref[3 - k, c, x, row : row + 8])
                    tail_ref[k - 1, c, x, row : row + 8] = v[k]
                for k in range(1, 6):
                    sums[k - 1] = sums[k - 1] + v[k // 2] * v[k - k // 2]
        return tuple(sums)

    sums = lax.fori_loop(0, OX, collect, (zero,) * 5, unroll=3)
    lane = lax.broadcasted_iota(jnp.int32, (1, DZ), 1)
    line = jnp.zeros((1, DZ), F32)
    for k in range(12):
        dot = dots_ref[k : k + 1] if k < 7 else sum_rows(sums[k - 7])
        line = jnp.where(lane == k, jnp.sum(dot, axis=1, keepdims=True), line)
    row_ref[...] = jnp.broadcast_to(line, row_ref.shape)


def b_at(ref, c, x, row):
    return ref[c, x + HALO, row + HALO : row + HALO + 8]


def times_matrix(p):
    out = [None] * (len(p) + 1)

    def add(k, value):
        out[k] = value if out[k] is None else out[k] + value

    for k, value in enumerate(p):
        add(k, value * (SPAN / 2))
        if k == 0:
            add(1, value * (SPAN / 2))
        else:
            add(k + 1, value * (SPAN / 4))
            add(k - 1, value * (SPAN / 4))
    return out


def tree_sum(values):
    while len(values) > 1:
        values = [a + b for a, b in zip(values[::2], values[1::2])] + ([values[-1]] if len(values) % 2 else [])
    return values[0]


def combine(p, a, q):
    out = []
    for k in range(max(len(p), len(q))):
        term = a * q[k] if k < len(q) else None
        if k < len(p):
            term = p[k] if term is None else p[k] + term
        out.append(term)
    return out


def coefficients(mu):
    gram = [[0.5 * (mu[i + j] + mu[abs(i - j)]) if i + j < len(mu) else None for j in range(7)] for i in range(7)]

    def inner(p, q):
        return tree_sum([p[i] * tree_sum([gram[i][j] * q[j] for j in range(len(q))]) for i in range(len(p))])

    remain = [jnp.ones_like(mu[0])]
    total = []
    for newton in range(NEWTON):
        direction = remain
        norm = inner(remain, remain)
        for step in range(CG_STEPS):
            image = times_matrix(direction)
            alpha = norm / inner(direction, image)
            total = combine(total, alpha, direction)
            remain = combine(remain, -alpha, image)
            if step + 1 < CG_STEPS:
                norm_next = inner(remain, remain)
                direction = combine(remain, norm_next / norm, direction)
                norm = norm_next
    return total, remain


def last_kernel(dots_ref, own_ref, tail_ref, displacement_hbm, residual_hbm, displacement_ref, residual_ref, sems):
    sums = jnp.sum(dots_ref[...], axis=0, keepdims=True)
    dots = [jnp.broadcast_to(sums[:, k : k + 1], (1, DZ)) for k in range(12)]
    mu = dots[:2]
    for k in range(2, 12):
        mu.append((dots[k] + dots[k]) - mu[k % 2])
    total, remain = coefficients(mu)
    total = [jnp.broadcast_to(value, (8, DZ)) for value in total]
    remain = [jnp.broadcast_to(value, (8, DZ)) for value in remain]
    copies = []
    for c in range(3):

        def write(x, _):
            for row in (0, 8):
                v = [own_ref[k, c, x, row : row + 8] for k in range(4)]
                v += [tail_ref[k, c, x, row : row + 8] for k in range(3)]
                displacement_ref[c, x, row : row + 8] = tree_sum([a * b for a, b in zip(total, v)])
                residual_ref[c, x, row : row + 8] = tree_sum([a * b for a, b in zip(remain, v)])
            return 0

        lax.fori_loop(0, OX, write, 0, unroll=3)
        for m, (source, target) in enumerate(((displacement_ref, displacement_hbm), (residual_ref, residual_hbm))):
            copies.append(pltpu.make_async_copy(source.at[c], target.at[c], sems.at[m, c]))
            copies[-1].start()
    for copy in copies:
        copy.wait()


def shape(*dims):
    return jax.ShapeDtypeStruct(dims, F32)


def call(kernel, outs, scratch=(), mebibytes=24, **more):
    return pl.pallas_call(
        kernel,
        out_shape=outs,
        scratch_shapes=[pltpu.VMEM(dims, F32) if isinstance(dims, tuple) else dims for dims in scratch],
        compiler_params=pltpu.CompilerParams(vmem_limit_bytes=mebibytes * 1024 * 1024),
        **more,
    )


STEP_SCRATCH = [(3, WX, WY, DZ)] * 4 + [(6, WX, WY + 8, DZ)] * 3


def rotate(value, axis, steps):
    count = lax.axis_size(axis)
    return lax.ppermute(value, axis, [(i, (i + steps) % count) for i in range(count)])


def wind(value, forward):
    count_x, count_y = lax.axis_size("gx"), lax.axis_size("gy")
    pairs = []
    for x in range(count_x):
        for y in range(count_y):
            ahead = y + 1 if (x % 2 == 0) == forward else y - 1
            goal = (x, ahead) if 0 <= ahead < count_y else (x ^ 1, y)
            pairs.append((x * count_y + y, goal[0] * count_y + goal[1]))
    return lax.ppermute(value, ("gx", "gy"), pairs)


def exchange(right, left, up, down):
    from_left = rotate(right, "gx", 1)
    from_right = rotate(left, "gx", -1)
    from_below = rotate(up, "gy", 1)
    from_above = rotate(down, "gy", -1)
    corner_left = rotate(jnp.concatenate([from_below[UP_HIGH], from_above[DOWN_HIGH]]), "gx", 1)
    corner_right = rotate(jnp.concatenate([from_below[UP_LOW], from_above[DOWN_LOW]]), "gx", -1)
    return from_left, from_right, from_below, from_above, corner_left, corner_right


def exchange_in_turn(right, left, first, second):
    from_left = rotate(right, "gx", 1)
    from_right = rotate(left, "gx", -1)
    first = jnp.concatenate([first, from_left[144:176], from_right[144:176]], axis=0)
    second = jnp.concatenate([second, from_left[176:208], from_right[176:208]], axis=0)
    return from_left, from_right, wind(first, True), wind(second, False)


def body(load, plastic_flags, flow_dir, contact_flags, die_depth):
    slabs = [(55, OY, DZ), (38, OY, DZ), (UP_ROWS, DZ), (DOWN_ROWS, DZ)]
    work = [(6, OX + 1, WY + 8, DZ)] * 2
    outside = pl.BlockSpec(memory_space=pl.ANY)
    inputs = (load, plastic_flags, flow_dir, contact_flags, die_depth)
    right, left, up, down = call(
        slab_kernel,
        [shape(*dims) for dims in slabs],
        slabs + [(3, OX + 1, WY, DZ), (OX, OY, DZ)] + work
        + [(3, OX, OY, DZ), pltpu.VMEM((8, OX, OY, DZ), jnp.int32), (6, OX, OY, DZ),
           pltpu.VMEM((OX, OY), jnp.int32), (OX, OY)]
        + [pltpu.SemaphoreType.DMA((count,)) for count in (3, 8, 6, 2, 6)],
        mebibytes=54,
        in_specs=[outside] * 5,
        out_specs=[outside] * 4,
    )(*inputs)
    part, contact = call(
        part_kernel, [shape(3, OX + 1, WY, DZ), shape(OX, OY, DZ)], work,
        cost_estimate=pl.CostEstimate(flops=400000, bytes_accessed=1000, transcendentals=0),
    )(*inputs)
    halos = exchange(right, left, up, down)
    els, own, dots, right, left, first, second = call(
        first_kernel,
        [shape(NEL + 1, WE, WY, DZ), shape(4, 3, OX, OY, DZ), shape(8, DZ), shape(208, DZ), shape(208, DZ), shape(88, DZ), shape(88, DZ)],
        STEP_SCRATCH,
    )(plastic_flags, flow_dir, contact, part, *halos)
    halos = exchange_in_turn(right, left, first, second)
    count = lax.axis_size("gx") * lax.axis_size("gy")
    tail, line = call(
        second_kernel, [shape(3, 3, OX, OY, DZ), shape(count, DZ)], STEP_SCRATCH
    )(els, own, dots, *halos)
    lines = lax.all_to_all(line, ("gx", "gy"), 0, 0, tiled=True)
    return tuple(
        call(
            last_kernel,
            [shape(3, OX, OY, DZ)] * 2,
            [(3, OX, OY, DZ)] * 2 + [pltpu.SemaphoreType.DMA((2, 3))],
            out_specs=[outside] * 2,
        )(lines, own, tail)
    )


def solution(mesh):
    in_specs = (
        P(None, "gx", "gy", None),
        P(None, "gx", "gy", None),
        P(None, "gx", "gy", None),
        P("gx", "gy"),
        P("gx", "gy"),
    )
    out_specs = (P(None, "gx", "gy", None), P(None, "gx", "gy", None))
    return jax.shard_map(body, mesh=mesh, in_specs=in_specs, out_specs=out_specs, check_vma=False)
```

```python
import math

import jax
import jax.numpy as jnp
from jax import lax
from jax.experimental import pallas as pl
from jax.experimental.pallas import tpu as pltpu
from jax.sharding import PartitionSpec as P

PLASTIC_GAIN = 6.0 / 3.1
YIELD_OFFSET = 0.05
CONTACT_STIFF = 4.0
CG_STEPS = 3
NEWTON = 2
ROOT_THIRD = 1.0 / math.sqrt(3.0)
THIRD = 1.0 / 3.0
SPAN = 10.0

HALO = 3
OX, OY, DZ = 9, 16, 128
WX = OX + 2 * HALO
WE = WX - 1
WY = 24
F32 = jnp.float32

FLOW_SENT = (0, 1, 3, 4, 5)
NEL = 14
CONTACT_AT = 13
ZZ_AT = 14
FOLD = 6
FOLDED = -1


UP_AT = (0, 54, 108, 168, 222, 276, 336, 390, 444, 498)
DOWN_AT = (0, 37, 74, 112, 149, 186, 224, 261, 298, 335)
UP_ROWS, DOWN_ROWS = 512, 344
UP_LOW, UP_HIGH = slice(0, 168), slice(336, 512)
DOWN_LOW, DOWN_HIGH = slice(0, 112), slice(224, 344)


def up_rows(x, c):
    at = UP_AT[x] + (42 if x < OX else 0) + 4 * c
    return slice(at, at + 4)


def down_rows(x, c):
    at = DOWN_AT[x] + (28 if x < OX else 0) + 3 * c
    return slice(at, at + 3)


def moved(rows, by):
    return slice(rows.start - by, rows.stop - by)


def lanes():
    return lax.broadcasted_iota(jnp.int32, (8, DZ), 1)


def z_pair(value, first_lane):
    low = jnp.where(first_lane, 0.0, pltpu.roll(value, 1, 1))
    return value + low, value - low


def z_merge(total, slope, last_lane):
    return total + slope + jnp.where(last_lane, 0.0, pltpu.roll(total - slope, DZ - 1, 1))


def to_points(s1, sx, sy, sz, syz, sxz, sxy):
    points = []
    for sign_x in (-1, 1):
        a0 = s1 + sx if sign_x > 0 else s1 - sx
        ay = sy + sxy if sign_x > 0 else sy - sxy
        az = sz + sxz if sign_x > 0 else sz - sxz
        for sign_y in (-1, 1):
            b0 = a0 + ay if sign_y > 0 else a0 - ay
            bz = az + syz if sign_y > 0 else az - syz
            points += [b0 - bz, b0 + bz]
    return points


def from_points(t):
    per_x = []
    for i in range(2):
        e0 = [t[4 * i + 2 * j + 1] + t[4 * i + 2 * j] for j in range(2)]
        ez = [t[4 * i + 2 * j + 1] - t[4 * i + 2 * j] for j in range(2)]
        per_x.append((e0[1] + e0[0], e0[1] - e0[0], ez[1] + ez[0], ez[1] - ez[0]))
    low, high = per_x
    t1, ty, tz, tyz = (high[m] + low[m] for m in range(4))
    tx, txy, txz = (high[m] - low[m] for m in range(3))
    return t1, tx, ty, tz, tyz, txz, txy


def plastic_forces(n, t):
    nxx, nyy, nzz, nxy, nyz, nzx = n
    t1, tx, ty, tz, tyz, txz, txy = t
    tx, ty, tz = tx * ROOT_THIRD, ty * ROOT_THIRD, tz * ROOT_THIRD
    tyz, txz, txy = tyz * THIRD, txz * THIRD, txy * THIRD
    a_xy, a_yz, a_zx = nxy * t1, nyz * t1, nzx * t1
    fx = [nxx * t1, a_xy, a_zx]
    fy = [a_xy, nyy * t1, a_yz]
    fz = [a_zx, a_yz, nzz * t1]
    xy_z, yz_x, zx_y = nxy * tz, nyz * tx, nzx * ty
    fxy = [nxx * ty + nxy * tx, nxy * ty + nyy * tx, zx_y + yz_x]
    fxz = [nxx * tz + nzx * tx, xy_z + yz_x, nzx * tz + nzz * tx]
    fyz = [xy_z + zx_y, nyy * tz + nyz * ty, nyz * tz + nzz * ty]
    fxyz = [
        nxx * tyz + nxy * txz + nzx * txy,
        nxy * tyz + nyy * txz + nyz * txy,
        nzx * tyz + nyz * txz + nzz * txy,
    ]
    return fx, fy, fz, fxy, fxz, fyz, fxyz


def element_core(modes, n, flags):
    ax, ay, az, axy, axz, ayz, axyz = modes
    nxx, nyy, nzz, nxy, nyz, nzx = n
    sh_xy, sh_yz, sh_zx = ax[1] + ay[0], ay[2] + az[1], az[0] + ax[2]
    k_x, k_y, k_z = axy[2] + axz[1], axy[2] + ayz[0], axz[1] + ayz[0]
    s1 = (nxx * ax[0] + nyy * ay[1] + nzz * az[2]) + (nxy * sh_xy + nyz * sh_yz + nzx * sh_zx)
    sx = (nxy * axy[0] + nyy * axy[1]) + (nyz * k_x + nzx * axz[0] + nzz * axz[2])
    sy = (nxx * axy[0] + nxy * axy[1]) + (nzx * k_y + nyz * ayz[1] + nzz * ayz[2])
    sz = (nxx * axz[0] + nxy * k_z) + (nzx * axz[2] + nyy * ayz[1] + nyz * ayz[2])
    syz = nxx * axyz[0] + nxy * axyz[1] + nzx * axyz[2]
    sxz = nxy * axyz[0] + nyy * axyz[1] + nyz * axyz[2]
    sxy = nzx * axyz[0] + nyz * axyz[1] + nzz * axyz[2]
    values = to_points(
        s1, sx * ROOT_THIRD, sy * ROOT_THIRD, sz * ROOT_THIRD, syz * THIRD, sxz * THIRD, sxy * THIRD
    )
    plastic = plastic_forces(n, from_points([value * flag for value, flag in zip(values, flags)]))
    trace = ax[0] + ay[1] + az[2]
    tr_x, tr_y, tr_z = (
        (axy[1] + axz[2]) * THIRD,
        (axy[0] + ayz[2]) * THIRD,
        (axz[0] + ayz[1]) * THIRD,
    )
    mixed = (k_x + ayz[0]) * THIRD
    elastic = (
        [trace + (ax[0] + ax[0]), sh_xy, sh_zx],
        [sh_xy, trace + (ay[1] + ay[1]), sh_yz],
        [sh_zx, sh_yz, trace + (az[2] + az[2])],
        [tr_y + axy[0], tr_x + axy[1], mixed + axy[2] * THIRD],
        [tr_z + axz[0], mixed + axz[1] * THIRD, tr_x + axz[2]],
        [mixed + ayz[0] * THIRD, tr_z + ayz[1], tr_y + ayz[2]],
        [axyz[c] * (5.0 / 9.0) for c in range(3)],
    )
    return [[elastic[m][c] + plastic[m][c] for c in range(3)] for m in range(7)]


def scatter_x(forces, behind):
    fx, fy, fz, fxy, fxz, fyz, fxyz = forces
    node, ahead = [], []
    for c in range(3):
        node += [
            behind[4 * c] - fx[c],
            behind[4 * c + 1] + (fy[c] - fxy[c]),
            behind[4 * c + 2] + (fz[c] - fxz[c]),
            behind[4 * c + 3] + (fyz[c] - fxyz[c]),
        ]
        ahead += [fx[c], fy[c] + fxy[c], fz[c] + fxz[c], fyz[c] + fxyz[c]]
    return node, ahead


def store_y(node, lower_ref, upper_ref, x, row, upper_keep=None):
    for c in range(3):
        ss, sd, ds, dd = node[4 * c : 4 * c + 4]
        lower_ref[2 * c, x, row : row + 8] = ss - sd
        lower_ref[2 * c + 1, x, row : row + 8] = ds - dd
        up_s, up_d = ss + sd, ds + dd
        if upper_keep is not None:
            up_s, up_d = jnp.where(upper_keep, up_s, 0.0), jnp.where(upper_keep, up_d, 0.0)
        upper_ref[2 * c, x, row + 8 : row + 16] = up_s
        upper_ref[2 * c + 1, x, row + 8 : row + 16] = up_d


def merge_yz(lower_ref, upper_ref, c, x, row, last_lane):
    total = lower_ref[2 * c, x, row : row + 8] + upper_ref[2 * c, x, row + 7 : row + 15]
    slope = lower_ref[2 * c + 1, x, row : row + 8] + upper_ref[2 * c + 1, x, row + 7 : row + 15]
    return z_merge(total, slope, last_lane)


def place():
    index_x, index_y = lax.axis_index("gx"), lax.axis_index("gy")
    return (
        index_x == 0,
        index_x == lax.axis_size("gx") - 1,
        index_y == 0,
        index_y == lax.axis_size("gy") - 1,
    )


def odd():
    return lax.rem(lax.axis_index("gx"), 2)


def ask(flag):
    return jnp.where(flag, 0.0, 1.0).astype(F32)


def top_fields(active_ref, die_ref):
    last = lax.broadcasted_iota(jnp.int32, (OY, DZ), 1) == DZ - 1
    same = lax.broadcasted_iota(jnp.int32, (OY, OY), 0) == lax.broadcasted_iota(jnp.int32, (OY, OY), 1)

    def on_rows(row):
        turned = jnp.sum(jnp.where(same, jnp.broadcast_to(row, (OY, OY)), 0.0), axis=1, keepdims=True)
        return jnp.where(last, turned, 0.0)

    contact, die = [], []
    for x in range(OX):
        stiff = CONTACT_STIFF * active_ref[x : x + 1].astype(F32)
        contact.append(on_rows(stiff))
        die.append(on_rows(stiff * die_ref[x : x + 1]))
    return contact, die


def own_part(flags_ref, flow_ref, part_ref, lower_ref, upper_ref):
    last_lane = lanes() == DZ - 1
    zero = jnp.zeros((8, DZ), F32)

    def clear(x, _):
        for m in range(6):
            lower_ref[m, x, 16:24] = zero
            upper_ref[m, x, 0:8] = zero
        return 0

    lax.fori_loop(0, OX + 1, clear, 0)
    for row in (0, 8):

        def element(x, behind):
            flags = [flags_ref[q, x, row : row + 8].astype(F32) * (0.5 * PLASTIC_GAIN * YIELD_OFFSET) for q in range(8)]
            n = [flow_ref[m, x, row : row + 8] for m in range(6)]
            node, ahead = scatter_x(plastic_forces(n, from_points(flags)), behind)
            store_y(node, lower_ref, upper_ref, x, row)
            return ahead

        behind = lax.fori_loop(0, OX, element, [zero] * 12, unroll=3)
        store_y(behind, lower_ref, upper_ref, OX, row)
    for x in range(OX + 1):
        for c in range(3):
            for row in (0, 8, 16):
                part_ref[c, x, row : row + 8] = merge_yz(lower_ref, upper_ref, c, x, row, last_lane) * (-1.0 / 16.0)


def add_load(part_ref, load_ref, die):
    for x in range(OX):
        for c in range(3):
            value = part_ref[c, x, 0:OY] + load_ref[c, x]
            part_ref[c, x, 0:OY] = value + die[x] if c == 2 else value


def part_kernel(load_ref, flags_ref, flow_ref, active_ref, die_ref, part_ref, contact_ref, lower_ref, upper_ref):
    contact, die = top_fields(active_ref, die_ref)
    for x in range(OX):
        contact_ref[x] = contact[x]
    own_part(flags_ref, flow_ref, part_ref, lower_ref, upper_ref)
    add_load(part_ref, load_ref, die)


def slab_kernel(load_hbm, flags_hbm, flow_hbm, active_hbm, die_hbm, right_hbm, left_hbm, up_hbm, down_hbm,
                right_ref, left_ref, up_ref, down_ref, part_ref, contact_ref, lower_ref, upper_ref,
                load_ref, flags_ref, flow_ref, active_ref, die_ref, load_sem, flags_sem, flow_sem, top_sem, out_sem):
    small = [
        pltpu.make_async_copy(active_hbm, active_ref, top_sem.at[0]),
        pltpu.make_async_copy(die_hbm, die_ref, top_sem.at[1]),
    ]
    large = [
        [pltpu.make_async_copy(source.at[m : m + step], target.at[m : m + step], sem.at[m])
         for m in range(0, source.shape[0], step)]
        for source, target, sem, step in (
            (flags_hbm, flags_ref, flags_sem, 4), (flow_hbm, flow_ref, flow_sem, 3), (load_hbm, load_ref, load_sem, 3))
    ]
    for group in (small, *large):
        for copy in group:
            copy.start()
    for copy in small:
        copy.wait()
    contact, die = top_fields(active_ref, die_ref)
    for x in range(OX):
        contact_ref[x] = contact[x]

    def field(f, x, rows):
        if f < 8:
            return flags_ref[f, x, rows].astype(F32) * (-PLASTIC_GAIN / 8.0)
        if f < CONTACT_AT:
            return flow_ref[FLOW_SENT[f - 8], x, rows]
        return contact_ref[x, rows]

    whole = slice(0, OY)
    arrived = {0: large[0][0], 4: large[0][1], 8: large[1][0], 10: large[1][1]}
    for f in range(NEL):
        if f in arrived:
            arrived[f].wait()
        for i in range(3):
            right_ref[3 * f + i] = field(f, 6 + i, whole)
        for i in range(2):
            left_ref[2 * f + i] = field(f, i, whole)
        for x in range(OX):
            up_ref[UP_AT[x] + 3 * f : UP_AT[x] + 3 * f + 3] = field(f, x, slice(13, 16))
            down_ref[DOWN_AT[x] + 2 * f : DOWN_AT[x] + 2 * f + 2] = field(f, x, slice(0, 2))
    outs = [
        pltpu.make_async_copy(right_ref.at[0:42], right_hbm.at[0:42], out_sem.at[0]),
        pltpu.make_async_copy(left_ref.at[0:28], left_hbm.at[0:28], out_sem.at[1]),
    ]
    for copy in outs:
        copy.start()
    own_part(flags_ref, flow_ref, part_ref, lower_ref, upper_ref)
    for copy in large[2]:
        copy.wait()
    add_load(part_ref, load_ref, die)

    for x in range(OX + 1):
        for c in range(3):
            up_ref[up_rows(x, c)] = part_ref[c, x, 13:17]
            down_ref[down_rows(x, c)] = part_ref[c, x, 0:3]
    outs += [
        pltpu.make_async_copy(up_ref, up_hbm, out_sem.at[2]),
        pltpu.make_async_copy(down_ref, down_hbm, out_sem.at[3]),
    ]
    for copy in outs[2:]:
        copy.start()
    for c in range(3):
        for i in range(4):
            right_ref[42 + 4 * c + i] = part_ref[c, 6 + i, 0:16]
            right_ref[54, 4 * c + i : 4 * c + i + 1] = part_ref[c, 6 + i, 16:17]
        for i in range(3):
            left_ref[28 + 3 * c + i] = part_ref[c, i, 0:16]
            left_ref[37, 3 * c + i : 3 * c + i + 1] = part_ref[c, i, 16:17]
    outs += [
        pltpu.make_async_copy(right_ref.at[42:55], right_hbm.at[42:55], out_sem.at[4]),
        pltpu.make_async_copy(left_ref.at[28:38], left_hbm.at[28:38], out_sem.at[5]),
    ]
    for copy in outs[4:]:
        copy.start()
    for copy in outs:
        copy.wait()


def three_steps(els_ref, basis, z_ref, lower_ref, upper_ref):
    at_first_x, at_last_x, at_first_y, at_last_y = place()
    lane = lanes()
    first_lane, last_lane = lane == 0, lane == DZ - 1
    rows = lax.broadcasted_iota(jnp.int32, (8, DZ), 0)
    keep_upper = jnp.logical_or(rows >= HALO, jnp.logical_not(at_first_y))
    keep_node = jnp.logical_or(rows < HALO, jnp.logical_not(at_last_y))
    zero = jnp.zeros((8, DZ), F32)
    low_half = rows < 4

    def clear(x, _):
        for m in range(6):
            z_ref[m, x, 24:32] = zero
            upper_ref[m, x, 0:8] = zero
        return 0

    lax.fori_loop(0, WX, clear, 0)

    def first(x, _):
        for row in (0, 8, 16):
            for c in range(3):
                z_ref[2 * c, x, row : row + 8], z_ref[2 * c + 1, x, row : row + 8] = z_pair(
                    basis[0][c, x, row : row + 8], first_lane
                )
        return 0

    lax.fori_loop(0, WX, first, 0, unroll=5)

    for step in range(1, HALO + 1):
        start, end = step - 1, WX - 1 - step
        scale = (2.0 if step == 1 else 4.0) / SPAN
        for row in (0, 8, 16) if step == 1 else (FOLDED, 0, 8):

            def rows_of(ref, m, x, shift=0):
                if row != FOLDED:
                    return ref[m, x, row + shift : row + shift + 8]
                return jnp.where(
                    low_half, ref[m, x, 16 + shift : 24 + shift], ref[m, x + FOLD, 12 + shift : 20 + shift]
                )

            def plane(x):
                values = []
                for m in range(6):
                    low, high = rows_of(z_ref, m, x), rows_of(z_ref, m, x, 1)
                    values += [high + low, high - low]
                return values

            def element(x, carry):
                before, behind = carry
                after = plane(x + 1)
                p, q = before, after
                modes = (
                    [q[4 * c] - p[4 * c] for c in range(3)],
                    [q[4 * c + 1] + p[4 * c + 1] for c in range(3)],
                    [q[4 * c + 2] + p[4 * c + 2] for c in range(3)],
                    [q[4 * c + 1] - p[4 * c + 1] for c in range(3)],
                    [q[4 * c + 2] - p[4 * c + 2] for c in range(3)],
                    [q[4 * c + 3] + p[4 * c + 3] for c in range(3)],
                    [q[4 * c + 3] - p[4 * c + 3] for c in range(3)],
                )
                here = [rows_of(els_ref, f, x) for f in range(NEL + 1) if f != CONTACT_AT]
                n = (here[8], here[9], here[13], here[10], here[11], here[12])
                node, ahead = scatter_x(element_core(modes, n, here[:8]), behind)
                if row == FOLDED:
                    store_y(node, lower_ref, upper_ref, x, 16)
                    store_y(node, lower_ref, upper_ref, x + FOLD, 12)
                else:
                    store_y(node, lower_ref, upper_ref, x, row, keep_upper if row == 0 else None)
                return after, ahead

            first_x, last_x = (1, FOLD) if row == FOLDED else (start, end)
            gone = jnp.logical_and(at_first_x, low_half) if row == FOLDED else at_first_x
            carry = (plane(first_x), [zero] * 12)
            for x in range(first_x, HALO):
                carry = element(x, carry)
            carry = (carry[0], [jnp.where(gone, 0.0, value) for value in carry[1]])
            first_pair = HALO + (last_x + 1 - HALO) % 2
            if first_pair > HALO:
                carry = element(HALO, carry)

            def pair(k, carry):
                x = first_pair + 2 * k
                return element(x + 1, element(x, carry))

            carry = lax.fori_loop(0, (last_x + 1 - first_pair) // 2, pair, carry)
            if row == FOLDED:
                for c in range(3):
                    ss, sd, ds, dd = carry[1][4 * c : 4 * c + 4]
                    for m, value in ((2 * c, ss - sd), (2 * c + 1, ds - dd)):
                        lower_ref[m, FOLD + 1, 16:24] += jnp.where(low_half, value, 0.0)
                    for m, value in ((2 * c, ss + sd), (2 * c + 1, ds + dd)):
                        upper_ref[m, FOLD + 1, 24:32] += jnp.where(low_half, value, 0.0)

        for x in range(step, end + 1):
            for row in (0, 8, 16) if step < HALO else (HALO, HALO + 8):
                for c in range(3):
                    here = basis[step - 1][c, x, row : row + 8]
                    value = merge_yz(lower_ref, upper_ref, c, x, row, last_lane) * (scale / 16.0)
                    if c == 2:
                        value = value + (els_ref[CONTACT_AT, x, row : row + 8] * scale) * here
                    if step == 1:
                        value = value - here
                    else:
                        value = value - (here + here) - basis[step - 2][c, x, row : row + 8]
                    if x >= HALO + OX:
                        value = jnp.where(at_last_x, 0.0, value)
                    if row == 16:
                        value = jnp.where(keep_node, value, 0.0)
                    basis[step][c, x, row : row + 8] = value
                    if step < HALO:
                        z_ref[2 * c, x, row : row + 8], z_ref[2 * c + 1, x, row : row + 8] = z_pair(value, first_lane)


def sum_rows(values):
    return jnp.sum(values, axis=0, keepdims=True)


def first_kernel(flags_ref, flow_ref, contact_ref, part_ref, left_ref, right_ref, up_ref, down_ref, cl_ref, cr_ref,
                 els_ref, own_ref, dots_ref, right_out, left_out, first_out, second_out,
                 b0, b1, b2, b3, z_ref, lower_ref, upper_ref):
    at_first_x, at_last_x, at_first_y, at_last_y = place()
    has_l, has_r, has_u = ask(at_first_x), ask(at_last_x), ask(at_last_y)
    zero = jnp.zeros((8, DZ), F32)
    low, high = slice(0, 3), slice(19, 21)
    mid = slice(HALO, HALO + OY)

    def clear(x, _):
        for f in range(NEL):
            els_ref[f, x, 16:24] = zero
        return 0

    lax.fori_loop(0, WE, clear, 0)

    def clear_start(x, _):
        for c in range(3):
            for row in (0, 8, 16):
                b0[c, x, row : row + 8] = zero
        return 0

    lax.fori_loop(0, WX, clear_start, 0)

    def own(x, _):
        w = x + HALO
        for f in range(NEL):
            if f < 8:
                value = flags_ref[f, x].astype(F32) * (-PLASTIC_GAIN / 8.0)
            elif f < CONTACT_AT:
                value = flow_ref[FLOW_SENT[f - 8], x]
            else:
                value = contact_ref[x]
            els_ref[f, w, mid] = value
        for c in range(3):
            b0[c, w, mid] = part_ref[c, x, 0:16]
            b0[c, w, 19:20] = part_ref[c, x, 16:17] * has_u
        return 0

    lax.fori_loop(0, OX, own, 0)
    for x in range(OX):
        for f in range(NEL):
            els_ref[f, x + HALO, low] = up_ref[UP_AT[x] + 3 * f : UP_AT[x] + 3 * f + 3]
            els_ref[f, x + HALO, high] = down_ref[DOWN_AT[x] + 2 * f : DOWN_AT[x] + 2 * f + 2]
    for c in range(3):
        b0[c, 12, mid] = part_ref[c, OX, 0:16] * has_r
        b0[c, 12, 19:20] = part_ref[c, OX, 16:17] * (has_r * has_u)
    for i in range(3):
        for f in range(NEL):
            els_ref[f, i, mid] = left_ref[3 * f + i]
            els_ref[f, i, low] = cl_ref[UP_AT[i] + 3 * f : UP_AT[i] + 3 * f + 3]
            els_ref[f, i, high] = cl_ref[176 + DOWN_AT[i] + 2 * f : 176 + DOWN_AT[i] + 2 * f + 2]
    for i in range(2):
        for f in range(NEL):
            els_ref[f, 12 + i, mid] = right_ref[2 * f + i]
            els_ref[f, 12 + i, low] = cr_ref[UP_AT[i] + 3 * f : UP_AT[i] + 3 * f + 3]
            els_ref[f, 12 + i, high] = cr_ref[168 + DOWN_AT[i] + 2 * f : 168 + DOWN_AT[i] + 2 * f + 2]

    def zz(x, _):
        for row in (0, 8, 16):
            els_ref[ZZ_AT, x, row : row + 8] = -(els_ref[8, x, row : row + 8] + els_ref[9, x, row : row + 8])
        return 0

    lax.fori_loop(0, WE, zz, 0)

    def from_below(piece):
        return jnp.where(at_first_y, 0.0, piece)

    for c in range(3):
        for i in range(4):
            b0[c, i, mid] += left_ref[42 + 4 * c + i] * has_l
            b0[c, i, 19:20] += left_ref[54, 4 * c + i : 4 * c + i + 1] * (has_l * has_u)
            b0[c, i, 0:4] += from_below(cl_ref[moved(up_rows(6 + i, c), UP_HIGH.start)]) * has_l
            b0[c, i, 19:22] += cl_ref[moved(down_rows(6 + i, c), DOWN_HIGH.start - 176)] * (has_l * has_u)
        for i in range(3):
            b0[c, 12 + i, mid] += right_ref[28 + 3 * c + i] * has_r
            b0[c, 12 + i, 19:20] += right_ref[37, 3 * c + i : 3 * c + i + 1] * (has_r * has_u)
            b0[c, 12 + i, 0:4] += from_below(cr_ref[up_rows(i, c)]) * has_r
            b0[c, 12 + i, 19:22] += cr_ref[moved(down_rows(i, c), -168)] * (has_r * has_u)

    for x in range(OX + 1):
        inside = has_r if x == OX else 1.0
        for c in range(3):
            b0[c, x + HALO, 0:4] += from_below(up_ref[up_rows(x, c)]) * inside
            b0[c, x + HALO, 19:22] += down_ref[down_rows(x, c)] * (inside * has_u)

    basis = (b0, b1, b2, b3)
    three_steps(els_ref, basis, z_ref, lower_ref, upper_ref)

    def collect(x, sums):
        sums = list(sums)
        for row in (0, 8):
            for c in range(3):
                v = [b[c, x + HALO, row + HALO : row + HALO + 8] for b in basis]
                for k in range(4):
                    own_ref[k, c, x, row : row + 8] = v[k]
                for k in range(7):
                    sums[k] = sums[k] + v[k // 2] * v[k - k // 2]
        return tuple(sums)

    sums = lax.fori_loop(0, OX, collect, (zero,) * 7, unroll=3)
    dots_ref[...] = zero
    for k in range(7):
        dots_ref[k : k + 1] = sum_rows(sums[k])

    def edge_rows(c, x):
        last, start, goes_up = b3[c, x, 16:19], b3[c, x, 3:6], odd() == 0
        return jnp.where(goes_up, last, start), jnp.where(goes_up, start, last)

    for i in range(3):
        for c in range(3):
            for out, x in ((right_out, 9 + i), (left_out, 3 + i)):
                out[16 * (3 * c + i) : 16 * (3 * c + i) + 16] = b3[c, x, mid]
                first, second = edge_rows(c, x)
                at = 9 * i + 3 * c
                out[144 + at : 147 + at] = second
                out[176 + at : 179 + at] = first
    for x in range(OX):
        for c in range(3):
            first, second = edge_rows(c, x + HALO)
            at = 9 * x + 3 * c
            first_out[at : at + 3] = first
            second_out[at : at + 3] = second


def second_kernel(els_ref, own_ref, dots_ref, left_ref, right_ref, first_ref, second_ref,
                  tail_ref, row_ref, b0, b1, b2, b3, z_ref, lower_ref, upper_ref):
    _, at_last_x, _, at_last_y = place()
    has_r, has_u = ask(at_last_x), ask(at_last_y)
    below = odd()
    zero = jnp.zeros((8, DZ), F32)
    mid = slice(HALO, HALO + OY)

    def own(x, _):
        for c in range(3):
            b0[c, x + HALO, mid] = own_ref[3, c, x]
        return 0

    for x in range(WX):
        inside = has_r if x >= HALO + OX else 1.0
        for c in range(3):
            b0[c, x, 16:24] = zero
            at = 88 + 9 * x if x < HALO else 9 * (x - HALO) if x < HALO + OX else 120 + 9 * (x - HALO - OX)
            rows = slice(at + 3 * c, at + 3 * c + 3)
            one, two = first_ref[rows] * inside, second_ref[rows] * inside
            b0[c, x, 0:3] = jnp.where(below == 0, one, two)
            b0[c, x, 19:22] = jnp.where(below == 0, two, one) * has_u
    lax.fori_loop(0, OX, own, 0)
    for c in range(3):
        for i in range(3):
            block = slice(16 * (3 * c + i), 16 * (3 * c + i) + 16)
            b0[c, i, mid] = left_ref[block]
            b0[c, 12 + i, mid] = right_ref[block] * has_r

    basis = (b0, b1, b2, b3)
    three_steps(els_ref, basis, z_ref, lower_ref, upper_ref)

    def collect(x, sums):
        sums = list(sums)
        for row in (0, 8):
            for c in range(3):
                v = [own_ref[3, c, x, row : row + 8]]
                for k in range(1, 4):
                    w = b_at(basis[k], c, x, row)
                    v.append((w + w) - own_ref[3 - k, c, x, row : row + 8])
                    tail_ref[k - 1, c, x, row : row + 8] = v[k]
                for k in range(1, 6):
                    sums[k - 1] = sums[k - 1] + v[k // 2] * v[k - k // 2]
        return tuple(sums)

    sums = lax.fori_loop(0, OX, collect, (zero,) * 5, unroll=3)
    lane = lax.broadcasted_iota(jnp.int32, (1, DZ), 1)
    line = jnp.zeros((1, DZ), F32)
    for k in range(12):
        dot = dots_ref[k : k + 1] if k < 7 else sum_rows(sums[k - 7])
        line = jnp.where(lane == k, jnp.sum(dot, axis=1, keepdims=True), line)
    row_ref[...] = jnp.broadcast_to(line, row_ref.shape)


def b_at(ref, c, x, row):
    return ref[c, x + HALO, row + HALO : row + HALO + 8]


def times_matrix(p):
    out = [None] * (len(p) + 1)

    def add(k, value):
        out[k] = value if out[k] is None else out[k] + value

    for k, value in enumerate(p):
        add(k, value * (SPAN / 2))
        if k == 0:
            add(1, value * (SPAN / 2))
        else:
            add(k + 1, value * (SPAN / 4))
            add(k - 1, value * (SPAN / 4))
    return out


def tree_sum(values):
    while len(values) > 1:
        values = [a + b for a, b in zip(values[::2], values[1::2])] + ([values[-1]] if len(values) % 2 else [])
    return values[0]


def combine(p, a, q):
    out = []
    for k in range(max(len(p), len(q))):
        term = a * q[k] if k < len(q) else None
        if k < len(p):
            term = p[k] if term is None else p[k] + term
        out.append(term)
    return out


def coefficients(mu):
    gram = [[0.5 * (mu[i + j] + mu[abs(i - j)]) if i + j < len(mu) else None for j in range(7)] for i in range(7)]

    def inner(p, q):
        return tree_sum([p[i] * tree_sum([gram[i][j] * q[j] for j in range(len(q))]) for i in range(len(p))])

    remain = [jnp.ones_like(mu[0])]
    total = []
    for newton in range(NEWTON):
        direction = remain
        norm = inner(remain, remain)
        for step in range(CG_STEPS):
            image = times_matrix(direction)
            alpha = norm / inner(direction, image)
            total = combine(total, alpha, direction)
            remain = combine(remain, -alpha, image)
            if step + 1 < CG_STEPS:
                norm_next = inner(remain, remain)
                direction = combine(remain, norm_next / norm, direction)
                norm = norm_next
    return total, remain


def last_kernel(dots_ref, own_ref, tail_ref, displacement_hbm, residual_hbm, displacement_ref, residual_ref, sems):
    sums = jnp.sum(dots_ref[...], axis=0, keepdims=True)
    dots = [jnp.broadcast_to(sums[:, k : k + 1], (1, DZ)) for k in range(12)]
    mu = dots[:2]
    for k in range(2, 12):
        mu.append((dots[k] + dots[k]) - mu[k % 2])
    total, remain = coefficients(mu)
    total = [jnp.broadcast_to(value, (8, DZ)) for value in total]
    remain = [jnp.broadcast_to(value, (8, DZ)) for value in remain]
    copies = []
    for c in range(3):

        def write(x, _):
            for row in (0, 8):
                v = [own_ref[k, c, x, row : row + 8] for k in range(4)]
                v += [tail_ref[k, c, x, row : row + 8] for k in range(3)]
                displacement_ref[c, x, row : row + 8] = tree_sum([a * b for a, b in zip(total, v)])
                residual_ref[c, x, row : row + 8] = tree_sum([a * b for a, b in zip(remain, v)])
            return 0

        lax.fori_loop(0, OX, write, 0, unroll=3)
        for m, (source, target) in enumerate(((displacement_ref, displacement_hbm), (residual_ref, residual_hbm))):
            copies.append(pltpu.make_async_copy(source.at[c], target.at[c], sems.at[m, c]))
            copies[-1].start()
    for copy in copies:
        copy.wait()


def shape(*dims):
    return jax.ShapeDtypeStruct(dims, F32)


def call(kernel, outs, scratch=(), mebibytes=24, **more):
    return pl.pallas_call(
        kernel,
        out_shape=outs,
        scratch_shapes=[pltpu.VMEM(dims, F32) if isinstance(dims, tuple) else dims for dims in scratch],
        compiler_params=pltpu.CompilerParams(vmem_limit_bytes=mebibytes * 1024 * 1024),
        **more,
    )


STEP_SCRATCH = [(3, WX, WY, DZ)] * 4 + [(6, WX, WY + 8, DZ)] * 3


def rotate(value, axis, steps):
    count = lax.axis_size(axis)
    return lax.ppermute(value, axis, [(i, (i + steps) % count) for i in range(count)])


def wind(value, forward):
    count_x, count_y = lax.axis_size("gx"), lax.axis_size("gy")
    pairs = []
    for x in range(count_x):
        for y in range(count_y):
            ahead = y + 1 if (x % 2 == 0) == forward else y - 1
            goal = (x, ahead) if 0 <= ahead < count_y else (x ^ 1, y)
            pairs.append((x * count_y + y, goal[0] * count_y + goal[1]))
    return lax.ppermute(value, ("gx", "gy"), pairs)


def exchange(right, left, up, down):
    from_left = rotate(right, "gx", 1)
    from_right = rotate(left, "gx", -1)
    from_below = rotate(up, "gy", 1)
    from_above = rotate(down, "gy", -1)
    corner_left = rotate(jnp.concatenate([from_below[UP_HIGH], from_above[DOWN_HIGH]]), "gx", 1)
    corner_right = rotate(jnp.concatenate([from_below[UP_LOW], from_above[DOWN_LOW]]), "gx", -1)
    return from_left, from_right, from_below, from_above, corner_left, corner_right


def exchange_in_turn(right, left, first, second):
    from_left = rotate(right, "gx", 1)
    from_right = rotate(left, "gx", -1)
    first = jnp.concatenate([first, from_left[144:176], from_right[144:176]], axis=0)
    second = jnp.concatenate([second, from_left[176:208], from_right[176:208]], axis=0)
    return from_left, from_right, wind(first, True), wind(second, False)


def body(load, plastic_flags, flow_dir, contact_flags, die_depth):
    slabs = [(55, OY, DZ), (38, OY, DZ), (UP_ROWS, DZ), (DOWN_ROWS, DZ)]
    work = [(6, OX + 1, WY + 8, DZ)] * 2
    outside = pl.BlockSpec(memory_space=pl.ANY)
    inputs = (load, plastic_flags, flow_dir, contact_flags, die_depth)
    right, left, up, down = call(
        slab_kernel,
        [shape(*dims) for dims in slabs],
        slabs + [(3, OX + 1, WY, DZ), (OX, OY, DZ)] + work
        + [(3, OX, OY, DZ), pltpu.VMEM((8, OX, OY, DZ), jnp.int32), (6, OX, OY, DZ),
           pltpu.VMEM((OX, OY), jnp.int32), (OX, OY)]
        + [pltpu.SemaphoreType.DMA((count,)) for count in (3, 8, 6, 2, 6)],
        mebibytes=54,
        in_specs=[outside] * 5,
        out_specs=[outside] * 4,
    )(*inputs)
    part, contact = call(
        part_kernel, [shape(3, OX + 1, WY, DZ), shape(OX, OY, DZ)], work,
        cost_estimate=pl.CostEstimate(flops=400000, bytes_accessed=1000, transcendentals=0),
    )(*inputs)
    halos = exchange(right, left, up, down)
    els, own, dots, right, left, first, second = call(
        first_kernel,
        [shape(NEL + 1, WE, WY, DZ), shape(4, 3, OX, OY, DZ), shape(8, DZ), shape(208, DZ), shape(208, DZ), shape(88, DZ), shape(88, DZ)],
        STEP_SCRATCH,
    )(plastic_flags, flow_dir, contact, part, *halos)
    halos = exchange_in_turn(right, left, first, second)
    count = lax.axis_size("gx") * lax.axis_size("gy")
    tail, line = call(
        second_kernel, [shape(3, 3, OX, OY, DZ), shape(count, DZ)], STEP_SCRATCH
    )(els, own, dots, *halos)
    lines = lax.all_to_all(line, ("gx", "gy"), 0, 0, tiled=True)
    return tuple(
        call(
            last_kernel,
            [shape(3, OX, OY, DZ)] * 2,
            [(3, OX, OY, DZ)] * 2 + [pltpu.SemaphoreType.DMA((2, 3))],
            out_specs=[outside] * 2,
        )(lines, own, tail)
    )


def solution(mesh):
    in_specs = (
        P(None, "gx", "gy", None),
        P(None, "gx", "gy", None),
        P(None, "gx", "gy", None),
        P("gx", "gy"),
        P("gx", "gy"),
    )
    out_specs = (P(None, "gx", "gy", None), P(None, "gx", "gy", None))
    return jax.shard_map(body, mesh=mesh, in_specs=in_specs, out_specs=out_specs, check_vma=False)
```
